128 devices in a mesh: grp: 8 (over x_lo, y), gx: 16 (over z, x_hi, core).
Axes of the slice: x: 4 (x_hi: 2, x_lo: 2; x = x_hi * 2 + x_lo), y: 4, z: 4, core: 2. Of those that a mesh axis runs over, the one named last changes fastest.
Arguments:
- velocity: float32 [3, 64, 64, 4096], P(None, 'gx', 'grp'), may hold values from -6 to 6
- snapshot_index: int32 [4], replicated, may hold values from 0 to 63
- labels_fine: int32 [4, 64, 4096], P(None, 'grp', 'gx'), may hold values from 0 to 7
- labels_coarse: int32 [4, 32, 2048], P(None, 'grp', 'gx'), may hold values from 0 to 7
- conv_first: bfloat16 [3, 3, 64, 3], replicated, may hold values from -1.25 to 1.25
- conv_second: bfloat16 [3, 3, 64, 64], replicated, may hold values from -0.25 to 0.25
- conv_middle: bfloat16 [3, 3, 128, 64], replicated, may hold values from -0.25 to 0.25
- conv_joined: bfloat16 [3, 3, 64, 192], replicated, may hold values from -0.15625 to 0.15625
- head_fine: float32 [8, 64], replicated
- head_coarse: float32 [8, 128], replicated
Outputs:
- velocity_out: float32 [3, 64, 64, 4096], P(None, 'gx', 'grp')
- logits_fine: float32 [4, 64, 8, 4096], P(None, 'grp', None, 'gx')
- loss: float32 [], replicated
- grad_fine: float32 [8, 64], replicated
- grad_coarse: float32 [8, 128], replicated
The draws below stay inside these ranges and needn't reach their ends.
All inputs are finite; a program needn't handle non-finite values.
Results may differ from the reference program's by a relative error of at most 0.0095.
Values may be sent and summed in bfloat16 or wider, within the bound.
No kernel may reach another device: no remote copies, remote signals or barrier semaphores. Data moves between devices by JAX's collectives and lax.ppermute only.
A program may use at most 192 MiB of HBM per device.

```python
import jax
import jax.numpy as jnp
from jax import lax

RX = 256
SNAP = 4
STEPS = 2
C1 = 64
C2 = 128
NCLS = 8
NZ = 64
NY = 64
NX = 4096


def block_classes(key):
    block_key = jax.random.fold_in(key, 5)
    return jax.random.randint(block_key, (SNAP, 1, NX // RX), 0, NCLS, dtype=jnp.int32)


def mixed_labels(key, classes, rows, width, cols):
    coin_key, free_key = jax.random.split(key)
    dominant = jnp.broadcast_to(jnp.repeat(classes, width, axis=2), (SNAP, rows, cols))
    coin = jax.random.randint(coin_key, (SNAP, rows, cols), 0, 10, dtype=jnp.int32)
    free_class = jax.random.randint(free_key, (SNAP, rows, cols), 0, NCLS, dtype=jnp.int32)
    return jnp.where(coin < 8, dominant, free_class).astype(jnp.int32)


def draw_labels_fine(key, part):
    classes = block_classes(key)
    key = jax.random.fold_in(key, 31)
    return mixed_labels(key, classes, NY, RX, NX)


def draw_labels_coarse(key, part):
    classes = block_classes(key)
    key = jax.random.fold_in(key, 37)
    return mixed_labels(key, classes, NY // 2, RX // 2, NX // 2)


def draw_head_fine(key, part):
    key = jax.random.fold_in(key, 11)
    values = jax.random.normal(key, (NCLS, C1), jnp.float32)
    return values * (3.0 / C1 ** 0.5)


def draw_head_coarse(key, part):
    key = jax.random.fold_in(key, 23)
    values = jax.random.normal(key, (NCLS, C2), jnp.float32)
    return values * (3.0 / C2 ** 0.5)


def with_ends(array, own_key, low, top_value):
    dims = array.shape
    spot = [jax.random.randint(jax.random.fold_in(own_key, axis), (), 0, dims[axis]) for axis in range(len(dims))]
    array = array.at[tuple(spot)].set(low)
    longest = dims.index(max(dims))
    spot[longest] = (spot[longest] + 1) % dims[longest]
    return array.at[tuple(spot)].set(top_value)


def level_of(key, extent, shards, smallest, high):
    loudness = 1.0
    for position, parts in shards:
        steps = jax.random.uniform(jax.random.fold_in(jax.random.fold_in(key, 6), position), (parts,), jnp.float32, smallest / len(shards), high / len(shards))
        loudness = loudness * jnp.repeat(jnp.exp(steps), extent[position] // parts).reshape((-1,) + (1,) * (len(extent) - 1 - position))
    return loudness


def normal_values(stream_key, shape, scale, bound, cuts=(), held_as=jnp.bfloat16):
    entries = scale * jax.random.normal(stream_key, shape, jnp.float32)
    if cuts:
        entries = entries * level_of(stream_key, shape, cuts, -0.22, 0.18)
    return jnp.clip(entries, -bound, bound).astype(held_as)


def setup_inputs(seed: int = 0) -> dict:
    arg_keys = jax.random.split(jax.random.key(seed), 11)
    return {
        "velocity": normal_values(arg_keys[0], (3, NZ, NY, NX), 1.0, 6.0, ((1, 16), (2, 8)), jnp.float32),
        "snapshot_index": with_ends(jax.random.randint(arg_keys[1], (SNAP,), 0, NZ), jax.random.fold_in(arg_keys[1], 1), 0, NZ - 1).astype(jnp.int32),
        "labels_fine": draw_labels_fine(jax.random.fold_in(arg_keys[10], 71), 0),
        "labels_coarse": draw_labels_coarse(jax.random.fold_in(arg_keys[10], 71), 0),
        "conv_first": normal_values(arg_keys[4], (3, 3, C1, 3), 27 ** -0.5, 1.25),
        "conv_second": normal_values(arg_keys[5], (3, 3, C1, C1), (9 * C1) ** -0.5, 0.25),
        "conv_middle": normal_values(arg_keys[6], (3, 3, C2, C1), (9 * C1) ** -0.5, 0.25),
        "conv_joined": normal_values(arg_keys[7], (3, 3, C1, C2 + C1), (9 * (C2 + C1)) ** -0.5, 0.15625),
        "head_fine": draw_head_fine(jax.random.fold_in(arg_keys[10], 71), 0),
        "head_coarse": draw_head_coarse(jax.random.fold_in(arg_keys[10], 71), 0),
    }


time_step = 0.2
viscosity = 0.1


def advance_plane(three):
    center = three[:, 1]
    z_plus = three[:, 2]
    z_minus = three[:, 0]
    y_plus = jnp.roll(center, -1, axis=1)
    y_minus = jnp.roll(center, 1, axis=1)
    x_plus = jnp.roll(center, -1, axis=2)
    x_minus = jnp.roll(center, 1, axis=2)
    transport = center[0:1] * ((z_plus - z_minus) * 0.5) + center[1:2] * ((y_plus - y_minus) * 0.5) + center[2:3] * ((x_plus - x_minus) * 0.5)
    laplace = z_plus + z_minus + y_plus + y_minus + x_plus + x_minus - 6.0 * center
    return center - time_step * transport + viscosity * laplace


def advance_full(field):
    padded = jnp.concatenate([field[:, -1:], field, field[:, :1]], axis=1)
    planes = lax.map(lambda plane_pos: advance_plane(lax.dynamic_slice_in_dim(padded, plane_pos, 3, 1)), jnp.arange(NZ, dtype=jnp.int32))
    return jnp.transpose(planes, (1, 0, 2, 3))


def convolve(feature, weight):
    padded = jnp.pad(feature.astype(jnp.float32), ((0, 0), (1, 1), (1, 1)), mode="wrap")
    result = lax.conv_general_dilated(padded[None], weight.astype(jnp.float32), (1, 1), "VALID", dimension_numbers=("NCHW", "HWOI", "NCHW"), precision=lax.Precision.HIGHEST)[0]
    return jnp.maximum(result, 0.0).astype(jnp.bfloat16)


def head_terms(head, feature, labels, count):
    logits = jnp.einsum("kc,cyx->kyx", head, feature.astype(jnp.float32), precision=lax.Precision.HIGHEST)
    log_probs = jax.nn.log_softmax(logits, axis=0)
    onehot = (labels[None] == jnp.arange(NCLS, dtype=jnp.int32)[:, None, None]).astype(jnp.float32)
    loss_part = -jnp.sum(onehot * log_probs) / count
    slope = (jnp.exp(log_probs) - onehot) / count
    grad_part = jnp.einsum("kyx,cyx->kc", slope, feature.astype(jnp.float32), precision=lax.Precision.HIGHEST)
    return logits, loss_part, grad_part


def reference(velocity, snapshot_index, labels_fine, labels_coarse, conv_first, conv_second, conv_middle, conv_joined, head_fine, head_coarse):
    images = jnp.transpose(velocity[:, snapshot_index].astype(jnp.bfloat16), (1, 0, 2, 3))
    field = velocity
    for repeat in range(STEPS):
        field = advance_full(field)
    count_fine = jnp.float32(SNAP * NY * NX)
    count_coarse = jnp.float32(SNAP * NY * NX // 4)

    def network(inputs):
        image, lab_fine, lab_coarse = inputs
        first = convolve(image, conv_first)
        second = convolve(first, conv_second)
        channels = second.shape[0]
        pooled = second.reshape(channels, NY // 2, 2, NX // 2, 2).max(axis=(2, 4))
        middle = convolve(pooled, conv_middle)
        lifted = jnp.repeat(jnp.repeat(middle, 2, axis=1), 2, axis=2)
        joined = jnp.concatenate([lifted, second], axis=0)
        decoded = convolve(joined, conv_joined)
        logits, loss_one, grad_one = head_terms(head_fine, decoded, lab_fine, count_fine)
        unused, loss_two, grad_two = head_terms(head_coarse, middle, lab_coarse, count_coarse)
        return logits, loss_one + loss_two, grad_one, grad_two

    logits, losses, grads_one, grads_two = lax.map(network, (images, labels_fine, labels_coarse))
    return field, jnp.transpose(logits, (0, 2, 1, 3)), jnp.sum(losses), jnp.sum(grads_one, axis=0), jnp.sum(grads_two, axis=0)
```

```python
import functools

import jax
import jax.numpy as jnp
import numpy as np
from jax import lax
from jax.experimental import pallas as pl
from jax.experimental.pallas import tpu as pltpu
from jax.sharding import PartitionSpec as P

F32, BF16 = jnp.float32, jnp.bfloat16
AXES = ("grp", "gx")
SNAP, NCLS = 4, 8
ROWS, COLS = 8, 256
XB = 144
M = SNAP * XB
NX = 4096
CHUNK = 512
time_step = 0.2
viscosity = 0.1
GROUP_COL = (0, 1, 2, -1)
VMEM_LIMIT = 48 * 1024 * 1024


def dot_nn(a, b):
    return lax.dot_general(a, b, (((1,), (0,)), ((), ())), preferred_element_type=F32)


def dot_nt(a, b):
    return lax.dot_general(a, b, (((1,), (1,)), ((), ())), preferred_element_type=F32)


def split_two(value):
    high = value.astype(BF16)
    return high, (value - high.astype(F32)).astype(BF16)


def pack_kernel(index_ref, vel_ref, send_ref, last_ref, first_ref, planes):
    for snap in range(SNAP):
        local = index_ref[snap] - index_ref[SNAP]
        here = jnp.logical_and(local >= 0, local < 4)
        spot = jnp.clip(local, 0, 3)

        @pl.when(here)
        def _():
            for comp in range(3):
                planes[pl.ds((snap * 3 + comp) * ROWS, ROWS), :] = vel_ref[comp, spot]

        @pl.when(jnp.logical_not(here))
        def _():
            planes[pl.ds(snap * 24, 24), :] = jnp.zeros((24, NX), F32)

    lane = lax.broadcasted_iota(jnp.int32, (16, 128), 1)

    def target(j, carry):
        base = pl.multiple_of(j * COLS, COLS)
        send_ref[j, 0:96, :] = planes[:, pl.ds(base, 128)].astype(BF16)
        send_ref[j, 96:192, :] = planes[:, pl.ds(base + 128, 128)].astype(BF16)
        after = pl.multiple_of(lax.rem(base + COLS, NX), 128)
        before = pl.multiple_of(lax.rem(base + NX - 128, NX), 128)
        packed = jnp.zeros((16, 128), F32)
        for pair in range(6):
            edge = jnp.where(
                lane < 64,
                planes[pl.ds(16 * pair, 16), pl.ds(after, 128)],
                planes[pl.ds(16 * pair, 16), pl.ds(before, 128)],
            )
            edge = pltpu.roll(edge, 16 * pair + 8, 1)
            packed = jnp.where((lane >> 4) == pair, edge, packed)
        send_ref[j, 192:208, :] = packed.astype(BF16)
        return carry

    lax.fori_loop(0, 16, target, 0)
    for comp in range(3):
        for plane in range(2):
            rows = pl.ds((comp * 2 + plane) * 8, 8)
            planes[rows, :] = vel_ref[comp, 2 + plane]
            planes[pl.ds(48 + (comp * 2 + plane) * 8, 8), :] = vel_ref[comp, plane]
    last_ref[...] = planes[0:48, :].astype(BF16)
    first_ref[...] = planes[48:96, :].astype(BF16)


def pack(velocity, index):
    vmem = pl.BlockSpec(memory_space=pltpu.VMEM)
    return pl.pallas_call(
        pack_kernel,
        out_shape=(
            jax.ShapeDtypeStruct((16, 208, 128), BF16),
            jax.ShapeDtypeStruct((48, NX), BF16),
            jax.ShapeDtypeStruct((48, NX), BF16),
        ),
        in_specs=[pl.BlockSpec(memory_space=pltpu.SMEM), vmem],
        out_specs=(vmem, vmem, vmem),
        scratch_shapes=[pltpu.VMEM((96, NX), F32)],
        compiler_params=pltpu.CompilerParams(vmem_limit_bytes=VMEM_LIMIT),
        cost_estimate=pl.CostEstimate(flops=0, bytes_accessed=6_000_000, transcendentals=0),
        name="pack",
    )(index, velocity)


def reduce_scatter_gx(blocks):
    place = lax.axis_index("gx")
    core, half, depth = place % 2, (place // 2) % 2, place // 4
    x = blocks.reshape(4, 2, 2, 208, 128)
    pick = functools.partial(lax.dynamic_index_in_dim, keepdims=False)
    got = lax.ppermute(pick(x, 1 - core, 2), "gx", [(i, i ^ 1) for i in range(16)])
    x = pick(x, core, 2) + got
    parts = [pick(x, depth, 0)]
    for k in (1, 2, 3):
        pairs = [(i, (i + 4 * k) % 16) for i in range(16)]
        parts.append(lax.ppermute(pick(x, (depth + k) % 4, 0), "gx", pairs))
    x = parts[0] + parts[1] + parts[2] + parts[3]
    got = lax.ppermute(pick(x, 1 - half, 0), "gx", [(i, i ^ 2) for i in range(16)])
    return pick(x, half, 0) + got


def edges_kernel(vel_ref, before_ref, after_ref, last_ref, first_ref, rows):
    for out_ref, lo, one in ((last_ref, 6, 7), (first_ref, 0, 0)):
        rows[24:32, :] = jnp.zeros((8, NX), F32)
        for comp in range(3):
            near = before_ref[pl.ds(16 * comp, 16), :].astype(F32)
            rows[pl.ds(10 * comp, 1), :] = near[8 + one : 9 + one, :]
            for z in range(4):
                rows[pl.ds(10 * comp + 1 + 2 * z, 2), :] = vel_ref[comp, z, lo : lo + 2, :]
            near = after_ref[pl.ds(16 * comp, 16), :].astype(F32)
            rows[pl.ds(10 * comp + 9, 1), :] = near[one : one + 1, :]
        out_ref[...] = rows[...].astype(BF16)


def edges(velocity, before, after):
    vmem = pl.BlockSpec(memory_space=pltpu.VMEM)
    shape = jax.ShapeDtypeStruct((32, NX), BF16)
    return pl.pallas_call(
        edges_kernel,
        out_shape=(shape, shape),
        in_specs=[vmem] * 3,
        out_specs=(vmem, vmem),
        scratch_shapes=[pltpu.VMEM((32, NX), F32)],
        compiler_params=pltpu.CompilerParams(vmem_limit_bytes=VMEM_LIMIT),
        cost_estimate=pl.CostEstimate(flops=0, bytes_accessed=4_000_000, transcendentals=0),
        name="edges",
    )(velocity, before, after)


def stepped(center, z_minus, z_plus, y_minus, y_plus):
    wide = CHUNK + 256
    mid = [c[:, 128 : 128 + CHUNK] for c in center]
    out = []
    for d in range(3):
        x_plus = pltpu.roll(center[d], wide - 1, 1)[:, 128 : 128 + CHUNK]
        x_minus = pltpu.roll(center[d], 1, 1)[:, 128 : 128 + CHUNK]
        transport = (
            mid[0] * (z_plus[d] - z_minus[d])
            + mid[1] * (y_plus[d] - y_minus[d])
            + mid[2] * (x_plus - x_minus)
        )
        around = z_plus[d] + z_minus[d] + y_plus[d] + y_minus[d] + x_plus + x_minus
        out.append(
            (1.0 - 6.0 * viscosity) * mid[d]
            - (0.5 * time_step) * transport
            + viscosity * around
        )
    return out


def advance_kernel(vel_ref, zb_ref, za_ref, yb_ref, ya_ref, out_ref, old, new):
    body = pl.ds(128, NX)
    for comp in range(3):
        for z in range(4):
            old[comp, pl.ds(24 * (z + 2) + 8, 8), body] = vel_ref[comp, z]
        low = zb_ref[pl.ds(16 * comp, 16), :].astype(F32)
        high = za_ref[pl.ds(16 * comp, 16), :].astype(F32)
        for p in range(2):
            old[comp, pl.ds(24 * p + 8, 8), body] = low[8 * p : 8 * p + 8]
            old[comp, pl.ds(24 * (p + 6) + 8, 8), body] = high[8 * p : 8 * p + 8]
    low = yb_ref[...].astype(F32)
    high = ya_ref[...].astype(F32)
    for comp in range(3):
        for z in range(4):
            row = 10 * comp + 1 + 2 * z
            old[comp, pl.ds(24 * (z + 2) + 6, 2), body] = low[row : row + 2]
            old[comp, pl.ds(24 * (z + 2) + 16, 2), body] = high[row : row + 2]
        for z, row in ((-1, 10 * comp), (4, 10 * comp + 9)):
            old[comp, pl.ds(24 * (z + 2) + 7, 1), body] = low[row : row + 1]
            old[comp, pl.ds(24 * (z + 2) + 16, 1), body] = high[row : row + 1]

    def wrap(buf):
        buf[:, :, 0:128] = buf[:, :, NX : NX + 128]
        buf[:, :, NX + 128 : NX + 256] = buf[:, :, 128:256]

    wrap(old)

    def first(n, carry):
        wide = pl.ds(pl.multiple_of(n * CHUNK, 128), CHUNK + 256)
        here = pl.ds(pl.multiple_of(n * CHUNK + 128, 128), CHUNK)
        for z in range(-1, 5):
            at = 24 * (z + 2) + 8
            get = lambda row, where: [old[c, pl.ds(row, 8), where] for c in range(3)]
            res = stepped(
                get(at, wide), get(at - 24, here), get(at + 24, here),
                get(at - 1, here), get(at + 1, here),
            )
            for c in range(3):
                new[c, pl.ds(24 * (z + 1) + 8, 8), here] = res[c]
        for z in range(4):
            for block, pick, row in ((0, 7, 7), (16, 0, 16)):
                at = 24 * (z + 2) + block
                get = lambda row, where: [old[c, pl.ds(row, 8), where] for c in range(3)]
                res = stepped(
                    get(at, wide), get(at - 24, here), get(at + 24, here),
                    get(at - 1, here), get(at + 1, here),
                )
                for c in range(3):
                    new[c, pl.ds(24 * (z + 1) + row, 1), here] = res[c][pick : pick + 1]
        return carry

    lax.fori_loop(0, NX // CHUNK, first, 0)
    wrap(new)

    def second(n, carry):
        wide = pl.ds(pl.multiple_of(n * CHUNK, 128), CHUNK + 256)
        here = pl.ds(pl.multiple_of(n * CHUNK + 128, 128), CHUNK)
        there = pl.ds(pl.multiple_of(n * CHUNK, 128), CHUNK)
        for z in range(4):
            at = 24 * (z + 1) + 8
            get = lambda row, where: [new[c, pl.ds(row, 8), where] for c in range(3)]
            res = stepped(
                get(at, wide), get(at - 24, here), get(at + 24, here),
                get(at - 1, here), get(at + 1, here),
            )
            for c in range(3):
                out_ref[c, z, :, there] = res[c]
        return carry

    lax.fori_loop(0, NX // CHUNK, second, 0)


def advance_twice(velocity, zb, za, yb, ya):
    vmem = pl.BlockSpec(memory_space=pltpu.VMEM)
    return pl.pallas_call(
        advance_kernel,
        out_shape=jax.ShapeDtypeStruct((3, 4, ROWS, NX), F32),
        in_specs=[vmem] * 5,
        out_specs=vmem,
        scratch_shapes=[
            pltpu.VMEM((3, 24 * 8, NX + 256), F32),
            pltpu.VMEM((3, 24 * 6, NX + 256), F32),
        ],
        compiler_params=pltpu.CompilerParams(vmem_limit_bytes=VMEM_LIMIT),
        cost_estimate=pl.CostEstimate(flops=30_000_000, bytes_accessed=20_000_000, transcendentals=0),
        name="advance",
    )(velocity, zb, za, yb, ya)


def first_layer_places():
    places = np.zeros((6, 4, 144, 32), np.float32)
    for r in range(6):
        for group, col in enumerate(GROUP_COL):
            for a in range(3):
                for b in range(3):
                    for c in range(3):
                        j = b + 1 + col
                        places[r, group, j * 24 + c * 8 + r + a, a * 9 + b * 3 + c] = 1.0
    return places


def weights_kernel(
    places_ref, first_ref, second_ref, middle_ref, joined_ref, fine_ref, coarse_ref,
    w1_ref, w2_ref, w3_ref, w4_ref, hf_ref, hc_ref,
):
    for r in range(6):
        parts = [dot_nn(places_ref[r, g], first_ref[...]) for g in range(4)]
        w1_ref[r] = jnp.concatenate(parts, axis=1).astype(BF16)

    none = jnp.zeros((64, 64), F32)

    def spread(taps, out_ref):
        for k in range(4):
            for group, col in enumerate(GROUP_COL):
                blocks = []
                for py in range(2):
                    for px in range(2):
                        a, b = k - py, col - px + 1
                        inside = 0 <= a <= 2 and 0 <= b <= 2
                        blocks.append(taps[a][b] if inside else none)
                block = jnp.concatenate(blocks, axis=1).astype(BF16)
                out_ref[pl.ds(k * 256 + group * 64, 64), :] = block

    spread([[second_ref[a, b].astype(F32).T for b in range(3)] for a in range(3)], w2_ref)

    wide_none = jnp.zeros((64, 128), F32)
    taps = [[middle_ref[a, b].astype(F32).T for b in range(3)] for a in range(3)]
    for k in range(4):
        for place, b in enumerate((0, 2, 1, None)):
            blocks = []
            for e in range(2):
                inside = b is not None and 0 <= k - e <= 2
                blocks.append(taps[k - e][b] if inside else wide_none)
            block = jnp.concatenate(blocks, axis=1).astype(BF16)
            w3_ref[pl.ds(k * 256 + place * 64, 64), :] = block

    joined = [[joined_ref[a, b].astype(F32).T for b in range(3)] for a in range(3)]
    spread([[joined[a][b][128:192] for b in range(3)] for a in range(3)], w4_ref)
    for dy in range(3):
        for dx in range(3):
            blocks = []
            for py in range(2):
                for px in range(2):
                    total = jnp.zeros((128, 64), F32)
                    for a in range(3):
                        for b in range(3):
                            if (py + a - 1) // 2 + 1 == dy and (px + b - 1) // 2 + 1 == dx:
                                total = total + joined[a][b][0:128]
                    blocks.append(total)
            block = jnp.concatenate(blocks, axis=1).astype(BF16)
            w4_ref[pl.ds(1024 + (dy * 3 + dx) * 128, 128), :] = block

    head = fine_ref[...]
    high = head.astype(BF16).astype(F32)
    empty = jnp.zeros((NCLS, 64), F32)
    rows = []
    for part in (high, head - high):
        for spot in range(4):
            rows.append(jnp.concatenate([part if i == spot else empty for i in range(4)], axis=1))
    hf_ref[...] = jnp.concatenate(rows, axis=0).astype(BF16)
    head = coarse_ref[...]
    high = head.astype(BF16).astype(F32)
    hc_ref[...] = jnp.concatenate([high, head - high], axis=0).astype(BF16)


def block_weights(conv_first, conv_second, conv_middle, conv_joined, head_fine, head_coarse):
    flat = jnp.transpose(conv_first, (0, 1, 3, 2)).reshape(27, 64)
    flat = jnp.pad(flat, ((0, 5), (0, 0)))
    places = jnp.asarray(first_layer_places(), BF16)
    vmem = pl.BlockSpec(memory_space=pltpu.VMEM)
    return pl.pallas_call(
        weights_kernel,
        out_shape=(
            jax.ShapeDtypeStruct((6, 144, 256), BF16),
            jax.ShapeDtypeStruct((1024, 256), BF16),
            jax.ShapeDtypeStruct((1024, 256), BF16),
            jax.ShapeDtypeStruct((1024 + 1152, 256), BF16),
            jax.ShapeDtypeStruct((64, 256), BF16),
            jax.ShapeDtypeStruct((16, 128), BF16),
        ),
        in_specs=[vmem] * 7,
        out_specs=(vmem,) * 6,
        compiler_params=pltpu.CompilerParams(vmem_limit_bytes=VMEM_LIMIT),
        cost_estimate=pl.CostEstimate(flops=0, bytes_accessed=6_000_000, transcendentals=0),
        name="block_weights",
    )(places, flat, conv_second, conv_middle, conv_joined, head_fine, head_coarse)


def network_kernel(
    up_ref, mid_ref, down_ref, labf_ref, labc_ref,
    w1_ref, w2_ref, w3_ref, w4_ref, hf_ref, hc_ref,
    logits_ref, sums_ref,
    win, taps, h1, h2, ph, mh, mid_keep, dec, sbuf, pbuf, mbuf, labs, planar, slope,
):
    lane384 = lax.broadcasted_iota(jnp.int32, (8, 384), 1)
    row384 = lax.broadcasted_iota(jnp.int32, (8, 384), 0)
    tiles = [ref[...].astype(F32) for ref in (up_ref, mid_ref, down_ref)]
    for q in range(12):
        pieces = []
        for tile in tiles:
            edge = tile[192 + 8 * (q % 2) : 200 + 8 * (q % 2)]
            edge = pltpu.roll(edge, 128 - (16 * (q // 2) + 8), 1)
            pieces.append(
                jnp.concatenate([tile[8 * q : 8 * q + 8], tile[96 + 8 * q : 104 + 8 * q], edge], axis=1)
            )
        top, center, bottom = pieces
        snap, comp = q // 3, q % 3
        rows = pl.ds(comp * 8, 8)
        win[0, snap, rows, :] = jnp.where(row384 < 6, pltpu.roll(top, 6, 0), pltpu.roll(center, 6, 0))
        win[1, snap, rows, :] = center
        win[2, snap, rows, :] = jnp.where(row384 < 2, pltpu.roll(center, 2, 0), pltpu.roll(bottom, 2, 0))

    spot = lax.broadcasted_iota(jnp.int32, (XB, 384), 0)
    wanted = jnp.where(spot >= 142, 2 * spot + 94, 2 * spot - 2)
    wanted = jnp.where(wanted < 0, wanted + 384, wanted)
    even = (lax.broadcasted_iota(jnp.int32, (XB, 384), 1) == wanted).astype(F32).astype(BF16)
    own = lax.broadcasted_iota(jnp.int32, (XB, 144), 0) < 142
    for group in range(3):
        found = []
        for snap in range(SNAP):
            window = win[group, snap]
            shifted = [window] + [pltpu.roll(window, 384 - j, 1) for j in range(1, 6)]
            stack = jnp.concatenate(shifted, axis=0).astype(BF16)
            found.append(dot_nt(even, stack))
        for snap in range(SNAP):
            rows = jnp.where(own, found[snap], found[(snap + 1) % SNAP])
            taps[group, pl.ds(snap * XB, XB), :] = rows.astype(BF16)

    def first_row(i, carry):
        group, r = i // 6, i % 6
        out = dot_nn(taps[group], w1_ref[r])
        h1[i] = jnp.maximum(out, 0.0).astype(BF16)
        return carry

    lax.fori_loop(0, 18, first_row, 0)

    def keep_padded(buf, value):
        buf[8 : 8 + M, :] = value
        buf[7:8, :] = value[M - 1 : M]
        buf[8 + M : 9 + M, :] = value[0:1]

    side = lax.broadcasted_iota(jnp.int32, (M, 128), 1) < 64

    def second_row(q, carry):
        lhs = jnp.concatenate([h1[2 * q + k] for k in range(4)], axis=1)
        out = jnp.maximum(dot_nn(lhs, w2_ref[...]), 0.0)
        keep_padded(sbuf, out)
        for py in range(2):
            lanes = pl.ds(128 * py, 128)
            h2[2 * q + py, :, 0:128] = out[:, 128 * py : 128 * py + 128].astype(BF16)
            beside = jnp.where(side, sbuf[9 : 9 + M, lanes], sbuf[7 : 7 + M, lanes])
            h2[2 * q + py, :, 128:256] = beside.astype(BF16)
        pooled = jnp.maximum(out[:, 0:128], out[:, 128:256])
        pooled = jnp.maximum(pooled, pltpu.roll(pooled, 64, 1))
        keep_padded(pbuf, pooled)
        ph[q, :, 0:128] = jnp.where(side, pbuf[7 : 7 + M, :], pbuf[9 : 9 + M, :]).astype(BF16)
        ph[q, :, 128:256] = pooled.astype(BF16)
        return carry

    lax.fori_loop(0, 8, second_row, 0)

    def middle_rows(t, carry):
        lhs = jnp.concatenate([ph[2 * t + k] for k in range(4)], axis=1)
        out = jnp.maximum(dot_nn(lhs, w3_ref[...]), 0.0)
        for e in range(2):
            value = out[:, 128 * e : 128 * e + 128]
            keep_padded(mbuf, value)
            row = 2 * t + e
            kept = value.astype(BF16)
            mh[row, :, 0:128] = mbuf[7 : 7 + M, :].astype(BF16)
            mh[row, :, 128:256] = kept
            mh[row, :, 256:384] = mbuf[9 : 9 + M, :].astype(BF16)
        return carry

    lax.fori_loop(0, 3, middle_rows, 0)

    def decoded_row(y, carry):
        lhs = jnp.concatenate(
            [h2[2 * y + 3 + k] for k in range(4)] + [mh[y + k] for k in range(3)], axis=1
        )
        dec[y] = jnp.maximum(dot_nn(lhs, w4_ref[...]), 0.0).astype(BF16)
        return carry

    lax.fori_loop(0, 4, decoded_row, 0)

    col = lax.broadcasted_iota(jnp.int32, (256, 256), 0)
    planar_col = lax.broadcasted_iota(jnp.int32, (256, 256), 1)
    source = 2 * (planar_col & 127) + (planar_col >> 7)
    to_planar = (col == source).astype(F32).astype(BF16)
    labs[...] = dot_nn(labf_ref[...].astype(F32).astype(BF16), to_planar)
    to_cols = (planar_col == 2 * (col & 127) + (col >> 7)).astype(F32).astype(BF16)

    classes = lax.broadcasted_iota(jnp.int32, (NCLS, 128), 0).astype(F32)

    def terms(logits, label):
        peak = jnp.max(logits, axis=0, keepdims=True)
        powers = jnp.exp(logits - peak)
        total = jnp.sum(powers, axis=0, keepdims=True)
        onehot = (classes == label).astype(F32)
        lost = onehot * (peak + jnp.log(total) - logits)
        return lost, powers / total - onehot

    lost_fine = jnp.zeros((NCLS, 128), F32)
    grad_fine = jnp.zeros((64, 256), F32)
    lost_coarse = jnp.zeros((NCLS, 128), F32)
    grad_coarse = jnp.zeros((16, 128), F32)
    for y in range(4):
        for snap in range(SNAP):
            cells = pl.ds(snap * XB, 128)
            feature = dec[y, cells, :]
            both = dot_nt(hf_ref[...], feature)
            logits = both[0:32] + both[32:64]
            slopes = []
            for py in range(2):
                row = snap * 8 + 2 * y + py
                for px in range(2):
                    mine = logits[(2 * py + px) * 8 : (2 * py + px) * 8 + 8]
                    planar[pl.ds(row * 8, 8), pl.ds(128 * px, 128)] = mine
                    lost, grad = terms(mine, labs[pl.ds(row, 1), pl.ds(128 * px, 128)])
                    lost_fine = lost_fine + lost
                    slopes.append(grad)
            high, low = split_two(jnp.concatenate(slopes, axis=0))
            grad_fine = grad_fine + dot_nn(jnp.concatenate([high, low], axis=0), feature)

            feature = mh[y + 1, cells, 128:256]
            both = dot_nt(hc_ref[...], feature)
            label = labc_ref[pl.ds(snap * 4 + y, 1), :].astype(F32)
            lost, grad = terms(both[0:8] + both[8:16], label)
            lost_coarse = lost_coarse + lost
            high, low = split_two(grad)
            grad_coarse = grad_coarse + dot_nn(
                jnp.concatenate([high.astype(F32), low.astype(F32)], axis=0).astype(BF16), feature
            )

    whole = planar[...]
    high, rest = whole.astype(BF16), whole
    rest = rest - high.astype(F32)
    middle_term = rest.astype(BF16)
    low = (rest - middle_term.astype(F32)).astype(BF16)
    ordered = dot_nn(high, to_cols) + dot_nn(middle_term, to_cols) + dot_nn(low, to_cols)
    for row in range(32):
        logits_ref[row] = ordered[8 * row : 8 * row + 8]

    fine_cells = 1048576.0
    coarse_cells = 262144.0
    sums_ref[0:8, :] = (grad_coarse[0:8] + grad_coarse[8:16]) * (1.0 / coarse_cells)
    total = jnp.zeros((NCLS, 64), F32)
    for spot in range(4):
        for part in (0, 32):
            block = grad_fine[part + 8 * spot : part + 8 * spot + 8]
            total = total + block[:, 64 * spot : 64 * spot + 64]
    loss = jnp.sum(lost_fine) * (1.0 / fine_cells) + jnp.sum(lost_coarse) * (1.0 / coarse_cells)
    sums_ref[8:16, :] = jnp.concatenate(
        [total * (1.0 / fine_cells), jnp.broadcast_to(loss, (NCLS, 64))], axis=1
    )


def network(up, mid, down, labels_fine, labels_coarse, weights):
    vmem = pl.BlockSpec(memory_space=pltpu.VMEM)
    return pl.pallas_call(
        network_kernel,
        out_shape=(
            jax.ShapeDtypeStruct((32, NCLS, COLS), F32),
            jax.ShapeDtypeStruct((16, 128), F32),
        ),
        in_specs=[vmem] * 11,
        out_specs=(vmem, vmem),
        scratch_shapes=[
            pltpu.VMEM((3, SNAP, 24, 384), F32),
            pltpu.VMEM((3, M, 144), BF16),
            pltpu.VMEM((18, M, 256), BF16),
            pltpu.VMEM((16, M, 256), BF16),
            pltpu.VMEM((8, M, 256), BF16),
            pltpu.VMEM((6, M, 384), BF16),
            pltpu.VMEM((8, 128), F32),
            pltpu.VMEM((4, M, 256), BF16),
            pltpu.VMEM((M + 16, 256), F32),
            pltpu.VMEM((M + 16, 128), F32),
            pltpu.VMEM((M + 16, 128), F32),
            pltpu.VMEM((32, 256), F32),
            pltpu.VMEM((256, 256), F32),
            pltpu.VMEM((64, 128), F32),
        ],
        compiler_params=pltpu.CompilerParams(vmem_limit_bytes=VMEM_LIMIT),
        cost_estimate=pl.CostEstimate(
            flops=8_000_000_000, bytes_accessed=6_000_000, transcendentals=200_000
        ),
        name="network",
    )(up, mid, down, labels_fine, labels_coarse, *weights)


def mesh_pairs(change):
    pairs = []
    for device in range(128):
        grp, gx = device // 16, device % 16
        at = {"x": (gx // 2 % 2) * 2 + grp // 4, "y": grp % 4, "z": gx // 4, "core": gx % 2}
        change(at)
        grp = (at["x"] % 2) * 4 + at["y"]
        gx = (at["z"] * 2 + at["x"] // 2) * 2 + at["core"]
        pairs.append((device, grp * 16 + gx))
    return pairs


def sum_everywhere(x):
    def flip(name, bits):
        def change(at):
            at[name] ^= bits

        return lax.ppermute(x, AXES, mesh_pairs(change))

    x = x + flip("core", 1)
    for name in ("z", "y", "x"):
        x = (x + flip(name, 1)) + (flip(name, 2) + flip(name, 3))
    return x


def ring(axis, size, step):
    return [(i, (i + step) % size) for i in range(size)]


def body(
    velocity, snapshot_index, labels_fine, labels_coarse,
    conv_first, conv_second, conv_middle, conv_joined, head_fine, head_coarse,
):
    up = functools.partial(lax.ppermute, axis_name="grp", perm=ring("grp", 8, 1))
    down = functools.partial(lax.ppermute, axis_name="grp", perm=ring("grp", 8, -1))
    first_plane = (lax.axis_index("gx") * 4).astype(jnp.int32)
    index = jnp.concatenate([snapshot_index, first_plane[None]])
    send, last_planes, first_planes = pack(velocity, index)
    weights = block_weights(conv_first, conv_second, conv_middle, conv_joined, head_fine, head_coarse)
    tile = reduce_scatter_gx(send)
    z_before = lax.ppermute(last_planes, "gx", ring("gx", 16, 1))
    z_after = lax.ppermute(first_planes, "gx", ring("gx", 16, -1))
    tile_up, tile_down = up(tile), down(tile)
    last_rows, first_rows = edges(velocity, z_before, z_after)
    y_before, y_after = up(last_rows), down(first_rows)
    logits, sums = network(
        tile_up, tile, tile_down,
        labels_fine.reshape(SNAP * ROWS, COLS), labels_coarse.reshape(SNAP * 4, 128), weights,
    )
    field = advance_twice(velocity, z_before, z_after, y_before, y_after)
    sums = sum_everywhere(sums)
    return (
        field,
        logits.reshape(SNAP, ROWS, NCLS, COLS),
        sums[8, 64],
        sums[8:16, 0:64],
        sums[0:8, :],
    )


def solution(mesh):
    return jax.shard_map(
        body,
        mesh=mesh,
        in_specs=(
            P(None, "gx", "grp", None),
            P(),
            P(None, "grp", "gx"),
            P(None, "grp", "gx"),
            P(),
            P(),
            P(),
            P(),
            P(),
            P(),
        ),
        out_specs=(P(None, "gx", "grp", None), P(None, "grp", None, "gx"), P(), P(), P()),
        check_vma=False,
    )
```

```python
import functools

import jax
import jax.numpy as jnp
import numpy as np
from jax import lax
from jax.experimental import pallas as pl
from jax.experimental.pallas import tpu as pltpu
from jax.sharding import PartitionSpec as P

F32, BF16 = jnp.float32, jnp.bfloat16
AXES = ("grp", "gx")
SNAP, NCLS = 4, 8
ROWS, COLS = 8, 256
XB = 144
M = SNAP * XB
NX = 4096
CHUNK = 1024
time_step = 0.2
viscosity = 0.1
GROUP_COL = (0, 1, 2, -1)


def dot_nn(a, b):
    return lax.dot_general(a, b, (((1,), (0,)), ((), ())), preferred_element_type=F32)


def dot_nt(a, b):
    return lax.dot_general(a, b, (((1,), (1,)), ((), ())), preferred_element_type=F32)


def split_two(value):
    high = value.astype(BF16)
    return high, (value - high.astype(F32)).astype(BF16)


def call(kernel, name, outs, scratch, flops, limit, *args, scalars=0):
    vmem = pl.BlockSpec(memory_space=pltpu.VMEM)
    smem = pl.BlockSpec(memory_space=pltpu.SMEM)
    return pl.pallas_call(
        kernel,
        out_shape=tuple(jax.ShapeDtypeStruct(*out) for out in outs),
        in_specs=[smem] * scalars + [vmem] * (len(args) - scalars),
        out_specs=(vmem,) * len(outs),
        scratch_shapes=[pltpu.VMEM(*one) for one in scratch],
        compiler_params=pltpu.CompilerParams(vmem_limit_bytes=limit * 1024 * 1024),
        cost_estimate=pl.CostEstimate(flops=flops, bytes_accessed=1_000_000, transcendentals=0),
        name=name,
    )(*args)


def exchange_a(x, axis):
    return lax.ppermute(x, axis, [(i, i ^ 1) for i in range(lax.axis_size(axis))])


def exchange_b(x, axis):
    count = lax.axis_size(axis)
    return lax.ppermute(x, axis, [(i, (((i + 1) ^ 1) - 1) % count) for i in range(count)])


def is_even(axis):
    return lax.rem(lax.axis_index(axis), 2) == 0


def pack_kernel(index_ref, vel_ref, keep_ref, give_ref, planes, sems):
    place = lax.axis_index("gx")
    fetches = []
    for snap in range(SNAP):
        local = index_ref[snap] - place * 4
        here = jnp.logical_and(local >= 0, local < 4)
        spot = jnp.clip(local, 0, 3)
        copies = [
            pltpu.make_async_copy(
                vel_ref.at[comp, spot],
                planes.at[pl.ds((snap * 3 + comp) * ROWS, ROWS), :],
                sems.at[snap * 3 + comp],
            )
            for comp in range(3)
        ]
        fetches.append((here, copies))

        @pl.when(here)
        def _():
            for copy in copies:
                copy.start()

        @pl.when(jnp.logical_not(here))
        def _():
            planes[pl.ds(snap * 24, 24), :] = jnp.zeros((24, NX), F32)

    for here, copies in fetches:

        @pl.when(here)
        def _():
            for copy in copies:
                copy.wait()

    lane = lax.broadcasted_iota(jnp.int32, (16, 128), 1)
    core = lax.rem(place, 2)

    def targets(n, carry):
        for other, out_ref in ((0, keep_ref), (1, give_ref)):
            j = 2 * n + (core + other * (1 - 2 * core))
            depth, half = n // 2, lax.rem(n, 2)
            base = pl.multiple_of(j * COLS, COLS)
            out_ref[depth, half, 0:96, :] = planes[:, pl.ds(base, 128)].astype(BF16)
            out_ref[depth, half, 96:192, :] = planes[:, pl.ds(base + 128, 128)].astype(BF16)
            after = pl.multiple_of(lax.rem(base + COLS, NX), 128)
            before = pl.multiple_of(lax.rem(base + NX - 128, NX), 128)
            packed = jnp.zeros((16, 128), F32)
            for pair in range(6):
                edge = jnp.where(
                    lane < 64,
                    planes[pl.ds(16 * pair, 16), pl.ds(after, 128)],
                    planes[pl.ds(16 * pair, 16), pl.ds(before, 128)],
                )
                edge = pltpu.roll(edge, 16 * pair + 8, 1)
                packed = jnp.where((lane >> 4) == pair, edge, packed)
            out_ref[depth, half, 192:208, :] = packed.astype(BF16)
        return carry

    lax.fori_loop(0, 8, targets, 0)


def pack(velocity, index):
    vmem = pl.BlockSpec(memory_space=pltpu.VMEM)
    blocks = jax.ShapeDtypeStruct((4, 2, 208, 128), BF16)
    return pl.pallas_call(
        pack_kernel,
        out_shape=(blocks, blocks),
        in_specs=[pl.BlockSpec(memory_space=pltpu.SMEM), pl.BlockSpec(memory_space=pl.ANY)],
        out_specs=(vmem, vmem),
        scratch_shapes=[pltpu.VMEM((96, NX), F32), pltpu.SemaphoreType.DMA((12,))],
        compiler_params=pltpu.CompilerParams(vmem_limit_bytes=10 * 1024 * 1024),
        cost_estimate=pl.CostEstimate(flops=0, bytes_accessed=1_000_000, transcendentals=0),
        name="pack",
    )(index, velocity)


def merge_kernel(keep_ref, got_ref, own, one, two, three):
    depth = lax.axis_index("gx") // 4
    high, low = depth // 2, lax.rem(depth, 2)
    for k, out_ref in enumerate((own, one, two, three)):
        flip_low = low if k % 2 == 0 else 1 - low
        flip_high = high if k // 2 == 0 else 1 - high
        at = 2 * flip_high + flip_low
        out_ref[...] = keep_ref[at] + got_ref[at]


def sides(even, a_ref, b_ref, rows):
    a, b = a_ref[rows, :].astype(F32), b_ref[rows, :].astype(F32)
    return jnp.where(even, b, a), jnp.where(even, a, b)


def lines_kernel(vel_ref, a_ref, b_ref, rows):
    rows[:, 24:32, :] = jnp.zeros((2, 8, NX), F32)
    for comp in range(3):
        for slot, at in ((0, 6), (1, 0)):
            for z in range(4):
                rows[slot, pl.ds(8 * comp + 2 * z, 2), :] = vel_ref[comp, z, at : at + 2, :]
    odd = lax.rem(lax.axis_index("grp"), 2)
    a_ref[...] = rows[odd].astype(BF16)
    b_ref[...] = rows[1 - odd].astype(BF16)


def outer_lines(velocity):
    slab = ((32, NX), BF16)
    return call(lines_kernel, "outer_lines", [slab, slab], [((2, 32, NX), F32)], 0, 8, velocity)


def planes_kernel(vel_ref, ya_ref, yb_ref, a_ref, b_ref, rows):
    before, after = sides(is_even("grp"), ya_ref, yb_ref, pl.ds(0, 32))
    for slot, base, edge in ((0, 2, 3), (1, 0, 0)):
        rows[slot, 48:64, :] = jnp.zeros((16, NX), F32)
        for comp in range(3):
            for p in range(2):
                rows[slot, pl.ds((comp * 2 + p) * 8, 8), :] = vel_ref[comp, base + p]
            at = 8 * comp + 2 * edge
            rows[slot, pl.ds(48 + 2 * comp, 1), :] = before[at + 1 : at + 2]
            rows[slot, pl.ds(49 + 2 * comp, 1), :] = after[at : at + 1]
    odd = lax.rem(lax.axis_index("gx"), 2)
    a_ref[...] = rows[odd].astype(BF16)
    b_ref[...] = rows[1 - odd].astype(BF16)


def outer_planes(velocity, ya, yb):
    slab = ((64, NX), BF16)
    return call(
        planes_kernel, "outer_planes", [slab, slab], [((2, 64, NX), F32)], 0, 10, velocity, ya, yb
    )


def stepped(center, z_minus, z_plus, y_minus, y_plus):
    wide = CHUNK + 256
    mid = [c[:, 128 : 128 + CHUNK] for c in center]
    half, mix = 0.5 * time_step, viscosity
    plus = [mix - half * u for u in mid]
    minus = [mix + half * u for u in mid]
    out = []
    for d in range(3):
        x_plus = pltpu.roll(center[d], wide - 1, 1)[:, 128 : 128 + CHUNK]
        x_minus = pltpu.roll(center[d], 1, 1)[:, 128 : 128 + CHUNK]
        along_z = plus[0] * z_plus[d] + minus[0] * z_minus[d]
        along_y = plus[1] * y_plus[d] + minus[1] * y_minus[d]
        along_x = plus[2] * x_plus + minus[2] * x_minus
        out.append(((1.0 - 6.0 * mix) * mid[d] + along_z) + (along_y + along_x))
    return out


def wrap(buf):
    buf[..., 0:128] = buf[..., NX : NX + 128]
    buf[..., NX + 128 : NX + 256] = buf[..., 128:256]


def lanes_of(n):
    wide = pl.ds(pl.multiple_of(n * CHUNK, 128), CHUNK + 256)
    here = pl.ds(pl.multiple_of(n * CHUNK + 128, 128), CHUNK)
    return wide, here


def step_one_kernel(vel_ref, za_ref, zb_ref, ya_ref, yb_ref, new, old, line):
    body = pl.ds(128, NX)
    even = is_even("gx")
    for comp in range(3):
        for z in range(4):
            old[comp, pl.ds(16 * (z + 2), 8), body] = vel_ref[comp, z]
        low, high = sides(even, za_ref, zb_ref, pl.ds(16 * comp, 16))
        for p in range(2):
            old[comp, pl.ds(16 * p, 8), body] = low[8 * p : 8 * p + 8]
            old[comp, pl.ds(16 * (p + 6), 8), body] = high[8 * p : 8 * p + 8]
    corners = sides(even, za_ref, zb_ref, pl.ds(48, 16))
    slabs = sides(is_even("grp"), ya_ref, yb_ref, pl.ds(0, 32))
    for side, row, own, near, far in ((0, -1, 0, 1, 0), (1, 8, 7, 0, 1)):
        for comp in range(3):
            for z in range(-1, 5):
                if 0 <= z < 4:
                    at = 8 * comp + 2 * z
                    value = slabs[side][at + near : at + near + 1]
                    line[side, comp, 0, pl.ds(2 + z, 1), body] = slabs[side][at + far : at + far + 1]
                    line[side, comp, 2, pl.ds(2 + z, 1), body] = vel_ref[comp, z, own : own + 1, :]
                else:
                    at = 2 * comp + side
                    value = corners[0 if z < 0 else 1][at : at + 1]
                line[side, comp, 1, pl.ds(2 + z, 1), body] = value
                old[comp, pl.ds(16 * (z + 2) + row, 1), body] = value
    wrap(old)
    wrap(line)

    def chunk(n, carry):
        wide, here = lanes_of(n)
        for z in range(-1, 5):
            at = 16 * (z + 2)
            get = lambda row, where: [old[c, pl.ds(row, 8), where] for c in range(3)]
            res = stepped(
                get(at, wide), get(at - 16, here), get(at + 16, here),
                get(at - 1, here), get(at + 1, here),
            )
            for c in range(3):
                new[c, pl.ds(16 * (z + 1), 8), here] = res[c]
        for side, row in ((0, -1), (1, 8)):
            center = [line[side, c, 1, :, wide] for c in range(3)]
            inner = [line[side, c, 1, :, here] for c in range(3)]
            outer = [line[side, c, 0, :, here] for c in range(3)]
            own = [line[side, c, 2, :, here] for c in range(3)]
            z_minus = [pltpu.roll(v, 1, 0) for v in inner]
            z_plus = [pltpu.roll(v, 7, 0) for v in inner]
            pair = (outer, own) if side == 0 else (own, outer)
            res = stepped(center, z_minus, z_plus, *pair)
            for c in range(3):
                for z in range(4):
                    new[c, pl.ds(16 * (z + 1) + row, 1), here] = res[c][2 + z : 3 + z]
        return carry

    lax.fori_loop(0, NX // CHUNK, chunk, 0)
    wrap(new)


def step_two_kernel(new, out_ref):
    def chunk(n, carry):
        wide, here = lanes_of(n)
        there = pl.ds(pl.multiple_of(n * CHUNK, 128), CHUNK)
        for z in range(4):
            at = 16 * (z + 1)
            get = lambda row, where: [new[c, pl.ds(row, 8), where] for c in range(3)]
            res = stepped(
                get(at, wide), get(at - 16, here), get(at + 16, here),
                get(at - 1, here), get(at + 1, here),
            )
            for c in range(3):
                out_ref[c, z, :, there] = res[c]
        return carry

    lax.fori_loop(0, NX // CHUNK, chunk, 0)


def step_one(velocity, za, zb, ya, yb):
    return call(
        step_one_kernel, "step_one", [((3, 16 * 6, NX + 256), F32)],
        [((3, 16 * 8, NX + 256), F32), ((2, 3, 3, 8, NX + 256), F32)],
        20_000_000, 24, velocity, za, zb, ya, yb,
    )[0]


def step_two(new):
    return call(
        step_two_kernel, "step_two", [((3, 4, ROWS, NX), F32)], [], 10_000_000, 12, new
    )[0]


def first_layer_places():
    places = np.zeros((6, 4, 144, 32), np.float32)
    for r in range(6):
        for group, col in enumerate(GROUP_COL):
            for a in range(3):
                for b in range(3):
                    for c in range(3):
                        j = b + 1 + col
                        places[r, group, j * 24 + c * 8 + r + a, a * 9 + b * 3 + c] = 1.0
    return places


def weights_kernel(
    places_ref, first_ref, second_ref, middle_ref, joined_ref, fine_ref, coarse_ref,
    w1_ref, w2_ref, w3_ref, w4_ref, hf_ref, hc_ref, flat,
):
    flat[...] = jnp.zeros((32, 64), F32)
    for tap in range(9):
        flat[pl.ds(3 * tap, 3), :] = first_ref[tap // 3, tap % 3].astype(F32)
    first_taps = flat[...].astype(BF16)
    for r in range(6):
        parts = [dot_nn(places_ref[r, g], first_taps) for g in range(4)]
        w1_ref[r] = jnp.concatenate(parts, axis=1).astype(BF16)

    none = jnp.zeros((64, 64), F32)

    def spread(taps, out_ref):
        for k in range(4):
            for group, col in enumerate(GROUP_COL):
                blocks = []
                for py in range(2):
                    for px in range(2):
                        a, b = k - py, col - px + 1
                        inside = 0 <= a <= 2 and 0 <= b <= 2
                        blocks.append(taps[a][b] if inside else none)
                block = jnp.concatenate(blocks, axis=1).astype(BF16)
                out_ref[pl.ds(k * 256 + group * 64, 64), :] = block

    spread([[second_ref[a, b].astype(F32).T for b in range(3)] for a in range(3)], w2_ref)

    wide_none = jnp.zeros((64, 128), F32)
    taps = [[middle_ref[a, b].astype(F32) for b in range(3)] for a in range(3)]
    for k in range(4):
        for place, b in enumerate((0, 2, 1, None)):
            blocks = []
            for e in range(2):
                inside = b is not None and 0 <= k - e <= 2
                blocks.append(taps[k - e][b] if inside else wide_none)
            block = jnp.concatenate(blocks, axis=1).astype(BF16)
            w3_ref[pl.ds(k * 256 + place * 64, 64), :] = block

    joined = [[joined_ref[a, b].astype(F32).T for b in range(3)] for a in range(3)]
    spread([[joined[a][b][128:192] for b in range(3)] for a in range(3)], w4_ref)
    for dy in range(3):
        for dx in range(3):
            blocks = []
            for py in range(2):
                for px in range(2):
                    total = jnp.zeros((128, 64), F32)
                    for a in range(3):
                        for b in range(3):
                            if (py + a - 1) // 2 + 1 == dy and (px + b - 1) // 2 + 1 == dx:
                                total = total + joined[a][b][0:128]
                    blocks.append(total)
            block = jnp.concatenate(blocks, axis=1).astype(BF16)
            w4_ref[pl.ds(1024 + (dy * 3 + dx) * 128, 128), :] = block

    head = fine_ref[...]
    high = head.astype(BF16).astype(F32)
    empty = jnp.zeros((NCLS, 64), F32)
    rows = []
    for part in (high, head - high):
        for spot in range(4):
            rows.append(jnp.concatenate([part if i == spot else empty for i in range(4)], axis=1))
    hf_ref[...] = jnp.concatenate(rows, axis=0).astype(BF16)
    head = coarse_ref[...]
    high = head.astype(BF16).astype(F32)
    hc_ref[...] = jnp.concatenate([high, head - high], axis=0).astype(BF16)


def block_weights(conv_first, conv_second, conv_middle, conv_joined, head_fine, head_coarse):
    swapped = (0, 1, 3, 2)
    return call(
        weights_kernel, "block_weights",
        [
            ((6, 144, 256), BF16), ((1024, 256), BF16), ((1024, 256), BF16),
            ((1024 + 1152, 256), BF16), ((64, 256), BF16), ((16, 128), BF16),
        ],
        [((32, 64), F32)], 0, 12,
        jnp.asarray(first_layer_places(), BF16), jnp.transpose(conv_first, swapped), conv_second,
        jnp.transpose(conv_middle, swapped), conv_joined, head_fine, head_coarse,
    )


def keep_padded(buf, value):
    buf[8 : 8 + M, :] = value
    buf[7:8, :] = value[M - 1 : M]
    buf[8 + M : 9 + M, :] = value[0:1]


def first_kernel(a_ref, mid_ref, b_ref, w1_ref, h1, win, taps):
    row384 = lax.broadcasted_iota(jnp.int32, (8, 384), 0)
    up, down = sides(is_even("grp"), a_ref, b_ref, pl.ds(0, 208))
    tiles = [up, mid_ref[...].astype(F32), down]
    for q in range(12):
        pieces = []
        for tile in tiles:
            edge = tile[192 + 8 * (q % 2) : 200 + 8 * (q % 2)]
            edge = pltpu.roll(edge, 128 - (16 * (q // 2) + 8), 1)
            pieces.append(
                jnp.concatenate([tile[8 * q : 8 * q + 8], tile[96 + 8 * q : 104 + 8 * q], edge], axis=1)
            )
        top, center, bottom = pieces
        snap, comp = q // 3, q % 3
        rows = pl.ds(comp * 8, 8)
        win[0, snap, rows, :] = jnp.where(row384 < 6, pltpu.roll(top, 6, 0), pltpu.roll(center, 6, 0))
        win[1, snap, rows, :] = center
        win[2, snap, rows, :] = jnp.where(row384 < 2, pltpu.roll(center, 2, 0), pltpu.roll(bottom, 2, 0))

    spot = lax.broadcasted_iota(jnp.int32, (XB, 384), 0)
    wanted = jnp.where(spot >= 142, 2 * spot + 94, 2 * spot - 2)
    wanted = jnp.where(wanted < 0, wanted + 384, wanted)
    even = (lax.broadcasted_iota(jnp.int32, (XB, 384), 1) == wanted).astype(F32).astype(BF16)
    own = lax.broadcasted_iota(jnp.int32, (XB, 144), 0) < 142
    for group in range(3):
        found = []
        for snap in range(SNAP):
            window = win[group, snap]
            shifted = [window] + [pltpu.roll(window, 384 - j, 1) for j in range(1, 6)]
            stack = jnp.concatenate(shifted, axis=0).astype(BF16)
            found.append(dot_nt(even, stack))
        for snap in range(SNAP):
            rows = jnp.where(own, found[snap], found[(snap + 1) % SNAP])
            taps[group, pl.ds(snap * XB, XB), :] = rows.astype(BF16)

    def first_row(i, carry):
        out = dot_nn(taps[i // 6], w1_ref[i % 6])
        h1[i] = jnp.maximum(out, 0.0).astype(BF16)
        return carry

    lax.fori_loop(0, 18, first_row, 0)


def second_kernel(h1, w2_ref, h2, ph, sbuf, pbuf):
    side = lax.broadcasted_iota(jnp.int32, (M, 128), 1) < 64

    def pool(q, out):
        pooled = jnp.maximum(out[:, 0:128], out[:, 128:256])
        pooled = jnp.maximum(pooled, pltpu.roll(pooled, 64, 1))
        keep_padded(pbuf, pooled)
        ph[q, :, 0:128] = jnp.where(side, pbuf[7 : 7 + M, :], pbuf[9 : 9 + M, :]).astype(BF16)
        ph[q, :, 128:256] = pooled.astype(BF16)

    def row(q):
        lhs = jnp.concatenate([h1[2 * q + k] for k in range(4)], axis=1)
        return jnp.maximum(dot_nn(lhs, w2_ref[...]), 0.0)

    def outer_row(t, carry):
        pool(7 * t, row(7 * t))
        return carry

    lax.fori_loop(0, 2, outer_row, 0)

    def inner_row(q, carry):
        out = row(q)
        keep_padded(sbuf, out)
        for py in range(2):
            lanes = pl.ds(128 * py, 128)
            h2[2 * q - 2 + py, :, 0:128] = out[:, 128 * py : 128 * py + 128].astype(BF16)
            beside = jnp.where(side, sbuf[9 : 9 + M, lanes], sbuf[7 : 7 + M, lanes])
            h2[2 * q - 2 + py, :, 128:256] = beside.astype(BF16)
        pool(q, out)
        return carry

    lax.fori_loop(1, 7, inner_row, 0)


def class_terms(logits, label):
    classes = lax.broadcasted_iota(jnp.int32, (NCLS, 128), 0).astype(F32)
    peak = jnp.max(logits, axis=0, keepdims=True)
    powers = jnp.exp(logits - peak)
    total = jnp.sum(powers, axis=0, keepdims=True)
    onehot = (classes == label).astype(F32)
    lost = onehot * (peak + jnp.log(total) - logits)
    return lost, powers / total - onehot


def middle_kernel(ph, w3_ref, hc_ref, labc_ref, mh, sums_ref, mbuf):
    def middle_rows(t, carry):
        lhs = jnp.concatenate([ph[2 * t + k] for k in range(4)], axis=1)
        out = jnp.maximum(dot_nn(lhs, w3_ref[...]), 0.0)
        for e in range(2):
            value = out[:, 128 * e : 128 * e + 128]
            keep_padded(mbuf, value)
            row = 2 * t + e
            mh[row, :, 0:128] = mbuf[7 : 7 + M, :].astype(BF16)
            mh[row, :, 128:256] = value.astype(BF16)
            mh[row, :, 256:384] = mbuf[9 : 9 + M, :].astype(BF16)
        return carry

    lax.fori_loop(0, 3, middle_rows, 0)

    lost_coarse = jnp.zeros((NCLS, 128), F32)
    grad_coarse = jnp.zeros((16, 128), F32)
    for y in range(4):
        for snap in range(SNAP):
            feature = mh[y + 1, pl.ds(snap * XB, 128), 128:256]
            both = dot_nt(hc_ref[...], feature)
            label = labc_ref[pl.ds(snap * 4 + y, 1), :].astype(F32)
            lost, grad = class_terms(both[0:8] + both[8:16], label)
            lost_coarse = lost_coarse + lost
            high, low = split_two(grad)
            grad_coarse = grad_coarse + dot_nn(
                jnp.concatenate([high.astype(F32), low.astype(F32)], axis=0).astype(BF16), feature
            )
    coarse_cells = 262144.0
    sums_ref[0:8, :] = (grad_coarse[0:8] + grad_coarse[8:16]) * (1.0 / coarse_cells)
    sums_ref[8:16, :] = lost_coarse * (1.0 / coarse_cells)


def decoded_kernel(
    h2, mh, w4_ref, hf_ref, labf_ref, coarse_ref, logits_ref, sums_ref, dec, labs, planar
):
    def decoded_row(y, carry):
        lhs = jnp.concatenate(
            [h2[2 * y + 1 + k] for k in range(4)] + [mh[y + k] for k in range(3)], axis=1
        )
        dec[y] = jnp.maximum(dot_nn(lhs, w4_ref[...]), 0.0).astype(BF16)
        return carry

    lax.fori_loop(0, 4, decoded_row, 0)

    col = lax.broadcasted_iota(jnp.int32, (256, 256), 0)
    planar_col = lax.broadcasted_iota(jnp.int32, (256, 256), 1)
    to_planar = (col == 2 * (planar_col & 127) + (planar_col >> 7)).astype(F32).astype(BF16)
    labs[...] = dot_nn(labf_ref[...].astype(F32).astype(BF16), to_planar)
    to_cols = (planar_col == 2 * (col & 127) + (col >> 7)).astype(F32).astype(BF16)

    lost_fine = jnp.zeros((NCLS, 128), F32)
    grad_fine = jnp.zeros((64, 256), F32)
    for y in range(4):
        for snap in range(SNAP):
            feature = dec[y, pl.ds(snap * XB, 128), :]
            both = dot_nt(hf_ref[...], feature)
            logits = both[0:32] + both[32:64]
            slopes = []
            for py in range(2):
                row = snap * 8 + 2 * y + py
                for px in range(2):
                    mine = logits[(2 * py + px) * 8 : (2 * py + px) * 8 + 8]
                    planar[pl.ds(row * 8, 8), pl.ds(128 * px, 128)] = mine
                    lost, grad = class_terms(mine, labs[pl.ds(row, 1), pl.ds(128 * px, 128)])
                    lost_fine = lost_fine + lost
                    slopes.append(grad)
            high, low = split_two(jnp.concatenate(slopes, axis=0))
            grad_fine = grad_fine + dot_nn(jnp.concatenate([high, low], axis=0), feature)

    whole = planar[...]
    high = whole.astype(BF16)
    rest = whole - high.astype(F32)
    middle_term = rest.astype(BF16)
    low = (rest - middle_term.astype(F32)).astype(BF16)
    ordered = dot_nn(high, to_cols) + dot_nn(middle_term, to_cols) + dot_nn(low, to_cols)
    for row in range(32):
        logits_ref[row] = ordered[8 * row : 8 * row + 8]

    fine_cells = 1048576.0
    total = jnp.zeros((NCLS, 64), F32)
    for spot in range(4):
        for part in (0, 32):
            block = grad_fine[part + 8 * spot : part + 8 * spot + 8]
            total = total + block[:, 64 * spot : 64 * spot + 64]
    loss = jnp.sum(lost_fine) * (1.0 / fine_cells) + jnp.sum(coarse_ref[8:16, :])
    sums_ref[0:8, :] = coarse_ref[0:8, :]
    sums_ref[8:16, :] = jnp.concatenate(
        [total * (1.0 / fine_cells), jnp.broadcast_to(loss, (NCLS, 64))], axis=1
    )


def first(a, mid, b, w1):
    return call(
        first_kernel, "first", [((18, M, 256), BF16)],
        [((3, SNAP, 24, 384), F32), ((3, M, 144), BF16)],
        2_000_000_000, 14, a, mid, b, w1,
    )[0]


def second(h1, w2):
    return call(
        second_kernel, "second", [((12, M, 256), BF16), ((8, M, 256), BF16)],
        [((M + 16, 256), F32), ((M + 16, 128), F32)],
        2_500_000_000, 18, h1, w2,
    )


def middle(ph, w3, hc, labels):
    return call(
        middle_kernel, "middle", [((6, M, 384), BF16), ((16, 128), F32)],
        [((M + 16, 128), F32)], 1_000_000_000, 12, ph, w3, hc, labels,
    )


def decoded(h2, mh, w4, hf, labels, coarse):
    return call(
        decoded_kernel, "decoded", [((32, NCLS, COLS), F32), ((16, 128), F32)],
        [((4, M, 256), BF16), ((32, 256), F32), ((256, 256), F32)],
        2_500_000_000, 16, h2, mh, w4, hf, labels, coarse,
    )


def mesh_pairs(change):
    pairs = []
    for device in range(128):
        grp, gx = device // 16, device % 16
        at = {"x": (gx // 2 % 2) * 2 + grp // 4, "y": grp % 4, "z": gx // 4, "core": gx % 2}
        change(at)
        grp = (at["x"] % 2) * 4 + at["y"]
        gx = (at["z"] * 2 + at["x"] // 2) * 2 + at["core"]
        pairs.append((device, grp * 16 + gx))
    return pairs


def flip(x, name, bits):
    def change(at):
        at[name] ^= bits

    return lax.ppermute(x, AXES, mesh_pairs(change))


def finish_kernel(a, b, c, d, loss, fine, coarse):
    total = (a[...] + b[...]) + (c[...] + d[...])
    coarse[...] = total[0:8]
    fine[...] = total[8:16, 0:64]
    loss[...] = total[8:9, 64:65]


tie = lax.optimization_barrier


def body(
    velocity, snapshot_index, labels_fine, labels_coarse,
    conv_first, conv_second, conv_middle, conv_joined, head_fine, head_coarse,
):
    keep, give = pack(velocity, snapshot_index)
    line_a, line_b = outer_lines(velocity)
    weights = block_weights(conv_first, conv_second, conv_middle, conv_joined, head_fine, head_coarse)
    got = exchange_a(give, "gx")
    block = ((2, 208, 128), BF16)
    own, one, two, three = call(merge_kernel, "merge", [block] * 4, [], 1, 8, keep, got)
    own, line_a, line_b = tie((own, line_a, line_b))
    two, one, three = flip(two, "z", 2), flip(one, "z", 1), flip(three, "z", 3)
    line_a, line_b = exchange_a(line_a, "grp"), exchange_b(line_b, "grp")
    own, weights = tie((own, weights))
    own = (own + two) + (one + three)
    pick = functools.partial(lax.dynamic_index_in_dim, keepdims=False)
    half = (lax.axis_index("gx") // 2) % 2
    mine, theirs = pick(own, half, 0), pick(own, 1 - half, 0)
    got = lax.ppermute(theirs, "gx", [(i, i ^ 2) for i in range(16)])
    mine, line_a, line_b = tie((mine, line_a, line_b))
    plane_a, plane_b = outer_planes(velocity, line_a, line_b)
    tile = mine + got
    tile, plane_a, plane_b = tie((tile, plane_a, plane_b))
    tile_a, tile_b = exchange_a(tile, "grp"), exchange_b(tile, "grp")
    plane_b, plane_a = exchange_b(plane_b, "gx"), exchange_a(plane_a, "gx")
    w1, w2, w3, w4, hf, hc = weights
    h2, ph = second(first(tile_a, tile, tile_b, w1), w2)
    mh, coarse = middle(ph, w3, hc, labels_coarse.reshape(SNAP * 4, 128))
    logits, sums = decoded(h2, mh, w4, hf, labels_fine.reshape(SNAP * ROWS, COLS), coarse)

    sums, plane_a, plane_b = tie((sums, plane_a, plane_b))
    sums = sums + flip(sums, "core", 1)
    sums, plane_a, plane_b = tie((sums, plane_a, plane_b))
    got = flip(sums, "z", 1)
    new = step_one(velocity, plane_a, plane_b, line_a, line_b)
    sums, new = tie((sums + got, new))
    got = flip(sums, "z", 3)
    field = step_two(new)
    sums, field = tie((sums + got, field))
    sums = (sums + flip(sums, "y", 1)) + (flip(sums, "y", 2) + flip(sums, "y", 3))
    loss, grad_fine, grad_coarse = call(
        finish_kernel, "finish", [((1, 1), F32), ((8, 64), F32), ((8, 128), F32)], [], 1, 4,
        sums, flip(sums, "x", 1), flip(sums, "x", 2), flip(sums, "x", 3),
    )
    return (
        field,
        logits.reshape(SNAP, ROWS, NCLS, COLS),
        loss.reshape(()),
        grad_fine,
        grad_coarse,
    )


def solution(mesh):
    return jax.shard_map(
        body,
        mesh=mesh,
        in_specs=(
            P(None, "gx", "grp", None),
            P(),
            P(None, "grp", "gx"),
            P(None, "grp", "gx"),
            P(),
            P(),
            P(),
            P(),
            P(),
            P(),
        ),
        out_specs=(P(None, "gx", "grp", None), P(None, "grp", None, "gx"), P(), P(), P()),
        check_vma=False,
    )
```

```python
import functools

import jax
import jax.numpy as jnp
import numpy as np
from jax import lax
from jax.experimental import pallas as pl
from jax.experimental.pallas import tpu as pltpu
from jax.sharding import PartitionSpec as P

F32, BF16 = jnp.float32, jnp.bfloat16
AXES = ("grp", "gx")
SNAP, NCLS = 4, 8
ROWS, COLS = 8, 256
XB = 144
M = SNAP * XB
NX = 4096
CHUNK = 1024
time_step = 0.2
viscosity = 0.1
GROUP_COL = (0, 1, 2, -1)


def dot_nn(a, b):
    return lax.dot_general(a, b, (((1,), (0,)), ((), ())), preferred_element_type=F32)


def dot_nt(a, b):
    return lax.dot_general(a, b, (((1,), (1,)), ((), ())), preferred_element_type=F32)


def split_two(value):
    high = value.astype(BF16)
    return high, (value - high.astype(F32)).astype(BF16)


def call(kernel, name, outs, scratch, flops, limit, *args, scalars=0):
    vmem = pl.BlockSpec(memory_space=pltpu.VMEM)
    smem = pl.BlockSpec(memory_space=pltpu.SMEM)
    return pl.pallas_call(
        kernel,
        out_shape=tuple(jax.ShapeDtypeStruct(*out) for out in outs),
        in_specs=[smem] * scalars + [vmem] * (len(args) - scalars),
        out_specs=(vmem,) * len(outs),
        scratch_shapes=[pltpu.VMEM(*one) for one in scratch],
        compiler_params=pltpu.CompilerParams(vmem_limit_bytes=limit * 1024 * 1024),
        cost_estimate=pl.CostEstimate(flops=flops, bytes_accessed=1_000_000, transcendentals=0),
        name=name,
    )(*args)


def exchange_a(x, axis):
    return lax.ppermute(x, axis, [(i, i ^ 1) for i in range(lax.axis_size(axis))])


def exchange_b(x, axis):
    count = lax.axis_size(axis)
    return lax.ppermute(x, axis, [(i, (((i + 1) ^ 1) - 1) % count) for i in range(count)])


def is_even(axis):
    return lax.rem(lax.axis_index(axis), 2) == 0


def pack_kernel(index_hbm, vel_ref, keep_ref, give_ref, planes, index_ref, sems):
    copy = pltpu.make_async_copy(index_hbm, index_ref, sems.at[12])
    copy.start()
    copy.wait()
    place = lax.axis_index("gx")
    fetches = []
    for snap in range(SNAP):
        local = index_ref[snap] - place * 4
        here = jnp.logical_and(local >= 0, local < 4)
        spot = jnp.clip(local, 0, 3)
        copies = [
            pltpu.make_async_copy(
                vel_ref.at[comp, spot],
                planes.at[pl.ds((snap * 3 + comp) * ROWS, ROWS), :],
                sems.at[snap * 3 + comp],
            )
            for comp in range(3)
        ]
        fetches.append((here, copies))

        @pl.when(here)
        def _():
            for copy in copies:
                copy.start()

        @pl.when(jnp.logical_not(here))
        def _():
            planes[pl.ds(snap * 24, 24), :] = jnp.zeros((24, NX), F32)

    for here, copies in fetches:

        @pl.when(here)
        def _():
            for copy in copies:
                copy.wait()

    lane = lax.broadcasted_iota(jnp.int32, (16, 128), 1)
    core = lax.rem(place, 2)

    def targets(n, carry):
        for other, out_ref in ((0, keep_ref), (1, give_ref)):
            j = 2 * n + (core + other * (1 - 2 * core))
            depth, half = n // 2, lax.rem(n, 2)
            base = pl.multiple_of(j * COLS, COLS)
            out_ref[depth, half, 0:96, :] = planes[:, pl.ds(base, 128)].astype(BF16)
            out_ref[depth, half, 96:192, :] = planes[:, pl.ds(base + 128, 128)].astype(BF16)
            after = pl.multiple_of(lax.rem(base + COLS, NX), 128)
            before = pl.multiple_of(lax.rem(base + NX - 128, NX), 128)
            packed = jnp.zeros((16, 128), F32)
            for pair in range(6):
                edge = jnp.where(
                    lane < 64,
                    planes[pl.ds(16 * pair, 16), pl.ds(after, 128)],
                    planes[pl.ds(16 * pair, 16), pl.ds(before, 128)],
                )
                edge = pltpu.roll(edge, 16 * pair + 8, 1)
                packed = jnp.where((lane >> 4) == pair, edge, packed)
            out_ref[depth, half, 192:208, :] = packed.astype(BF16)
        return carry

    lax.fori_loop(0, 8, targets, 0)


def pack(velocity, index):
    vmem = pl.BlockSpec(memory_space=pltpu.VMEM)
    blocks = jax.ShapeDtypeStruct((4, 2, 208, 128), BF16)
    return pl.pallas_call(
        pack_kernel,
        out_shape=(blocks, blocks),
        in_specs=[pl.BlockSpec(memory_space=pltpu.HBM)] * 2,
        out_specs=(vmem, vmem),
        scratch_shapes=[
            pltpu.VMEM((96, NX), F32),
            pltpu.SMEM((SNAP,), jnp.int32),
            pltpu.SemaphoreType.DMA((13,)),
        ],
        compiler_params=pltpu.CompilerParams(vmem_limit_bytes=10 * 1024 * 1024),
        cost_estimate=pl.CostEstimate(flops=0, bytes_accessed=1_000_000, transcendentals=0),
        name="pack",
    )(
        pltpu.with_memory_space_constraint(index, pltpu.HBM),
        pltpu.with_memory_space_constraint(velocity, pltpu.HBM),
    )


def merge_kernel(keep_ref, got_ref, own, one, two, three):
    depth = lax.axis_index("gx") // 4
    high, low = depth // 2, lax.rem(depth, 2)
    for k, out_ref in enumerate((own, one, two, three)):
        flip_low = low if k % 2 == 0 else 1 - low
        flip_high = high if k // 2 == 0 else 1 - high
        at = 2 * flip_high + flip_low
        out_ref[...] = keep_ref[at] + got_ref[at]


def sides(even, a_ref, b_ref, rows):
    a, b = a_ref[rows, :].astype(F32), b_ref[rows, :].astype(F32)
    return jnp.where(even, b, a), jnp.where(even, a, b)


def lines_kernel(vel_ref, a_ref, b_ref, rows):
    rows[:, 24:32, :] = jnp.zeros((2, 8, NX), F32)
    for comp in range(3):
        for slot, at in ((0, 6), (1, 0)):
            for z in range(4):
                rows[slot, pl.ds(8 * comp + 2 * z, 2), :] = vel_ref[comp, z, at : at + 2, :]
    odd = lax.rem(lax.axis_index("grp"), 2)
    a_ref[...] = rows[odd].astype(BF16)
    b_ref[...] = rows[1 - odd].astype(BF16)


def outer_lines(velocity):
    slab = ((32, NX), BF16)
    return call(lines_kernel, "outer_lines", [slab, slab], [((2, 32, NX), F32)], 0, 8, velocity)


def planes_kernel(vel_ref, ya_ref, yb_ref, a_ref, b_ref, rows):
    before, after = sides(is_even("grp"), ya_ref, yb_ref, pl.ds(0, 32))
    for slot, base, edge in ((0, 2, 3), (1, 0, 0)):
        rows[slot, 48:64, :] = jnp.zeros((16, NX), F32)
        for comp in range(3):
            for p in range(2):
                rows[slot, pl.ds((comp * 2 + p) * 8, 8), :] = vel_ref[comp, base + p]
            at = 8 * comp + 2 * edge
            rows[slot, pl.ds(48 + 2 * comp, 1), :] = before[at + 1 : at + 2]
            rows[slot, pl.ds(49 + 2 * comp, 1), :] = after[at : at + 1]
    odd = lax.rem(lax.axis_index("gx"), 2)
    a_ref[...] = rows[odd].astype(BF16)
    b_ref[...] = rows[1 - odd].astype(BF16)


def outer_planes(velocity, ya, yb):
    slab = ((64, NX), BF16)
    return call(
        planes_kernel, "outer_planes", [slab, slab], [((2, 64, NX), F32)], 0, 10, velocity, ya, yb
    )


def stepped(center, z_minus, z_plus, y_minus, y_plus):
    wide = CHUNK + 256
    mid = [c[:, 128 : 128 + CHUNK] for c in center]
    half, mix = 0.5 * time_step, viscosity
    plus = [mix - half * u for u in mid]
    minus = [mix + half * u for u in mid]
    out = []
    for d in range(3):
        x_plus = pltpu.roll(center[d], wide - 1, 1)[:, 128 : 128 + CHUNK]
        x_minus = pltpu.roll(center[d], 1, 1)[:, 128 : 128 + CHUNK]
        along_z = plus[0] * z_plus[d] + minus[0] * z_minus[d]
        along_y = plus[1] * y_plus[d] + minus[1] * y_minus[d]
        along_x = plus[2] * x_plus + minus[2] * x_minus
        out.append(((1.0 - 6.0 * mix) * mid[d] + along_z) + (along_y + along_x))
    return out


def wrap(buf):
    buf[..., 0:128] = buf[..., NX : NX + 128]
    buf[..., NX + 128 : NX + 256] = buf[..., 128:256]


def lanes_of(n):
    wide = pl.ds(pl.multiple_of(n * CHUNK, 128), CHUNK + 256)
    here = pl.ds(pl.multiple_of(n * CHUNK + 128, 128), CHUNK)
    return wide, here


def step_one_kernel(vel_ref, za_ref, zb_ref, ya_ref, yb_ref, new, old, line):
    body = pl.ds(128, NX)
    even = is_even("gx")
    for comp in range(3):
        for z in range(4):
            old[comp, pl.ds(16 * (z + 2), 8), body] = vel_ref[comp, z]
        low, high = sides(even, za_ref, zb_ref, pl.ds(16 * comp, 16))
        for p in range(2):
            old[comp, pl.ds(16 * p, 8), body] = low[8 * p : 8 * p + 8]
            old[comp, pl.ds(16 * (p + 6), 8), body] = high[8 * p : 8 * p + 8]
    corners = sides(even, za_ref, zb_ref, pl.ds(48, 16))
    slabs = sides(is_even("grp"), ya_ref, yb_ref, pl.ds(0, 32))
    for side, row, own, near, far in ((0, -1, 0, 1, 0), (1, 8, 7, 0, 1)):
        for comp in range(3):
            for z in range(-1, 5):
                if 0 <= z < 4:
                    at = 8 * comp + 2 * z
                    value = slabs[side][at + near : at + near + 1]
                    line[side, comp, 0, pl.ds(2 + z, 1), body] = slabs[side][at + far : at + far + 1]
                    line[side, comp, 2, pl.ds(2 + z, 1), body] = vel_ref[comp, z, own : own + 1, :]
                else:
                    at = 2 * comp + side
                    value = corners[0 if z < 0 else 1][at : at + 1]
                line[side, comp, 1, pl.ds(2 + z, 1), body] = value
                old[comp, pl.ds(16 * (z + 2) + row, 1), body] = value
    wrap(old)
    wrap(line)

    def chunk(n, carry):
        wide, here = lanes_of(n)
        for z in range(-1, 5):
            at = 16 * (z + 2)
            get = lambda row, where: [old[c, pl.ds(row, 8), where] for c in range(3)]
            res = stepped(
                get(at, wide), get(at - 16, here), get(at + 16, here),
                get(at - 1, here), get(at + 1, here),
            )
            for c in range(3):
                new[c, pl.ds(16 * (z + 1), 8), here] = res[c]
        for side, row in ((0, -1), (1, 8)):
            center = [line[side, c, 1, :, wide] for c in range(3)]
            inner = [line[side, c, 1, :, here] for c in range(3)]
            outer = [line[side, c, 0, :, here] for c in range(3)]
            own = [line[side, c, 2, :, here] for c in range(3)]
            z_minus = [pltpu.roll(v, 1, 0) for v in inner]
            z_plus = [pltpu.roll(v, 7, 0) for v in inner]
            pair = (outer, own) if side == 0 else (own, outer)
            res = stepped(center, z_minus, z_plus, *pair)
            for c in range(3):
                for z in range(4):
                    new[c, pl.ds(16 * (z + 1) + row, 1), here] = res[c][2 + z : 3 + z]
        return carry

    lax.fori_loop(0, NX // CHUNK, chunk, 0)
    wrap(new)


def step_two_kernel(new, out_ref):
    def chunk(n, carry):
        wide, here = lanes_of(n)
        there = pl.ds(pl.multiple_of(n * CHUNK, 128), CHUNK)
        for z in range(4):
            at = 16 * (z + 1)
            get = lambda row, where: [new[c, pl.ds(row, 8), where] for c in range(3)]
            res = stepped(
                get(at, wide), get(at - 16, here), get(at + 16, here),
                get(at - 1, here), get(at + 1, here),
            )
            for c in range(3):
                out_ref[c, z, :, there] = res[c]
        return carry

    lax.fori_loop(0, NX // CHUNK, chunk, 0)


def step_one(velocity, za, zb, ya, yb):
    return call(
        step_one_kernel, "step_one", [((3, 16 * 6, NX + 256), F32)],
        [((3, 16 * 8, NX + 256), F32), ((2, 3, 3, 8, NX + 256), F32)],
        20_000_000, 24, velocity, za, zb, ya, yb,
    )[0]


def step_two(new):
    return call(
        step_two_kernel, "step_two", [((3, 4, ROWS, NX), F32)], [], 10_000_000, 12, new
    )[0]


def first_layer_places():
    places = np.zeros((6, 4, 144, 32), np.float32)
    for r in range(6):
        for group, col in enumerate(GROUP_COL):
            for a in range(3):
                for b in range(3):
                    for c in range(3):
                        j = b + 1 + col
                        places[r, group, j * 24 + c * 8 + r + a, a * 9 + b * 3 + c] = 1.0
    return places


def weights_kernel(
    places_ref, first_ref, second_ref, middle_ref, joined_ref, fine_ref, coarse_ref,
    w1_ref, w2_ref, w3_ref, w4_ref, hf_ref, hc_ref, flat,
):
    flat[...] = jnp.zeros((32, 64), F32)
    for tap in range(9):
        flat[pl.ds(3 * tap, 3), :] = first_ref[tap // 3, tap % 3].astype(F32)
    first_taps = flat[...].astype(BF16)
    for r in range(6):
        parts = [dot_nn(places_ref[r, g], first_taps) for g in range(4)]
        w1_ref[r] = jnp.concatenate(parts, axis=1).astype(BF16)

    none = jnp.zeros((64, 64), F32)

    def spread(taps, out_ref):
        for k in range(4):
            for group, col in enumerate(GROUP_COL):
                blocks = []
                for py in range(2):
                    for px in range(2):
                        a, b = k - py, col - px + 1
                        inside = 0 <= a <= 2 and 0 <= b <= 2
                        blocks.append(taps[a][b] if inside else none)
                block = jnp.concatenate(blocks, axis=1).astype(BF16)
                out_ref[pl.ds(k * 256 + group * 64, 64), :] = block

    spread([[second_ref[a, b].astype(F32).T for b in range(3)] for a in range(3)], w2_ref)

    wide_none = jnp.zeros((64, 128), F32)
    taps = [[middle_ref[a, b].astype(F32) for b in range(3)] for a in range(3)]
    for k in range(4):
        for place, b in enumerate((0, 2, 1, None)):
            blocks = []
            for e in range(2):
                inside = b is not None and 0 <= k - e <= 2
                blocks.append(taps[k - e][b] if inside else wide_none)
            block = jnp.concatenate(blocks, axis=1).astype(BF16)
            w3_ref[pl.ds(k * 256 + place * 64, 64), :] = block

    joined = [[joined_ref[a, b].astype(F32).T for b in range(3)] for a in range(3)]
    spread([[joined[a][b][128:192] for b in range(3)] for a in range(3)], w4_ref)
    for dy in range(3):
        for dx in range(3):
            blocks = []
            for py in range(2):
                for px in range(2):
                    total = jnp.zeros((128, 64), F32)
                    for a in range(3):
                        for b in range(3):
                            if (py + a - 1) // 2 + 1 == dy and (px + b - 1) // 2 + 1 == dx:
                                total = total + joined[a][b][0:128]
                    blocks.append(total)
            block = jnp.concatenate(blocks, axis=1).astype(BF16)
            w4_ref[pl.ds(1024 + (dy * 3 + dx) * 128, 128), :] = block

    head = fine_ref[...]
    high = head.astype(BF16).astype(F32)
    empty = jnp.zeros((NCLS, 64), F32)
    rows = []
    for part in (high, head - high):
        for spot in range(4):
            rows.append(jnp.concatenate([part if i == spot else empty for i in range(4)], axis=1))
    hf_ref[...] = jnp.concatenate(rows, axis=0).astype(BF16)
    head = coarse_ref[...]
    high = head.astype(BF16).astype(F32)
    hc_ref[...] = jnp.concatenate([high, head - high], axis=0).astype(BF16)


def block_weights(conv_first, conv_second, conv_middle, conv_joined, head_fine, head_coarse):
    swapped = (0, 1, 3, 2)
    return call(
        weights_kernel, "block_weights",
        [
            ((6, 144, 256), BF16), ((1024, 256), BF16), ((1024, 256), BF16),
            ((1024 + 1152, 256), BF16), ((64, 256), BF16), ((16, 128), BF16),
        ],
        [((32, 64), F32)], 0, 12,
        jnp.asarray(first_layer_places(), BF16), jnp.transpose(conv_first, swapped), conv_second,
        jnp.transpose(conv_middle, swapped), conv_joined, head_fine, head_coarse,
    )


def keep_padded(buf, value):
    buf[8 : 8 + M, :] = value
    buf[7:8, :] = value[M - 1 : M]
    buf[8 + M : 9 + M, :] = value[0:1]


def first_kernel(a_ref, mid_ref, b_ref, w1_ref, h1, win, taps):
    row384 = lax.broadcasted_iota(jnp.int32, (8, 384), 0)
    up, down = sides(is_even("grp"), a_ref, b_ref, pl.ds(0, 208))
    tiles = [up, mid_ref[...].astype(F32), down]
    for q in range(12):
        pieces = []
        for tile in tiles:
            edge = tile[192 + 8 * (q % 2) : 200 + 8 * (q % 2)]
            edge = pltpu.roll(edge, 128 - (16 * (q // 2) + 8), 1)
            pieces.append(
                jnp.concatenate([tile[8 * q : 8 * q + 8], tile[96 + 8 * q : 104 + 8 * q], edge], axis=1)
            )
        top, center, bottom = pieces
        snap, comp = q // 3, q % 3
        rows = pl.ds(comp * 8, 8)
        win[0, snap, rows, :] = jnp.where(row384 < 6, pltpu.roll(top, 6, 0), pltpu.roll(center, 6, 0))
        win[1, snap, rows, :] = center
        win[2, snap, rows, :] = jnp.where(row384 < 2, pltpu.roll(center, 2, 0), pltpu.roll(bottom, 2, 0))

    spot = lax.broadcasted_iota(jnp.int32, (XB, 384), 0)
    wanted = jnp.where(spot >= 142, 2 * spot + 94, 2 * spot - 2)
    wanted = jnp.where(wanted < 0, wanted + 384, wanted)
    even = (lax.broadcasted_iota(jnp.int32, (XB, 384), 1) == wanted).astype(F32).astype(BF16)
    own = lax.broadcasted_iota(jnp.int32, (XB, 144), 0) < 142
    for group in range(3):
        found = []
        for snap in range(SNAP):
            window = win[group, snap]
            shifted = [window] + [pltpu.roll(window, 384 - j, 1) for j in range(1, 6)]
            stack = jnp.concatenate(shifted, axis=0).astype(BF16)
            found.append(dot_nt(even, stack))
        for snap in range(SNAP):
            rows = jnp.where(own, found[snap], found[(snap + 1) % SNAP])
            taps[group, pl.ds(snap * XB, XB), :] = rows.astype(BF16)

    for i in range(18):
        out = dot_nn(taps[i // 6], w1_ref[i % 6])
        h1[i] = jnp.maximum(out, 0.0).astype(BF16)


def second_kernel(h1, w2_ref, h2, ph, sbuf, pbuf):
    side = lax.broadcasted_iota(jnp.int32, (M, 128), 1) < 64

    def pool(q, out):
        pooled = jnp.maximum(out[:, 0:128], out[:, 128:256])
        pooled = jnp.maximum(pooled, pltpu.roll(pooled, 64, 1))
        keep_padded(pbuf, pooled)
        ph[q, :, 0:128] = jnp.where(side, pbuf[7 : 7 + M, :], pbuf[9 : 9 + M, :]).astype(BF16)
        ph[q, :, 128:256] = pooled.astype(BF16)

    def row(q):
        lhs = jnp.concatenate([h1[2 * q + k] for k in range(4)], axis=1)
        return jnp.maximum(dot_nn(lhs, w2_ref[...]), 0.0)

    for q in range(8):
        out = row(q)
        if 0 < q < 7:
            keep_padded(sbuf, out)
            for py in range(2):
                lanes = pl.ds(128 * py, 128)
                h2[2 * q - 2 + py, :, 0:128] = out[:, 128 * py : 128 * py + 128].astype(BF16)
                beside = jnp.where(side, sbuf[9 : 9 + M, lanes], sbuf[7 : 7 + M, lanes])
                h2[2 * q - 2 + py, :, 128:256] = beside.astype(BF16)
        pool(q, out)


def class_terms(logits, label):
    classes = lax.broadcasted_iota(jnp.int32, logits.shape, 0).astype(F32)
    peak = jnp.max(logits, axis=0, keepdims=True)
    powers = jnp.exp(logits - peak)
    total = jnp.sum(powers, axis=0, keepdims=True)
    onehot = (classes == label).astype(F32)
    lost = onehot * (peak + jnp.log(total) - logits)
    return lost, powers / total - onehot


def cells(kept, lanes):
    return jnp.concatenate(
        [kept[y, pl.ds(snap * XB, 128), lanes] for y in kept_rows(kept) for snap in range(SNAP)], axis=0
    )


def kept_rows(kept):
    return range(1, 5) if kept.shape[0] == 6 else range(4)


def fold(lost):
    total = lost[:, 0:128]
    for block in range(1, 16):
        total = total + lost[:, 128 * block : 128 * block + 128]
    return total


def middle_kernel(ph, w3_ref, hc_ref, labc_ref, mh, sums_ref, mbuf):
    def middle_rows(t, carry):
        lhs = jnp.concatenate([ph[2 * t + k] for k in range(4)], axis=1)
        out = jnp.maximum(dot_nn(lhs, w3_ref[...]), 0.0)
        for e in range(2):
            value = out[:, 128 * e : 128 * e + 128]
            keep_padded(mbuf, value)
            row = 2 * t + e
            mh[row, :, 0:128] = mbuf[7 : 7 + M, :].astype(BF16)
            mh[row, :, 128:256] = value.astype(BF16)
            mh[row, :, 256:384] = mbuf[9 : 9 + M, :].astype(BF16)
        return carry

    lax.fori_loop(0, 3, middle_rows, 0)

    feature = cells(mh, pl.ds(128, 128))
    both = dot_nt(hc_ref[...], feature)
    label = jnp.concatenate(
        [labc_ref[pl.ds(snap * 4 + y, 1), :] for y in range(4) for snap in range(SNAP)], axis=1
    ).astype(F32)
    lost, grad = class_terms(both[0:8] + both[8:16], label)
    high = grad.astype(BF16).astype(F32)
    slopes = jnp.concatenate([high, grad - high], axis=0).astype(BF16)
    total = dot_nn(slopes, feature)
    coarse_cells = 262144.0
    sums_ref[0:8, :] = (total[0:8] + total[8:16]) * (1.0 / coarse_cells)
    sums_ref[8:16, :] = fold(lost) * (1.0 / coarse_cells)


def decoded_kernel(
    h2, mh, w4_ref, hf_ref, labf_ref, coarse_ref, logits_ref, sums_ref, dec, labs
):
    for y in range(4):
        lhs = jnp.concatenate(
            [h2[2 * y + 1 + k] for k in range(4)] + [mh[y + k] for k in range(3)], axis=1
        )
        dec[y] = jnp.maximum(dot_nn(lhs, w4_ref[...]), 0.0).astype(BF16)

    col = lax.broadcasted_iota(jnp.int32, (256, 256), 0)
    planar_col = lax.broadcasted_iota(jnp.int32, (256, 256), 1)
    to_planar = (col == 2 * (planar_col & 127) + (planar_col >> 7)).astype(F32).astype(BF16)
    labs[...] = dot_nn(labf_ref[...].astype(F32).astype(BF16), to_planar)
    to_cols = (planar_col == 2 * (col & 127) + (col >> 7)).astype(F32).astype(BF16)

    feature = cells(dec, pl.ds(0, 256))
    both = dot_nt(hf_ref[...], feature)
    logits = both[0:32] + both[32:64]
    lost_fine = jnp.zeros((NCLS, 2048), F32)
    slopes = []
    for py in range(2):
        for px in range(2):
            lanes = pl.ds(128 * px, 128)
            label = jnp.concatenate(
                [labs[pl.ds(snap * 8 + 2 * y + py, 1), lanes] for y in range(4) for snap in range(SNAP)],
                axis=1,
            )
            at = (2 * py + px) * 8
            lost, grad = class_terms(logits[at : at + 8], label)
            lost_fine = lost_fine + lost
            slopes.append(grad)
    high, low = split_two(jnp.concatenate(slopes, axis=0))
    grad_fine = dot_nn(jnp.concatenate([high, low], axis=0), feature)

    order = [(snap, y, py) for snap in range(SNAP) for y in range(4) for py in range(2)]
    halves = []
    for px in range(2):
        blocks = []
        for snap, y, py in order:
            lane = 128 * (4 * y + snap)
            blocks.append(logits[(2 * py + px) * 8 : (2 * py + px) * 8 + 8, lane : lane + 128])
        halves.append(jnp.concatenate(blocks, axis=0))
    whole = jnp.concatenate(halves, axis=1)
    high = whole.astype(BF16)
    rest = whole - high.astype(F32)
    middle_term = rest.astype(BF16)
    low = (rest - middle_term.astype(F32)).astype(BF16)
    ordered = dot_nn(high, to_cols) + dot_nn(middle_term, to_cols) + dot_nn(low, to_cols)
    for row in range(32):
        logits_ref[row] = ordered[8 * row : 8 * row + 8]

    fine_cells = 1048576.0
    total = jnp.zeros((NCLS, 64), F32)
    for spot in range(4):
        for part in (0, 32):
            block = grad_fine[part + 8 * spot : part + 8 * spot + 8]
            total = total + block[:, 64 * spot : 64 * spot + 64]
    loss = jnp.sum(fold(lost_fine)) * (1.0 / fine_cells) + jnp.sum(coarse_ref[8:16, :])
    sums_ref[0:8, :] = coarse_ref[0:8, :]
    sums_ref[8:16, :] = jnp.concatenate(
        [total * (1.0 / fine_cells), jnp.broadcast_to(loss, (NCLS, 64))], axis=1
    )


def first(a, mid, b, w1):
    return call(
        first_kernel, "first", [((18, M, 256), BF16)],
        [((3, SNAP, 24, 384), F32), ((3, M, 144), BF16)],
        2_000_000_000, 14, a, mid, b, w1,
    )[0]


def second(h1, w2):
    return call(
        second_kernel, "second", [((12, M, 256), BF16), ((8, M, 256), BF16)],
        [((M + 16, 256), F32), ((M + 16, 128), F32)],
        2_500_000_000, 18, h1, w2,
    )


def middle(ph, w3, hc, labels):
    return call(
        middle_kernel, "middle", [((6, M, 384), BF16), ((16, 128), F32)],
        [((M + 16, 128), F32)], 1_000_000_000, 12, ph, w3, hc, labels,
    )


def decoded(h2, mh, w4, hf, labels, coarse):
    return call(
        decoded_kernel, "decoded", [((32, NCLS, COLS), F32), ((16, 128), F32)],
        [((4, M, 256), BF16), ((32, 256), F32)],
        2_500_000_000, 16, h2, mh, w4, hf, labels, coarse,
    )


def mesh_pairs(change):
    pairs = []
    for device in range(128):
        grp, gx = device // 16, device % 16
        at = {"x": (gx // 2 % 2) * 2 + grp // 4, "y": grp % 4, "z": gx // 4, "core": gx % 2}
        change(at)
        grp = (at["x"] % 2) * 4 + at["y"]
        gx = (at["z"] * 2 + at["x"] // 2) * 2 + at["core"]
        pairs.append((device, grp * 16 + gx))
    return pairs


def flip(x, name, bits):
    def change(at):
        at[name] ^= bits

    return lax.ppermute(x, AXES, mesh_pairs(change))


def finish_kernel(a, b, c, d, loss, fine, coarse):
    total = (a[...] + b[...]) + (c[...] + d[...])
    coarse[...] = total[0:8]
    fine[...] = total[8:16, 0:64]
    loss[...] = total[8:9, 64:65]


tie = lax.optimization_barrier


def body(
    velocity, snapshot_index, labels_fine, labels_coarse,
    conv_first, conv_second, conv_middle, conv_joined, head_fine, head_coarse,
):
    keep, give = pack(velocity, snapshot_index)
    line_a, line_b = outer_lines(velocity)
    weights = block_weights(conv_first, conv_second, conv_middle, conv_joined, head_fine, head_coarse)
    got = exchange_a(give, "gx")
    block = ((2, 208, 128), BF16)
    own, one, two, three = call(merge_kernel, "merge", [block] * 4, [], 1, 8, keep, got)
    own, line_a, line_b = tie((own, line_a, line_b))
    two, one, three = flip(two, "z", 2), flip(one, "z", 1), flip(three, "z", 3)
    line_a, line_b = exchange_a(line_a, "grp"), exchange_b(line_b, "grp")
    own, weights = tie((own, weights))
    own = (own + two) + (one + three)
    pick = functools.partial(lax.dynamic_index_in_dim, keepdims=False)
    half = (lax.axis_index("gx") // 2) % 2
    mine, theirs = pick(own, half, 0), pick(own, 1 - half, 0)
    got = lax.ppermute(theirs, "gx", [(i, i ^ 2) for i in range(16)])
    mine, line_a, line_b = tie((mine, line_a, line_b))
    plane_a, plane_b = outer_planes(velocity, line_a, line_b)
    tile = mine + got
    tile, plane_a, plane_b = tie((tile, plane_a, plane_b))
    tile_a, tile_b = exchange_a(tile, "grp"), exchange_b(tile, "grp")
    plane_b, plane_a = exchange_b(plane_b, "gx"), exchange_a(plane_a, "gx")
    w1, w2, w3, w4, hf, hc = weights
    h2, ph = second(first(tile_a, tile, tile_b, w1), w2)
    mh, coarse = middle(ph, w3, hc, labels_coarse.reshape(SNAP * 4, 128))
    logits, sums = decoded(h2, mh, w4, hf, labels_fine.reshape(SNAP * ROWS, COLS), coarse)

    sums, plane_a, plane_b = tie((sums, plane_a, plane_b))
    sums = sums + flip(sums, "core", 1)
    sums, plane_a, plane_b = tie((sums, plane_a, plane_b))
    got = flip(sums, "z", 1)
    new = step_one(velocity, plane_a, plane_b, line_a, line_b)
    sums, new = tie((sums + got, new))
    got = flip(sums, "z", 3)
    field = step_two(new)
    sums, field = tie((sums + got, field))
    sums = (sums + flip(sums, "y", 1)) + (flip(sums, "y", 2) + flip(sums, "y", 3))
    loss, grad_fine, grad_coarse = call(
        finish_kernel, "finish", [((1, 1), F32), ((8, 64), F32), ((8, 128), F32)], [], 1, 4,
        sums, flip(sums, "x", 1), flip(sums, "x", 2), flip(sums, "x", 3),
    )
    return (
        field,
        logits.reshape(SNAP, ROWS, NCLS, COLS),
        loss.reshape(()),
        grad_fine,
        grad_coarse,
    )


def solution(mesh):
    return jax.shard_map(
        body,
        mesh=mesh,
        in_specs=(
            P(None, "gx", "grp", None),
            P(),
            P(None, "grp", "gx"),
            P(None, "grp", "gx"),
            P(),
            P(),
            P(),
            P(),
            P(),
            P(),
        ),
        out_specs=(P(None, "gx", "grp", None), P(None, "grp", None, "gx"), P(), P(), P()),
        check_vma=False,
    )
```

```python
import functools

import jax
import jax.numpy as jnp
import numpy as np
from jax import lax
from jax.experimental import pallas as pl
from jax.experimental.pallas import tpu as pltpu
from jax.sharding import PartitionSpec as P

F32, BF16 = jnp.float32, jnp.bfloat16
AXES = ("grp", "gx")
SNAP, NCLS = 4, 8
ROWS, COLS = 8, 256
XB = 144
M = SNAP * XB
NX = 4096
CHUNK = 1024
COLUMNS = CHUNK // 128
HALF = NX // 2
UNROLL = 2
time_step = 0.2
viscosity = 0.1
GROUP_COL = (0, 1, 2, -1)


def dot_nn(a, b):
    return lax.dot_general(a, b, (((1,), (0,)), ((), ())), preferred_element_type=F32)


def dot_nt(a, b):
    return lax.dot_general(a, b, (((1,), (1,)), ((), ())), preferred_element_type=F32)


def split_two(value):
    high = value.astype(BF16)
    return high, (value - high.astype(F32)).astype(BF16)


def call(kernel, name, outs, scratch, flops, limit, *args, scalars=0):
    vmem = pl.BlockSpec(memory_space=pltpu.VMEM)
    smem = pl.BlockSpec(memory_space=pltpu.SMEM)
    return pl.pallas_call(
        kernel,
        out_shape=tuple(jax.ShapeDtypeStruct(*out) for out in outs),
        in_specs=[smem] * scalars + [vmem] * (len(args) - scalars),
        out_specs=(vmem,) * len(outs),
        scratch_shapes=[pltpu.VMEM(*one) for one in scratch],
        compiler_params=pltpu.CompilerParams(vmem_limit_bytes=limit * 1024 * 1024),
        cost_estimate=pl.CostEstimate(flops=flops, bytes_accessed=1_000_000, transcendentals=0),
        name=name,
    )(*args)


def exchange_a(x, axis):
    return lax.ppermute(x, axis, [(i, i ^ 1) for i in range(lax.axis_size(axis))])


def exchange_b(x, axis):
    count = lax.axis_size(axis)
    return lax.ppermute(x, axis, [(i, (((i + 1) ^ 1) - 1) % count) for i in range(count)])


def is_even(axis):
    return lax.rem(lax.axis_index(axis), 2) == 0


def pack_kernel(index_hbm, vel_hbm, keep_ref, give_ref, planes, vel_ref, index_ref, sems):
    fetch = pltpu.make_async_copy(index_hbm, index_ref, sems.at[0])
    fetch.start()
    copies = [pltpu.make_async_copy(vel_hbm.at[c], vel_ref.at[c], sems.at[1 + c]) for c in range(3)]
    for copy in copies:
        copy.start()
    planes[...] = jnp.zeros((96, NX), F32)
    place = lax.axis_index("gx")
    fetch.wait()
    for copy in copies:
        copy.wait()
    for snap in range(SNAP):
        local = index_ref[snap] - place * 4
        spot = jnp.clip(local, 0, 3)

        @pl.when(jnp.logical_and(local >= 0, local < 4))
        def _():
            for comp in range(3):
                planes[pl.ds((snap * 3 + comp) * ROWS, ROWS), :] = vel_ref[comp, spot]

    lane = lax.broadcasted_iota(jnp.int32, (16, 128), 1)
    core = lax.rem(place, 2)

    def targets(n, carry):
        for other, out_ref in ((0, keep_ref), (1, give_ref)):
            j = 2 * n + (core + other * (1 - 2 * core))
            depth, half = n // 2, lax.rem(n, 2)
            base = pl.multiple_of(j * COLS, COLS)
            out_ref[depth, half, 0:96, :] = planes[:, pl.ds(base, 128)].astype(BF16)
            out_ref[depth, half, 96:192, :] = planes[:, pl.ds(base + 128, 128)].astype(BF16)
            after = pl.multiple_of(lax.rem(base + COLS, NX), 128)
            before = pl.multiple_of(lax.rem(base + NX - 128, NX), 128)
            packed = jnp.zeros((16, 128), F32)
            for pair in range(6):
                edge = jnp.where(
                    lane < 64,
                    planes[pl.ds(16 * pair, 16), pl.ds(after, 128)],
                    planes[pl.ds(16 * pair, 16), pl.ds(before, 128)],
                )
                edge = pltpu.roll(edge, 16 * pair + 8, 1)
                packed = jnp.where((lane >> 4) == pair, edge, packed)
            out_ref[depth, half, 192:208, :] = packed.astype(BF16)
        return carry

    lax.fori_loop(0, 8, targets, 0, unroll=UNROLL)


def pack(velocity, index):
    vmem = pl.BlockSpec(memory_space=pltpu.VMEM)
    blocks = jax.ShapeDtypeStruct((4, 2, 208, 128), BF16)
    return pl.pallas_call(
        pack_kernel,
        out_shape=(blocks, blocks),
        in_specs=[pl.BlockSpec(memory_space=pltpu.HBM)] * 2,
        out_specs=(vmem, vmem),
        scratch_shapes=[
            pltpu.VMEM((96, NX), F32),
            pltpu.VMEM((3, 4, ROWS, NX), F32),
            pltpu.SMEM((SNAP,), jnp.int32),
            pltpu.SemaphoreType.DMA((4,)),
        ],
        compiler_params=pltpu.CompilerParams(vmem_limit_bytes=10 * 1024 * 1024),
        cost_estimate=pl.CostEstimate(flops=0, bytes_accessed=1_000_000, transcendentals=0),
        name="pack",
    )(
        pltpu.with_memory_space_constraint(index, pltpu.HBM),
        pltpu.with_memory_space_constraint(velocity, pltpu.HBM),
    )


def merge_kernel(keep_ref, got_ref, own, one, two, three):
    depth = lax.axis_index("gx") // 4
    high, low = depth // 2, lax.rem(depth, 2)
    for k, out_ref in enumerate((own, one, two, three)):
        flip_low = low if k % 2 == 0 else 1 - low
        flip_high = high if k // 2 == 0 else 1 - high
        at = 2 * flip_high + flip_low
        out_ref[...] = keep_ref[at] + got_ref[at]


def gather_kernel(own, two, one, three, mine, theirs):
    half = lax.rem(lax.axis_index("gx") // 2, 2)
    for out_ref, at in ((mine, half), (theirs, 1 - half)):
        out_ref[...] = (own[at] + two[at]) + (one[at] + three[at])


def sides(even, a_ref, b_ref, rows):
    a, b = a_ref[rows, :].astype(F32), b_ref[rows, :].astype(F32)
    return jnp.where(even, b, a), jnp.where(even, a, b)


def lines_kernel(vel_ref, a_ref, b_ref, rows):
    for comp in range(3):
        for slot, at in ((0, 6), (1, 0)):
            for z in range(4):
                for h in range(2):
                    rows[slot, pl.ds(24 * h + 8 * comp + 2 * z, 2), :] = vel_ref[
                        comp, z, at : at + 2, HALF * h : HALF * h + HALF
                    ]
    odd = lax.rem(lax.axis_index("grp"), 2)
    a_ref[...] = rows[odd].astype(BF16)
    b_ref[...] = rows[1 - odd].astype(BF16)


def line_of(slab, at):
    return jnp.concatenate([slab[at : at + 1], slab[24 + at : 25 + at]], axis=1)


def outer_lines(velocity):
    slab = ((48, HALF), BF16)
    return call(lines_kernel, "outer_lines", [slab, slab], [((2, 48, HALF), F32)], 0, 8, velocity)


def planes_kernel(vel_ref, ya_ref, yb_ref, a_ref, b_ref, rows):
    before, after = sides(is_even("grp"), ya_ref, yb_ref, pl.ds(0, 48))
    for slot, base, edge in ((0, 2, 3), (1, 0, 0)):
        rows[slot, 48:64, :] = jnp.zeros((16, NX), F32)
        for comp in range(3):
            for p in range(2):
                rows[slot, pl.ds((comp * 2 + p) * 8, 8), :] = vel_ref[comp, base + p]
            at = 8 * comp + 2 * edge
            rows[slot, pl.ds(48 + 2 * comp, 1), :] = line_of(before, at + 1)
            rows[slot, pl.ds(49 + 2 * comp, 1), :] = line_of(after, at)
    odd = lax.rem(lax.axis_index("gx"), 2)
    a_ref[...] = rows[odd].astype(BF16)
    b_ref[...] = rows[1 - odd].astype(BF16)


def outer_planes(velocity, ya, yb):
    slab = ((64, NX), BF16)
    return call(
        planes_kernel, "outer_planes", [slab, slab], [((2, 64, NX), F32)], 0, 10, velocity, ya, yb
    )


def stepped(columns, center, z_minus, z_plus, y_minus, y_plus, put):
    half, mix = 0.5 * time_step, viscosity
    lane = lax.broadcasted_iota(jnp.int32, (8, 128), 1)
    cells = [[center(d, j) for d in range(3)] for j in (-1, 0)]
    right = [[pltpu.roll(u, 1, 1) for u in column] for column in cells]
    left = [[pltpu.roll(u, 127, 1) for u in cells[1]]]
    for j in range(columns):
        mid, ahead = cells[1], [center(d, j + 1) for d in range(3)]
        right_ahead = [pltpu.roll(u, 1, 1) for u in ahead]
        left_ahead = [pltpu.roll(u, 127, 1) for u in ahead]
        plus = [mix - half * u for u in mid]
        minus = [mix + half * u for u in mid]
        for d in range(3):
            x_plus = jnp.where(lane == 127, left_ahead[d], left[0][d])
            x_minus = jnp.where(lane == 0, right[0][d], right[1][d])
            along_z = plus[0] * z_plus(d, j) + minus[0] * z_minus(d, j)
            along_y = plus[1] * y_plus(d, j) + minus[1] * y_minus(d, j)
            along_x = plus[2] * x_plus + minus[2] * x_minus
            put(d, j, ((1.0 - 6.0 * mix) * mid[d] + along_z) + (along_y + along_x))
        cells, right, left = [mid, ahead], [right[1], right_ahead], [left_ahead]


def wrap(buf):
    buf[..., 0:128] = buf[..., NX : NX + 128]
    buf[..., NX + 128 : NX + 256] = buf[..., 128:256]


def column(n, j):
    return pl.ds(pl.multiple_of(n * CHUNK + 128 * (j + 1), 128), 128)


def step_rows(buf, at, n, put):
    row = lax.broadcasted_iota(jnp.int32, (8, 128), 0)
    get = lambda row: lambda d, j: buf[d, pl.ds(row, 8), column(n, j)]
    center, edge = get(at), get(at + 8)
    y_minus = lambda d, j: jnp.where(row == 0, edge(d, j), pltpu.roll(center(d, j), 1, 0))
    y_plus = lambda d, j: jnp.where(row == 7, edge(d, j), pltpu.roll(center(d, j), 7, 0))
    stepped(COLUMNS, center, get(at - 16), get(at + 16), y_minus, y_plus, put)


def step_one_kernel(vel_ref, za_ref, zb_ref, ya_ref, yb_ref, new, old, line):
    body = pl.ds(128, NX)
    even = is_even("gx")
    for comp in range(3):
        for z in range(4):
            old[comp, pl.ds(16 * (z + 2), 8), body] = vel_ref[comp, z]
        low, high = sides(even, za_ref, zb_ref, pl.ds(16 * comp, 16))
        for p in range(2):
            old[comp, pl.ds(16 * p, 8), body] = low[8 * p : 8 * p + 8]
            old[comp, pl.ds(16 * (p + 6), 8), body] = high[8 * p : 8 * p + 8]
    corners = sides(even, za_ref, zb_ref, pl.ds(48, 16))
    slabs = sides(is_even("grp"), ya_ref, yb_ref, pl.ds(0, 48))
    for side, row, own, near, far in ((0, 8, 0, 1, 0), (1, 15, 7, 0, 1)):
        for comp in range(3):
            for z in range(-1, 5):
                if 0 <= z < 4:
                    at = 8 * comp + 2 * z
                    value = line_of(slabs[side], at + near)
                    line[side, comp, 0, pl.ds(2 + z, 1), body] = line_of(slabs[side], at + far)
                    line[side, comp, 2, pl.ds(2 + z, 1), body] = vel_ref[comp, z, own : own + 1, :]
                else:
                    at = 2 * comp + side
                    value = corners[0 if z < 0 else 1][at : at + 1]
                line[side, comp, 1, pl.ds(2 + z, 1), body] = value
                old[comp, pl.ds(16 * (z + 2) + row, 1), body] = value
    wrap(old)
    wrap(line)

    def chunk(n, carry):
        for z in range(-1, 5):

            def put(d, j, value):
                new[d, pl.ds(16 * (z + 1), 8), column(n, j)] = value

            step_rows(old, 16 * (z + 2), n, put)
        for side, row in ((0, 8), (1, 15)):
            get = lambda kind: lambda d, j: line[side, d, kind, :, column(n, j)]
            z_minus = lambda d, j: pltpu.roll(line[side, d, 1, :, column(n, j)], 1, 0)
            z_plus = lambda d, j: pltpu.roll(line[side, d, 1, :, column(n, j)], 7, 0)

            def put(d, j, value):
                for z in range(4):
                    new[d, pl.ds(16 * (z + 1) + row, 1), column(n, j)] = value[2 + z : 3 + z]

            outer, own = get(0), get(2)
            pair = (outer, own) if side == 0 else (own, outer)
            stepped(COLUMNS, get(1), z_minus, z_plus, *pair, put)
        return carry

    lax.fori_loop(0, NX // CHUNK, chunk, 0)
    wrap(new)


def step_two_kernel(new, out_ref, res, sems):
    def leave(n):
        lanes = pl.ds(pl.multiple_of(n * CHUNK, 128), CHUNK)
        return pltpu.make_async_copy(res.at[:, :, :, lanes], out_ref.at[:, :, :, lanes], sems.at[n])

    def chunk(n, carry):
        for z in range(4):

            def put(d, j, value):
                res[d, z, :, pl.ds(pl.multiple_of(n * CHUNK + 128 * j, 128), 128)] = value

            step_rows(new, 16 * (z + 1), n, put)
        leave(n).start()
        return carry

    lax.fori_loop(0, NX // CHUNK, chunk, 0)
    for n in range(NX // CHUNK):
        leave(n).wait()


def step_one(velocity, za, zb, ya, yb):
    return call(
        step_one_kernel, "step_one", [((3, 16 * 6, NX + 256), F32)],
        [((3, 16 * 8, NX + 256), F32), ((2, 3, 3, 8, NX + 256), F32)],
        20_000_000, 24, velocity, za, zb, ya, yb,
    )[0]


def step_two(new):
    return pl.pallas_call(
        step_two_kernel,
        out_shape=jax.ShapeDtypeStruct((3, 4, ROWS, NX), F32),
        in_specs=[pl.BlockSpec(memory_space=pltpu.VMEM)],
        out_specs=pl.BlockSpec(memory_space=pltpu.HBM),
        scratch_shapes=[
            pltpu.VMEM((3, 4, ROWS, NX), F32),
            pltpu.SemaphoreType.DMA((NX // CHUNK,)),
        ],
        compiler_params=pltpu.CompilerParams(vmem_limit_bytes=12 * 1024 * 1024),
        cost_estimate=pl.CostEstimate(flops=10_000_000, bytes_accessed=1_000_000, transcendentals=0),
        name="step_two",
    )(new)


def first_layer_places():
    places = np.zeros((6, 4, 144, 32), np.float32)
    for r in range(6):
        for group, col in enumerate(GROUP_COL):
            for a in range(3):
                for b in range(3):
                    for c in range(3):
                        j = b + 1 + col
                        places[r, group, j * 24 + c * 8 + r + a, a * 9 + b * 3 + c] = 1.0
    return places


def weights_kernel(
    places_ref, first_ref, second_ref, middle_ref, joined_ref, fine_ref, coarse_ref,
    w1_ref, w2_ref, w3_ref, w4_ref, hf_ref, hc_ref, flat,
):
    flat[...] = jnp.zeros((32, 64), F32)
    for tap in range(9):
        flat[pl.ds(3 * tap, 3), :] = first_ref[tap // 3, tap % 3].astype(F32)
    first_taps = flat[...].astype(BF16)
    for r in range(6):
        parts = [dot_nn(places_ref[r, g], first_taps) for g in range(4)]
        w1_ref[r] = jnp.concatenate(parts, axis=1).astype(BF16)

    none = jnp.zeros((64, 64), F32)

    def spread(taps, out_ref):
        for k in range(4):
            for group, col in enumerate(GROUP_COL):
                blocks = []
                for py in range(2):
                    for px in range(2):
                        a, b = k - py, col - px + 1
                        inside = 0 <= a <= 2 and 0 <= b <= 2
                        blocks.append(taps[a][b] if inside else none)
                block = jnp.concatenate(blocks, axis=1).astype(BF16)
                out_ref[pl.ds(k * 256 + group * 64, 64), :] = block

    spread([[second_ref[a, b].astype(F32).T for b in range(3)] for a in range(3)], w2_ref)

    wide_none = jnp.zeros((64, 128), F32)
    taps = [[middle_ref[a, b].astype(F32) for b in range(3)] for a in range(3)]
    for k in range(4):
        for place, b in enumerate((0, 2, 1, None)):
            blocks = []
            for e in range(2):
                inside = b is not None and 0 <= k - e <= 2
                blocks.append(taps[k - e][b] if inside else wide_none)
            block = jnp.concatenate(blocks, axis=1).astype(BF16)
            w3_ref[pl.ds(k * 256 + place * 64, 64), :] = block

    joined = [[joined_ref[a, b].astype(F32).T for b in range(3)] for a in range(3)]
    spread([[joined[a][b][128:192] for b in range(3)] for a in range(3)], w4_ref)
    for dy in range(3):
        for dx in range(3):
            blocks = []
            for py in range(2):
                for px in range(2):
                    total = jnp.zeros((128, 64), F32)
                    for a in range(3):
                        for b in range(3):
                            if (py + a - 1) // 2 + 1 == dy and (px + b - 1) // 2 + 1 == dx:
                                total = total + joined[a][b][0:128]
                    blocks.append(total)
            block = jnp.concatenate(blocks, axis=1).astype(BF16)
            w4_ref[pl.ds(1024 + (dy * 3 + dx) * 128, 128), :] = block

    head = fine_ref[...]
    high = head.astype(BF16).astype(F32)
    empty = jnp.zeros((NCLS, 64), F32)
    rows = []
    for part in (high, head - high):
        for spot in range(4):
            rows.append(jnp.concatenate([part if i == spot else empty for i in range(4)], axis=1))
    hf_ref[...] = jnp.concatenate(rows, axis=0).astype(BF16)
    head = coarse_ref[...]
    high = head.astype(BF16).astype(F32)
    hc_ref[...] = jnp.concatenate([high, head - high], axis=0).astype(BF16)


def block_weights(conv_first, conv_second, conv_middle, conv_joined, head_fine, head_coarse):
    swapped = (0, 1, 3, 2)
    return call(
        weights_kernel, "block_weights",
        [
            ((6, 144, 256), BF16), ((1024, 256), BF16), ((1024, 256), BF16),
            ((1024 + 1152, 256), BF16), ((64, 256), BF16), ((16, 128), BF16),
        ],
        [((32, 64), F32)], 0, 12,
        jnp.asarray(first_layer_places(), BF16), jnp.transpose(conv_first, swapped), conv_second,
        jnp.transpose(conv_middle, swapped), conv_joined, head_fine, head_coarse,
    )


def keep_padded(buf, value):
    buf[8 : 8 + M, :] = value
    buf[7:8, :] = value[M - 1 : M]
    buf[8 + M : 9 + M, :] = value[0:1]


def first_kernel(a_ref, mid_ref, b_ref, w1_ref, h1, win, taps):
    row384 = lax.broadcasted_iota(jnp.int32, (8, 384), 0)
    up, down = sides(is_even("grp"), a_ref, b_ref, pl.ds(0, 208))
    tiles = [up, mid_ref[...].astype(F32), down]
    for q in range(12):
        pieces = []
        for tile in tiles:
            edge = tile[192 + 8 * (q % 2) : 200 + 8 * (q % 2)]
            edge = pltpu.roll(edge, 128 - (16 * (q // 2) + 8), 1)
            pieces.append(
                jnp.concatenate([tile[8 * q : 8 * q + 8], tile[96 + 8 * q : 104 + 8 * q], edge], axis=1)
            )
        top, center, bottom = pieces
        snap, comp = q // 3, q % 3
        rows = pl.ds(comp * 8, 8)
        win[0, snap, rows, :] = jnp.where(row384 < 6, pltpu.roll(top, 6, 0), pltpu.roll(center, 6, 0))
        win[1, snap, rows, :] = center
        win[2, snap, rows, :] = jnp.where(row384 < 2, pltpu.roll(center, 2, 0), pltpu.roll(bottom, 2, 0))

    spot = lax.broadcasted_iota(jnp.int32, (XB, 384), 0)
    wanted = jnp.where(spot >= 142, 2 * spot + 94, 2 * spot - 2)
    wanted = jnp.where(wanted < 0, wanted + 384, wanted)
    even = (lax.broadcasted_iota(jnp.int32, (XB, 384), 1) == wanted).astype(F32).astype(BF16)
    own = lax.broadcasted_iota(jnp.int32, (XB, 144), 0) < 142
    for group in range(3):
        found = []
        for snap in range(SNAP):
            window = win[group, snap]
            shifted = [window] + [pltpu.roll(window, 384 - j, 1) for j in range(1, 6)]
            stack = jnp.concatenate(shifted, axis=0).astype(BF16)
            found.append(dot_nt(even, stack))
        for snap in range(SNAP):
            rows = jnp.where(own, found[snap], found[(snap + 1) % SNAP])
            taps[group, pl.ds(snap * XB, XB), :] = rows.astype(BF16)

    for i in range(18):
        out = dot_nn(taps[i // 6], w1_ref[i % 6])
        h1[i] = jnp.maximum(out, 0.0).astype(BF16)


def second_kernel(h1, w2_ref, h2, ph, sbuf, pbuf):
    side = lax.broadcasted_iota(jnp.int32, (M, 128), 1) < 64

    def pool(q, out):
        pooled = jnp.maximum(out[:, 0:128], out[:, 128:256])
        pooled = jnp.maximum(pooled, pltpu.roll(pooled, 64, 1))
        keep_padded(pbuf, pooled)
        ph[q, :, 0:128] = jnp.where(side, pbuf[7 : 7 + M, :], pbuf[9 : 9 + M, :]).astype(BF16)
        ph[q, :, 128:256] = pooled.astype(BF16)

    def row(q):
        lhs = jnp.concatenate([h1[2 * q + k] for k in range(4)], axis=1)
        return jnp.maximum(dot_nn(lhs, w2_ref[...]), 0.0)

    for q in range(8):
        out = row(q)
        if 0 < q < 7:
            keep_padded(sbuf, out)
            for py in range(2):
                lanes = pl.ds(128 * py, 128)
                h2[2 * q - 2 + py, :, 0:128] = out[:, 128 * py : 128 * py + 128].astype(BF16)
                beside = jnp.where(side, sbuf[9 : 9 + M, lanes], sbuf[7 : 7 + M, lanes])
                h2[2 * q - 2 + py, :, 128:256] = beside.astype(BF16)
        pool(q, out)


def class_terms(logits, label):
    classes = lax.broadcasted_iota(jnp.int32, logits.shape, 0).astype(F32)
    peak = jnp.max(logits, axis=0, keepdims=True)
    powers = jnp.exp(logits - peak)
    total = jnp.sum(powers, axis=0, keepdims=True)
    onehot = (classes == label).astype(F32)
    lost = onehot * (peak + jnp.log(total) - logits)
    return lost, powers / total - onehot


def cells(kept, lanes):
    return jnp.concatenate(
        [kept[y, pl.ds(snap * XB, 128), lanes] for y in kept_rows(kept) for snap in range(SNAP)], axis=0
    )


def kept_rows(kept):
    return range(1, 5) if kept.shape[0] == 6 else range(4)


def fold(lost):
    total = lost[:, 0:128]
    for block in range(1, 16):
        total = total + lost[:, 128 * block : 128 * block + 128]
    return total


def middle_kernel(ph, w3_ref, hc_ref, labc_ref, mh, sums_ref, mbuf):
    def middle_rows(t, carry):
        lhs = jnp.concatenate([ph[2 * t + k] for k in range(4)], axis=1)
        out = jnp.maximum(dot_nn(lhs, w3_ref[...]), 0.0)
        for e in range(2):
            value = out[:, 128 * e : 128 * e + 128]
            keep_padded(mbuf, value)
            row = 2 * t + e
            mh[row, :, 0:128] = mbuf[7 : 7 + M, :].astype(BF16)
            mh[row, :, 128:256] = value.astype(BF16)
            mh[row, :, 256:384] = mbuf[9 : 9 + M, :].astype(BF16)
        return carry

    lax.fori_loop(0, 3, middle_rows, 0)

    feature = cells(mh, pl.ds(128, 128))
    both = dot_nt(hc_ref[...], feature)
    label = jnp.concatenate(
        [labc_ref[pl.ds(snap * 4 + y, 1), :] for y in range(4) for snap in range(SNAP)], axis=1
    ).astype(F32)
    lost, grad = class_terms(both[0:8] + both[8:16], label)
    high = grad.astype(BF16).astype(F32)
    slopes = jnp.concatenate([high, grad - high], axis=0).astype(BF16)
    total = dot_nn(slopes, feature)
    coarse_cells = 262144.0
    sums_ref[0:8, :] = (total[0:8] + total[8:16]) * (1.0 / coarse_cells)
    sums_ref[8:16, :] = fold(lost) * (1.0 / coarse_cells)


def decoded_kernel(
    h2, mh, w4_ref, hf_ref, labf_ref, coarse_ref, planar_ref, sums_ref, dec, labs
):
    for y in range(4):
        lhs = jnp.concatenate(
            [h2[2 * y + 1 + k] for k in range(4)] + [mh[y + k] for k in range(3)], axis=1
        )
        dec[y] = jnp.maximum(dot_nn(lhs, w4_ref[...]), 0.0).astype(BF16)

    col = lax.broadcasted_iota(jnp.int32, (256, 256), 0)
    planar_col = lax.broadcasted_iota(jnp.int32, (256, 256), 1)
    to_planar = (col == 2 * (planar_col & 127) + (planar_col >> 7)).astype(F32).astype(BF16)
    labs[...] = dot_nn(labf_ref[...].astype(F32).astype(BF16), to_planar)

    feature = cells(dec, pl.ds(0, 256))
    both = dot_nt(hf_ref[...], feature)
    logits = both[0:32] + both[32:64]
    planar_ref[...] = logits
    lost_fine = jnp.zeros((NCLS, 2048), F32)
    slopes = []
    for py in range(2):
        for px in range(2):
            lanes = pl.ds(128 * px, 128)
            label = jnp.concatenate(
                [labs[pl.ds(snap * 8 + 2 * y + py, 1), lanes] for y in range(4) for snap in range(SNAP)],
                axis=1,
            )
            at = (2 * py + px) * 8
            lost, grad = class_terms(logits[at : at + 8], label)
            lost_fine = lost_fine + lost
            slopes.append(grad)
    high, low = split_two(jnp.concatenate(slopes, axis=0))
    grad_fine = dot_nn(jnp.concatenate([high, low], axis=0), feature)

    fine_cells = 1048576.0
    total = jnp.zeros((NCLS, 64), F32)
    for spot in range(4):
        for part in (0, 32):
            block = grad_fine[part + 8 * spot : part + 8 * spot + 8]
            total = total + block[:, 64 * spot : 64 * spot + 64]
    loss = jnp.sum(fold(lost_fine)) * (1.0 / fine_cells) + jnp.sum(coarse_ref[8:16, :])
    sums_ref[0:8, :] = coarse_ref[0:8, :]
    sums_ref[8:16, :] = jnp.concatenate(
        [total * (1.0 / fine_cells), jnp.broadcast_to(loss, (NCLS, 64))], axis=1
    )


def ordered_kernel(planar_ref, logits_ref):
    col = lax.broadcasted_iota(jnp.int32, (256, 256), 0)
    planar_col = lax.broadcasted_iota(jnp.int32, (256, 256), 1)
    to_cols = (planar_col == 2 * (col & 127) + (col >> 7)).astype(F32).astype(BF16)
    logits = planar_ref[...]
    order = [(snap, y, py) for snap in range(SNAP) for y in range(4) for py in range(2)]
    halves = []
    for px in range(2):
        blocks = []
        for snap, y, py in order:
            lane = 128 * (4 * y + snap)
            blocks.append(logits[(2 * py + px) * 8 : (2 * py + px) * 8 + 8, lane : lane + 128])
        halves.append(jnp.concatenate(blocks, axis=0))
    whole = jnp.concatenate(halves, axis=1)
    high = whole.astype(BF16)
    rest = whole - high.astype(F32)
    middle_term = rest.astype(BF16)
    low = (rest - middle_term.astype(F32)).astype(BF16)
    ordered = dot_nn(high, to_cols) + dot_nn(middle_term, to_cols) + dot_nn(low, to_cols)
    for row in range(32):
        logits_ref[row] = ordered[8 * row : 8 * row + 8]


def first(a, mid, b, w1):
    return call(
        first_kernel, "first", [((18, M, 256), BF16)],
        [((3, SNAP, 24, 384), F32), ((3, M, 144), BF16)],
        2_000_000_000, 14, a, mid, b, w1,
    )[0]


def second(h1, w2):
    return call(
        second_kernel, "second", [((12, M, 256), BF16), ((8, M, 256), BF16)],
        [((M + 16, 256), F32), ((M + 16, 128), F32)],
        2_500_000_000, 18, h1, w2,
    )


def middle(ph, w3, hc, labels):
    return call(
        middle_kernel, "middle", [((6, M, 384), BF16), ((16, 128), F32)],
        [((M + 16, 128), F32)], 1_000_000_000, 12, ph, w3, hc, labels,
    )


def decoded(h2, mh, w4, hf, labels, coarse):
    return call(
        decoded_kernel, "decoded", [((32, 2048), F32), ((16, 128), F32)],
        [((4, M, 256), BF16), ((32, 256), F32)],
        2_500_000_000, 16, h2, mh, w4, hf, labels, coarse,
    )


def ordered(planar):
    return call(
        ordered_kernel, "ordered", [((32, NCLS, COLS), F32)], [], 300_000_000, 6, planar
    )[0]


def mesh_pairs(change):
    pairs = []
    for device in range(128):
        grp, gx = device // 16, device % 16
        at = {"x": (gx // 2 % 2) * 2 + grp // 4, "y": grp % 4, "z": gx // 4, "core": gx % 2}
        change(at)
        grp = (at["x"] % 2) * 4 + at["y"]
        gx = (at["z"] * 2 + at["x"] // 2) * 2 + at["core"]
        pairs.append((device, grp * 16 + gx))
    return pairs


def flip(x, name, bits):
    def change(at):
        at[name] ^= bits

    return lax.ppermute(x, AXES, mesh_pairs(change))


def finish_kernel(a, b, c, d, loss, fine, coarse):
    total = (a[...] + b[...]) + (c[...] + d[...])
    coarse[...] = total[0:8]
    fine[...] = total[8:16, 0:64]
    loss[...] = total[8:9, 64:65]


tie = lax.optimization_barrier


def near(x):
    return pltpu.with_memory_space_constraint(x, pltpu.VMEM)


def body(
    velocity, snapshot_index, labels_fine, labels_coarse,
    conv_first, conv_second, conv_middle, conv_joined, head_fine, head_coarse,
):
    keep, give = pack(velocity, snapshot_index)
    line_a, line_b = outer_lines(velocity)
    weights = block_weights(conv_first, conv_second, conv_middle, conv_joined, head_fine, head_coarse)
    got = exchange_a(give, "gx")
    block = ((2, 208, 128), BF16)
    own, one, two, three = call(merge_kernel, "merge", [block] * 4, [], 1, 8, near(keep), near(got))
    own, line_a, line_b = tie((own, line_a, line_b))
    two, one, three = flip(two, "z", 2), flip(one, "z", 1), flip(three, "z", 3)
    line_a, line_b = exchange_a(line_a, "grp"), exchange_b(line_b, "grp")
    own, weights = tie((own, weights))
    block = ((208, 128), BF16)
    mine, theirs = call(
        gather_kernel, "gather", [block] * 2, [], 3_000_000_000, 8, near(own), near(two), near(one), near(three)
    )
    got = lax.ppermute(theirs, "gx", [(i, i ^ 2) for i in range(16)])
    mine, line_a, line_b = tie((mine, line_a, line_b))
    plane_a, plane_b = outer_planes(velocity, line_a, line_b)
    tile = mine + got
    tile, plane_a, plane_b = tie((tile, plane_a, plane_b))
    tile_a, tile_b = exchange_a(tile, "grp"), exchange_b(tile, "grp")
    plane_b, plane_a = exchange_b(plane_b, "gx"), exchange_a(plane_a, "gx")
    w1, w2, w3, w4, hf, hc = weights
    h2, ph = second(first(tile_a, tile, tile_b, w1), w2)
    mh, coarse = middle(ph, w3, hc, labels_coarse.reshape(SNAP * 4, 128))
    planar, sums = decoded(h2, mh, w4, hf, labels_fine.reshape(SNAP * ROWS, COLS), coarse)

    got = flip(sums, "core", 1)
    logits = ordered(planar)
    sums, logits, plane_a, plane_b = tie((sums + got, logits, plane_a, plane_b))
    got = flip(sums, "z", 1)
    new = step_one(velocity, plane_a, plane_b, line_a, line_b)
    sums, new = tie((sums + got, new))
    got = flip(sums, "z", 3)
    field = step_two(new)
    sums, field = tie((sums + got, field))
    sums = (sums + flip(sums, "y", 1)) + (flip(sums, "y", 2) + flip(sums, "y", 3))
    loss, grad_fine, grad_coarse = call(
        finish_kernel, "finish", [((1, 1), F32), ((8, 64), F32), ((8, 128), F32)], [], 1, 4,
        sums, flip(sums, "x", 1), flip(sums, "x", 2), flip(sums, "x", 3),
    )
    return (
        field,
        logits.reshape(SNAP, ROWS, NCLS, COLS),
        loss.reshape(()),
        grad_fine,
        grad_coarse,
    )


def solution(mesh):
    return jax.shard_map(
        body,
        mesh=mesh,
        in_specs=(
            P(None, "gx", "grp", None),
            P(),
            P(None, "grp", "gx"),
            P(None, "grp", "gx"),
            P(),
            P(),
            P(),
            P(),
            P(),
            P(),
        ),
        out_specs=(P(None, "gx", "grp", None), P(None, "grp", None, "gx"), P(), P(), P()),
        check_vma=False,
    )
```

```python
import functools

import jax
import jax.numpy as jnp
import numpy as np
from jax import lax
from jax.experimental import pallas as pl
from jax.experimental.pallas import tpu as pltpu
from jax.sharding import PartitionSpec as P

F32, BF16 = jnp.float32, jnp.bfloat16
AXES = ("grp", "gx")
SNAP, NCLS = 4, 8
ROWS, COLS = 8, 256
XB = 144
M = SNAP * XB
NX = 4096
CHUNK = 1024
COLUMNS = CHUNK // 128
HALF = NX // 2
UNROLL = 2
time_step = 0.2
viscosity = 0.1
GROUP_COL = (0, 1, 2, -1)


def dot_nn(a, b):
    return lax.dot_general(a, b, (((1,), (0,)), ((), ())), preferred_element_type=F32)


def dot_nt(a, b):
    return lax.dot_general(a, b, (((1,), (1,)), ((), ())), preferred_element_type=F32)


def split_two(value):
    high = value.astype(BF16)
    return high, (value - high.astype(F32)).astype(BF16)


def call(kernel, name, outs, scratch, flops, limit, *args, scalars=0):
    vmem = pl.BlockSpec(memory_space=pltpu.VMEM)
    smem = pl.BlockSpec(memory_space=pltpu.SMEM)
    return pl.pallas_call(
        kernel,
        out_shape=tuple(jax.ShapeDtypeStruct(*out) for out in outs),
        in_specs=[smem] * scalars + [vmem] * (len(args) - scalars),
        out_specs=(vmem,) * len(outs),
        scratch_shapes=[pltpu.VMEM(*one) for one in scratch],
        compiler_params=pltpu.CompilerParams(vmem_limit_bytes=limit * 1024 * 1024),
        cost_estimate=pl.CostEstimate(flops=flops, bytes_accessed=1_000_000, transcendentals=0),
        name=name,
    )(*args)


def exchange_a(x, axis):
    return lax.ppermute(x, axis, [(i, i ^ 1) for i in range(lax.axis_size(axis))])


def exchange_b(x, axis):
    count = lax.axis_size(axis)
    return lax.ppermute(x, axis, [(i, (((i + 1) ^ 1) - 1) % count) for i in range(count)])


def is_even(axis):
    return lax.rem(lax.axis_index(axis), 2) == 0


def pack_kernel(index_hbm, vel_hbm, keep_ref, give_ref, planes, vel_ref, index_ref, sems):
    fetch = pltpu.make_async_copy(index_hbm, index_ref, sems.at[0])
    fetch.start()
    copies = [pltpu.make_async_copy(vel_hbm.at[c], vel_ref.at[c], sems.at[1 + c]) for c in range(3)]
    for copy in copies:
        copy.start()
    planes[...] = jnp.zeros((96, NX), F32)
    place = lax.axis_index("gx")
    fetch.wait()
    for copy in copies:
        copy.wait()
    for snap in range(SNAP):
        local = index_ref[snap] - place * 4
        spot = jnp.clip(local, 0, 3)

        @pl.when(jnp.logical_and(local >= 0, local < 4))
        def _():
            for comp in range(3):
                planes[pl.ds((snap * 3 + comp) * ROWS, ROWS), :] = vel_ref[comp, spot]

    lane = lax.broadcasted_iota(jnp.int32, (16, 128), 1)
    core = lax.rem(place, 2)

    def targets(n, carry):
        for other, out_ref in ((0, keep_ref), (1, give_ref)):
            j = 2 * n + (core + other * (1 - 2 * core))
            depth, half = n // 2, lax.rem(n, 2)
            base = pl.multiple_of(j * COLS, COLS)
            out_ref[depth, half, 0:96, :] = planes[:, pl.ds(base, 128)].astype(BF16)
            out_ref[depth, half, 96:192, :] = planes[:, pl.ds(base + 128, 128)].astype(BF16)
            after = pl.multiple_of(lax.rem(base + COLS, NX), 128)
            before = pl.multiple_of(lax.rem(base + NX - 128, NX), 128)
            packed = jnp.zeros((16, 128), F32)
            for pair in range(6):
                edge = jnp.where(
                    lane < 64,
                    planes[pl.ds(16 * pair, 16), pl.ds(after, 128)],
                    planes[pl.ds(16 * pair, 16), pl.ds(before, 128)],
                )
                edge = pltpu.roll(edge, 16 * pair + 8, 1)
                packed = jnp.where((lane >> 4) == pair, edge, packed)
            out_ref[depth, half, 192:208, :] = packed.astype(BF16)
        return carry

    lax.fori_loop(0, 8, targets, 0, unroll=UNROLL)


def pack(velocity, index):
    vmem = pl.BlockSpec(memory_space=pltpu.VMEM)
    blocks = jax.ShapeDtypeStruct((4, 2, 208, 128), BF16)
    return pl.pallas_call(
        pack_kernel,
        out_shape=(blocks, blocks),
        in_specs=[pl.BlockSpec(memory_space=pltpu.HBM)] * 2,
        out_specs=(vmem, vmem),
        scratch_shapes=[
            pltpu.VMEM((96, NX), F32),
            pltpu.VMEM((3, 4, ROWS, NX), F32),
            pltpu.SMEM((SNAP,), jnp.int32),
            pltpu.SemaphoreType.DMA((4,)),
        ],
        compiler_params=pltpu.CompilerParams(vmem_limit_bytes=10 * 1024 * 1024),
        cost_estimate=pl.CostEstimate(flops=0, bytes_accessed=1_000_000, transcendentals=0),
        name="pack",
    )(
        pltpu.with_memory_space_constraint(index, pltpu.HBM),
        pltpu.with_memory_space_constraint(velocity, pltpu.HBM),
    )


def merge_kernel(keep_ref, got_ref, own, one, two, three):
    depth = lax.axis_index("gx") // 4
    high, low = depth // 2, lax.rem(depth, 2)
    for k, out_ref in enumerate((own, one, two, three)):
        flip_low = low if k % 2 == 0 else 1 - low
        flip_high = high if k // 2 == 0 else 1 - high
        at = 2 * flip_high + flip_low
        out_ref[...] = keep_ref[at] + got_ref[at]


def gather_kernel(own, two, one, three, mine, theirs):
    half = lax.rem(lax.axis_index("gx") // 2, 2)
    for out_ref, at in ((mine, half), (theirs, 1 - half)):
        out_ref[...] = (own[at] + two[at]) + (one[at] + three[at])


def sides(even, a_ref, b_ref, rows):
    a, b = a_ref[rows, :].astype(F32), b_ref[rows, :].astype(F32)
    return jnp.where(even, b, a), jnp.where(even, a, b)


def lines_kernel(vel_ref, a_ref, b_ref, rows):
    for comp in range(3):
        for slot, at in ((0, 6), (1, 0)):
            for z in range(4):
                for h in range(2):
                    rows[slot, pl.ds(24 * h + 8 * comp + 2 * z, 2), :] = vel_ref[
                        comp, z, at : at + 2, HALF * h : HALF * h + HALF
                    ]
    odd = lax.rem(lax.axis_index("grp"), 2)
    a_ref[...] = rows[odd].astype(BF16)
    b_ref[...] = rows[1 - odd].astype(BF16)


def line_of(slab, at):
    return jnp.concatenate([slab[at : at + 1], slab[24 + at : 25 + at]], axis=1)


def outer_lines(velocity):
    slab = ((48, HALF), BF16)
    return call(lines_kernel, "outer_lines", [slab, slab], [((2, 48, HALF), F32)], 0, 8, velocity)


def planes_kernel(vel_ref, ya_ref, yb_ref, a_ref, b_ref, rows):
    before, after = sides(is_even("grp"), ya_ref, yb_ref, pl.ds(0, 48))
    for slot, base, edge in ((0, 2, 3), (1, 0, 0)):
        rows[slot, 48:64, :] = jnp.zeros((16, NX), F32)
        for comp in range(3):
            for p in range(2):
                rows[slot, pl.ds((comp * 2 + p) * 8, 8), :] = vel_ref[comp, base + p]
            at = 8 * comp + 2 * edge
            rows[slot, pl.ds(48 + 2 * comp, 1), :] = line_of(before, at + 1)
            rows[slot, pl.ds(49 + 2 * comp, 1), :] = line_of(after, at)
    odd = lax.rem(lax.axis_index("gx"), 2)
    a_ref[...] = rows[odd].astype(BF16)
    b_ref[...] = rows[1 - odd].astype(BF16)


def outer_planes(velocity, ya, yb):
    slab = ((64, NX), BF16)
    return call(
        planes_kernel, "outer_planes", [slab, slab], [((2, 64, NX), F32)], 0, 10, velocity, ya, yb
    )


def stepped(columns, center, z_minus, z_plus, y_minus, y_plus, put):
    half, mix = 0.5 * time_step, viscosity
    lane = lax.broadcasted_iota(jnp.int32, (8, 128), 1)
    cells = [[center(d, j) for d in range(3)] for j in (-1, 0)]
    right = [[pltpu.roll(u, 1, 1) for u in column] for column in cells]
    left = [[pltpu.roll(u, 127, 1) for u in cells[1]]]
    for j in range(columns):
        mid, ahead = cells[1], [center(d, j + 1) for d in range(3)]
        right_ahead = [pltpu.roll(u, 1, 1) for u in ahead]
        left_ahead = [pltpu.roll(u, 127, 1) for u in ahead]
        plus = [mix - half * u for u in mid]
        minus = [mix + half * u for u in mid]
        for d in range(3):
            x_plus = jnp.where(lane == 127, left_ahead[d], left[0][d])
            x_minus = jnp.where(lane == 0, right[0][d], right[1][d])
            along_z = plus[0] * z_plus(d, j) + minus[0] * z_minus(d, j)
            along_y = plus[1] * y_plus(d, j) + minus[1] * y_minus(d, j)
            along_x = plus[2] * x_plus + minus[2] * x_minus
            put(d, j, ((1.0 - 6.0 * mix) * mid[d] + along_z) + (along_y + along_x))
        cells, right, left = [mid, ahead], [right[1], right_ahead], [left_ahead]


def column(n, j):
    return pl.ds(pl.multiple_of(lax.rem(n * CHUNK + 128 * j + NX, NX), 128), 128)


def step_plane(planes, edge, n, put):
    row = lax.broadcasted_iota(jnp.int32, (8, 128), 0)
    z_minus, center, z_plus = [lambda d, j, get=get: get(d, column(n, j)) for get in planes]
    rows = lambda d, j: edge(d, column(n, j))
    y_minus = lambda d, j: jnp.where(row == 0, rows(d, j), pltpu.roll(center(d, j), 1, 0))
    y_plus = lambda d, j: jnp.where(row == 7, rows(d, j), pltpu.roll(center(d, j), 7, 0))
    stepped(COLUMNS, center, z_minus, z_plus, y_minus, y_plus, put)


INNER, BELOW, ABOVE, Y_MINUS, Y_PLUS = range(5)


def step_one_kernel(vel_ref, za_ref, zb_ref, ya_ref, yb_ref, new, outer, edge, line):
    even = is_even("gx")
    for comp in range(3):
        low, high = sides(even, za_ref, zb_ref, pl.ds(16 * comp, 16))
        for p in range(2):
            outer[comp, p] = low[8 * p : 8 * p + 8]
            outer[comp, 2 + p] = high[8 * p : 8 * p + 8]
    corners = sides(even, za_ref, zb_ref, pl.ds(48, 16))
    slabs = sides(is_even("grp"), ya_ref, yb_ref, pl.ds(0, 48))
    for side, row, own, near, far in ((0, 0, 0, 1, 0), (1, 7, 7, 0, 1)):
        y_far, y_own = (Y_MINUS, Y_PLUS) if side == 0 else (Y_PLUS, Y_MINUS)
        for comp in range(3):
            for z in range(-1, 5):
                if 0 <= z < 4:
                    at = 8 * comp + 2 * z
                    value = line_of(slabs[side], at + near)
                    spot = pl.ds(4 * side + z, 1)
                    line[comp, INNER, spot, :] = value
                    line[comp, y_far, spot, :] = line_of(slabs[side], at + far)
                    line[comp, y_own, spot, :] = vel_ref[comp, z, own : own + 1, :]
                else:
                    at = 2 * comp + side
                    value = corners[0 if z < 0 else 1][at : at + 1]
                if z < 3:
                    line[comp, BELOW, pl.ds(4 * side + z + 1, 1), :] = value
                if z > 0:
                    line[comp, ABOVE, pl.ds(4 * side + z - 1, 1), :] = value
                edge[comp, z + 1, pl.ds(row, 1), :] = value

    def plane(z):
        if 0 <= z < 4:
            return lambda d, lanes: vel_ref[d, z, :, lanes]
        return lambda d, lanes: outer[d, z + 2 if z < 0 else z - 2, :, lanes]

    def chunk(n, carry):
        for z in range(-1, 5):

            def put(d, j, value):
                new[d, pl.ds(16 * (z + 1), 8), column(n, j)] = value

            step_plane(
                [plane(z - 1), plane(z), plane(z + 1)], lambda d, lanes: edge[d, z + 1, :, lanes], n, put
            )

        def put_line(d, j, value):
            for z in range(4):
                new[d, pl.ds(16 * (z + 1) + 8, 1), column(n, j)] = value[z : z + 1]
                new[d, pl.ds(16 * (z + 1) + 15, 1), column(n, j)] = value[4 + z : 5 + z]

        get = lambda kind: lambda d, j: line[d, kind, :, column(n, j)]
        stepped(COLUMNS, get(INNER), get(BELOW), get(ABOVE), get(Y_MINUS), get(Y_PLUS), put_line)
        return carry

    lax.fori_loop(0, NX // CHUNK, chunk, 0)


def step_two_kernel(new, out_ref, res, sems):
    def leave(n):
        lanes = pl.ds(pl.multiple_of(n * CHUNK, 128), CHUNK)
        return pltpu.make_async_copy(res.at[:, :, :, lanes], out_ref.at[:, :, :, lanes], sems.at[n])

    def plane(z):
        return lambda d, lanes: new[d, pl.ds(16 * (z + 1), 8), lanes]

    def chunk(n, carry):
        for z in range(4):

            def put(d, j, value):
                res[d, z, :, column(n, j)] = value

            step_plane(
                [plane(z - 1), plane(z), plane(z + 1)],
                lambda d, lanes: new[d, pl.ds(16 * (z + 1) + 8, 8), lanes], n, put,
            )
        leave(n).start()
        return carry

    lax.fori_loop(0, NX // CHUNK, chunk, 0)
    for n in range(NX // CHUNK):
        leave(n).wait()


def step_one(velocity, za, zb, ya, yb):
    return call(
        step_one_kernel, "step_one", [((3, 16 * 6, NX), F32)],
        [((3, 4, 8, NX), F32), ((3, 6, 8, NX), F32), ((3, 5, 8, NX), F32)],
        20_000_000, 24, velocity, za, zb, ya, yb,
    )[0]


def step_two(new):
    return pl.pallas_call(
        step_two_kernel,
        out_shape=jax.ShapeDtypeStruct((3, 4, ROWS, NX), F32),
        in_specs=[pl.BlockSpec(memory_space=pltpu.VMEM)],
        out_specs=pl.BlockSpec(memory_space=pltpu.HBM),
        scratch_shapes=[
            pltpu.VMEM((3, 4, ROWS, NX), F32),
            pltpu.SemaphoreType.DMA((NX // CHUNK,)),
        ],
        compiler_params=pltpu.CompilerParams(vmem_limit_bytes=12 * 1024 * 1024),
        cost_estimate=pl.CostEstimate(flops=10_000_000, bytes_accessed=1_000_000, transcendentals=0),
        name="step_two",
    )(new)


def first_layer_places():
    places = np.zeros((6, 4, 144, 32), np.float32)
    for r in range(6):
        for group, col in enumerate(GROUP_COL):
            for a in range(3):
                for b in range(3):
                    for c in range(3):
                        j = b + 1 + col
                        places[r, group, j * 24 + c * 8 + r + a, a * 9 + b * 3 + c] = 1.0
    return places


def weights_kernel(
    places_ref, first_ref, second_ref, middle_ref, joined_ref, fine_ref, coarse_ref, labf_ref, labc_ref,
    w1_ref, w2_ref, w3_ref, w4_ref, hf_ref, hc_ref, hits_fine, hits_coarse, even_ref, flat, planar,
):
    flat[...] = jnp.zeros((32, 64), F32)
    for tap in range(9):
        flat[pl.ds(3 * tap, 3), :] = first_ref[tap // 3, tap % 3].astype(F32)
    first_taps = flat[...].astype(BF16)
    for r in range(6):
        parts = [dot_nn(places_ref[r, g], first_taps) for g in range(4)]
        w1_ref[r] = jnp.concatenate(parts, axis=1).astype(BF16)

    none = jnp.zeros((64, 64), F32)

    def spread(taps, out_ref):
        for k in range(4):
            for group, col in enumerate(GROUP_COL):
                blocks = []
                for py in range(2):
                    for px in range(2):
                        a, b = k - py, col - px + 1
                        inside = 0 <= a <= 2 and 0 <= b <= 2
                        blocks.append(taps[a][b] if inside else none)
                block = jnp.concatenate(blocks, axis=1).astype(BF16)
                out_ref[pl.ds(k * 256 + group * 64, 64), :] = block

    spread([[second_ref[a, b].astype(F32).T for b in range(3)] for a in range(3)], w2_ref)

    wide_none = jnp.zeros((64, 128), F32)
    taps = [[middle_ref[a, b].astype(F32) for b in range(3)] for a in range(3)]
    for k in range(4):
        for place, b in enumerate((0, 2, 1, None)):
            blocks = []
            for e in range(2):
                inside = b is not None and 0 <= k - e <= 2
                blocks.append(taps[k - e][b] if inside else wide_none)
            block = jnp.concatenate(blocks, axis=1).astype(BF16)
            w3_ref[pl.ds(k * 256 + place * 64, 64), :] = block

    joined = [[joined_ref[a, b].astype(F32).T for b in range(3)] for a in range(3)]
    spread([[joined[a][b][128:192] for b in range(3)] for a in range(3)], w4_ref)
    for dy in range(3):
        for dx in range(3):
            blocks = []
            for py in range(2):
                for px in range(2):
                    total = jnp.zeros((128, 64), F32)
                    for a in range(3):
                        for b in range(3):
                            if (py + a - 1) // 2 + 1 == dy and (px + b - 1) // 2 + 1 == dx:
                                total = total + joined[a][b][0:128]
                    blocks.append(total)
            block = jnp.concatenate(blocks, axis=1).astype(BF16)
            w4_ref[pl.ds(1024 + (dy * 3 + dx) * 128, 128), :] = block

    col = lax.broadcasted_iota(jnp.int32, (256, 256), 0)
    planar_col = lax.broadcasted_iota(jnp.int32, (256, 256), 1)
    to_planar = (col == 2 * (planar_col & 127) + (planar_col >> 7)).astype(F32).astype(BF16)
    planar[...] = dot_nn(labf_ref[...].astype(F32).astype(BF16), to_planar)
    classes = lax.broadcasted_iota(jnp.int32, (NCLS, 128), 0)
    for y in range(4):
        for snap in range(SNAP):
            lanes = pl.ds(128 * (4 * y + snap), 128)
            hits_coarse[:, lanes] = (classes == labc_ref[pl.ds(snap * 4 + y, 1), :]).astype(F32)
            for py in range(2):
                row = pl.ds(snap * 8 + 2 * y + py, 1)
                for px in range(2):
                    label = planar[row, pl.ds(128 * px, 128)]
                    hits_fine[pl.ds((2 * py + px) * 8, 8), lanes] = (classes.astype(F32) == label).astype(F32)

    spot = lax.broadcasted_iota(jnp.int32, (XB, 384), 0)
    wanted = jnp.where(spot >= 142, 2 * spot + 94, 2 * spot - 2)
    wanted = jnp.where(wanted < 0, wanted + 384, wanted)
    hit = lax.broadcasted_iota(jnp.int32, (XB, 384), 1) == wanted
    even_ref[...] = hit.astype(F32).astype(BF16)

    head = fine_ref[...]
    high = head.astype(BF16).astype(F32)
    empty = jnp.zeros((NCLS, 64), F32)
    rows = []
    for part in (high, head - high):
        for spot in range(4):
            rows.append(jnp.concatenate([part if i == spot else empty for i in range(4)], axis=1))
    hf_ref[...] = jnp.concatenate(rows, axis=0).astype(BF16)
    head = coarse_ref[...]
    high = head.astype(BF16).astype(F32)
    hc_ref[...] = jnp.concatenate([high, head - high], axis=0).astype(BF16)


def block_weights(
    conv_first, conv_second, conv_middle, conv_joined, head_fine, head_coarse, labels_fine, labels_coarse
):
    swapped = (0, 1, 3, 2)
    return call(
        weights_kernel, "block_weights",
        [
            ((6, 144, 256), BF16), ((1024, 256), BF16), ((1024, 256), BF16),
            ((1024 + 1152, 256), BF16), ((64, 256), BF16), ((16, 128), BF16),
            ((32, 2048), F32), ((8, 2048), F32), ((XB, 384), BF16),
        ],
        [((32, 64), F32), ((32, 256), F32)], 0, 12,
        jnp.asarray(first_layer_places(), BF16), jnp.transpose(conv_first, swapped), conv_second,
        jnp.transpose(conv_middle, swapped), conv_joined, head_fine, head_coarse,
        labels_fine.reshape(SNAP * ROWS, COLS), labels_coarse.reshape(SNAP * 4, 128),
    )


def keep_padded(buf, value):
    buf[8 : 8 + M, :] = value
    buf[7:8, :] = value[M - 1 : M]
    buf[8 + M : 9 + M, :] = value[0:1]


def first_kernel(a_ref, mid_ref, b_ref, w1_ref, even_ref, h1, win, taps):
    row384 = lax.broadcasted_iota(jnp.int32, (8, 384), 0)
    up, down = sides(is_even("grp"), a_ref, b_ref, pl.ds(0, 208))
    tiles = [up, mid_ref[...].astype(F32), down]
    for q in range(12):
        pieces = []
        for tile in tiles:
            edge = tile[192 + 8 * (q % 2) : 200 + 8 * (q % 2)]
            edge = pltpu.roll(edge, 128 - (16 * (q // 2) + 8), 1)
            pieces.append(
                jnp.concatenate([tile[8 * q : 8 * q + 8], tile[96 + 8 * q : 104 + 8 * q], edge], axis=1)
            )
        top, center, bottom = pieces
        snap, comp = q // 3, q % 3
        rows = pl.ds(comp * 8, 8)
        win[0, snap, rows, :] = jnp.where(row384 < 6, pltpu.roll(top, 6, 0), pltpu.roll(center, 6, 0))
        win[1, snap, rows, :] = center
        win[2, snap, rows, :] = jnp.where(row384 < 2, pltpu.roll(center, 2, 0), pltpu.roll(bottom, 2, 0))

    even = even_ref[...]
    own = lax.broadcasted_iota(jnp.int32, (XB, 144), 0) < 142
    for group in range(3):
        found = []
        for snap in range(SNAP):
            window = win[group, snap]
            shifted = [window] + [pltpu.roll(window, 384 - j, 1) for j in range(1, 6)]
            stack = jnp.concatenate(shifted, axis=0).astype(BF16)
            found.append(dot_nt(even, stack))
        for snap in range(SNAP):
            rows = jnp.where(own, found[snap], found[(snap + 1) % SNAP])
            taps[group, pl.ds(snap * XB, XB), :] = rows.astype(BF16)

    for i in range(18):
        out = dot_nn(taps[i // 6], w1_ref[i % 6])
        h1[i] = jnp.maximum(out, 0.0).astype(BF16)


def second_kernel(h1, w2_ref, h2, ph, sbuf, pbuf):
    side = lax.broadcasted_iota(jnp.int32, (M, 128), 1) < 64

    def pool(q, out):
        pooled = jnp.maximum(out[:, 0:128], out[:, 128:256])
        pooled = jnp.maximum(pooled, pltpu.roll(pooled, 64, 1))
        keep_padded(pbuf, pooled)
        ph[q, :, 0:128] = jnp.where(side, pbuf[7 : 7 + M, :], pbuf[9 : 9 + M, :]).astype(BF16)
        ph[q, :, 128:256] = pooled.astype(BF16)

    def row(q):
        lhs = jnp.concatenate([h1[2 * q + k] for k in range(4)], axis=1)
        return jnp.maximum(dot_nn(lhs, w2_ref[...]), 0.0)

    for q in range(8):
        out = row(q)
        if 0 < q < 7:
            keep_padded(sbuf, out)
            for py in range(2):
                lanes = pl.ds(128 * py, 128)
                h2[2 * q - 2 + py, :, 0:128] = out[:, 128 * py : 128 * py + 128].astype(BF16)
                beside = jnp.where(side, sbuf[9 : 9 + M, lanes], sbuf[7 : 7 + M, lanes])
                h2[2 * q - 2 + py, :, 128:256] = beside.astype(BF16)
        pool(q, out)


def class_terms(logits, onehot):
    peak = jnp.max(logits, axis=0, keepdims=True)
    powers = jnp.exp(logits - peak)
    total = jnp.sum(powers, axis=0, keepdims=True)
    lost = onehot * (peak + jnp.log(total) - logits)
    return lost, powers / total - onehot


def cells(kept, lanes):
    return jnp.concatenate(
        [kept[y, pl.ds(snap * XB, 128), lanes] for y in kept_rows(kept) for snap in range(SNAP)], axis=0
    )


def kept_rows(kept):
    return range(1, 5) if kept.shape[0] == 6 else range(4)


def fold(lost):
    total = lost[:, 0:128]
    for block in range(1, 16):
        total = total + lost[:, 128 * block : 128 * block + 128]
    return total


def middle_kernel(ph, w3_ref, hc_ref, hits_ref, mh, sums_ref, mbuf):
    def middle_rows(t, carry):
        lhs = jnp.concatenate([ph[2 * t + k] for k in range(4)], axis=1)
        out = jnp.maximum(dot_nn(lhs, w3_ref[...]), 0.0)
        for e in range(2):
            value = out[:, 128 * e : 128 * e + 128]
            keep_padded(mbuf, value)
            row = 2 * t + e
            mh[row, :, 0:128] = mbuf[7 : 7 + M, :].astype(BF16)
            mh[row, :, 128:256] = value.astype(BF16)
            mh[row, :, 256:384] = mbuf[9 : 9 + M, :].astype(BF16)
        return carry

    lax.fori_loop(0, 3, middle_rows, 0)

    feature = cells(mh, pl.ds(128, 128))
    both = dot_nt(hc_ref[...], feature)
    lost, grad = class_terms(both[0:8] + both[8:16], hits_ref[...])
    high = grad.astype(BF16).astype(F32)
    slopes = jnp.concatenate([high, grad - high], axis=0).astype(BF16)
    total = dot_nn(slopes, feature)
    coarse_cells = 262144.0
    sums_ref[0:8, :] = (total[0:8] + total[8:16]) * (1.0 / coarse_cells)
    sums_ref[8:16, :] = fold(lost) * (1.0 / coarse_cells)


def decoded_kernel(
    h2, mh, w4_ref, hf_ref, hits_ref, coarse_ref, planar_ref, sums_ref, dec
):
    for y in range(4):
        lhs = jnp.concatenate(
            [h2[2 * y + 1 + k] for k in range(4)] + [mh[y + k] for k in range(3)], axis=1
        )
        dec[y] = jnp.maximum(dot_nn(lhs, w4_ref[...]), 0.0).astype(BF16)

    feature = cells(dec, pl.ds(0, 256))
    both = dot_nt(hf_ref[...], feature)
    logits = both[0:32] + both[32:64]
    planar_ref[...] = logits
    lost_fine = jnp.zeros((NCLS, 2048), F32)
    slopes = []
    for py in range(2):
        for px in range(2):
            at = (2 * py + px) * 8
            lost, grad = class_terms(logits[at : at + 8], hits_ref[pl.ds(at, 8), :])
            lost_fine = lost_fine + lost
            slopes.append(grad)
    high, low = split_two(jnp.concatenate(slopes, axis=0))
    grad_fine = dot_nn(jnp.concatenate([high, low], axis=0), feature)

    fine_cells = 1048576.0
    total = jnp.zeros((NCLS, 64), F32)
    for spot in range(4):
        for part in (0, 32):
            block = grad_fine[part + 8 * spot : part + 8 * spot + 8]
            total = total + block[:, 64 * spot : 64 * spot + 64]
    loss = jnp.sum(fold(lost_fine)) * (1.0 / fine_cells) + jnp.sum(coarse_ref[8:16, :])
    sums_ref[0:8, :] = coarse_ref[0:8, :]
    sums_ref[8:16, :] = jnp.concatenate(
        [total * (1.0 / fine_cells), jnp.broadcast_to(loss, (NCLS, 64))], axis=1
    )


def ordered_kernel(planar_ref, logits_ref):
    col = lax.broadcasted_iota(jnp.int32, (256, 256), 0)
    planar_col = lax.broadcasted_iota(jnp.int32, (256, 256), 1)
    to_cols = (planar_col == 2 * (col & 127) + (col >> 7)).astype(F32).astype(BF16)
    logits = planar_ref[...]
    order = [(snap, y, py) for snap in range(SNAP) for y in range(4) for py in range(2)]
    halves = []
    for px in range(2):
        blocks = []
        for snap, y, py in order:
            lane = 128 * (4 * y + snap)
            blocks.append(logits[(2 * py + px) * 8 : (2 * py + px) * 8 + 8, lane : lane + 128])
        halves.append(jnp.concatenate(blocks, axis=0))
    whole = jnp.concatenate(halves, axis=1)
    high = whole.astype(BF16)
    rest = whole - high.astype(F32)
    middle_term = rest.astype(BF16)
    low = (rest - middle_term.astype(F32)).astype(BF16)
    ordered = dot_nn(high, to_cols) + dot_nn(middle_term, to_cols) + dot_nn(low, to_cols)
    for row in range(32):
        logits_ref[row] = ordered[8 * row : 8 * row + 8]


def first(a, mid, b, w1, even):
    return call(
        first_kernel, "first", [((18, M, 256), BF16)],
        [((3, SNAP, 24, 384), F32), ((3, M, 144), BF16)],
        2_000_000_000, 14, a, mid, b, w1, even,
    )[0]


def second(h1, w2):
    return call(
        second_kernel, "second", [((12, M, 256), BF16), ((8, M, 256), BF16)],
        [((M + 16, 256), F32), ((M + 16, 128), F32)],
        2_500_000_000, 18, h1, w2,
    )


def middle(ph, w3, hc, labels):
    return call(
        middle_kernel, "middle", [((6, M, 384), BF16), ((16, 128), F32)],
        [((M + 16, 128), F32)], 1_000_000_000, 12, ph, w3, hc, labels,
    )


def decoded(h2, mh, w4, hf, labels, coarse):
    return call(
        decoded_kernel, "decoded", [((32, 2048), F32), ((16, 128), F32)],
        [((4, M, 256), BF16)],
        2_500_000_000, 16, h2, mh, w4, hf, labels, coarse,
    )


def ordered(planar):
    return call(
        ordered_kernel, "ordered", [((32, NCLS, COLS), F32)], [], 300_000_000, 6, planar
    )[0]


def mesh_pairs(change):
    pairs = []
    for device in range(128):
        grp, gx = device // 16, device % 16
        at = {"x": (gx // 2 % 2) * 2 + grp // 4, "y": grp % 4, "z": gx // 4, "core": gx % 2}
        change(at)
        grp = (at["x"] % 2) * 4 + at["y"]
        gx = (at["z"] * 2 + at["x"] // 2) * 2 + at["core"]
        pairs.append((device, grp * 16 + gx))
    return pairs


def flip(x, name, bits):
    def change(at):
        at[name] ^= bits

    return lax.ppermute(x, AXES, mesh_pairs(change))


def finish_kernel(a, b, c, d, loss, fine, coarse):
    total = (a[...] + b[...]) + (c[...] + d[...])
    coarse[...] = total[0:8]
    fine[...] = total[8:16, 0:64]
    loss[...] = total[8:9, 64:65]


tie = lax.optimization_barrier


def near(x):
    return pltpu.with_memory_space_constraint(x, pltpu.VMEM)


def body(
    velocity, snapshot_index, labels_fine, labels_coarse,
    conv_first, conv_second, conv_middle, conv_joined, head_fine, head_coarse,
):
    keep, give = pack(velocity, snapshot_index)
    line_a, line_b = outer_lines(velocity)
    weights = block_weights(
        conv_first, conv_second, conv_middle, conv_joined, head_fine, head_coarse, labels_fine, labels_coarse
    )
    got = exchange_a(give, "gx")
    block = ((2, 208, 128), BF16)
    own, one, two, three = call(merge_kernel, "merge", [block] * 4, [], 1, 8, near(keep), near(got))
    own, line_a, line_b = tie((own, line_a, line_b))
    two, one, three = flip(two, "z", 2), flip(one, "z", 1), flip(three, "z", 3)
    line_a, line_b = exchange_a(line_a, "grp"), exchange_b(line_b, "grp")
    own, weights = tie((own, weights))
    block = ((208, 128), BF16)
    mine, theirs = call(
        gather_kernel, "gather", [block] * 2, [], 3_000_000_000, 8, near(own), near(two), near(one), near(three)
    )
    got = lax.ppermute(theirs, "gx", [(i, i ^ 2) for i in range(16)])
    mine, line_a, line_b = tie((mine, line_a, line_b))
    plane_a, plane_b = outer_planes(velocity, line_a, line_b)
    tile = mine + got
    tile, plane_a, plane_b = tie((tile, plane_a, plane_b))
    tile_a, tile_b = exchange_a(tile, "grp"), exchange_b(tile, "grp")
    plane_b, plane_a = exchange_b(plane_b, "gx"), exchange_a(plane_a, "gx")
    w1, w2, w3, w4, hf, hc, hits_fine, hits_coarse, even = weights
    h2, ph = second(first(tile_a, tile, tile_b, w1, even), w2)
    mh, coarse = middle(ph, w3, hc, hits_coarse)
    planar, sums = decoded(h2, mh, w4, hf, hits_fine, coarse)

    got = flip(sums, "core", 1)
    logits = ordered(planar)
    sums, logits, plane_a, plane_b = tie((sums + got, logits, plane_a, plane_b))
    got = flip(sums, "z", 1)
    new = step_one(velocity, plane_a, plane_b, line_a, line_b)
    sums, new = tie((sums + got, new))
    got = flip(sums, "z", 3)
    field = step_two(new)
    sums, field = tie((sums + got, field))
    sums = (sums + flip(sums, "y", 1)) + (flip(sums, "y", 2) + flip(sums, "y", 3))
    loss, grad_fine, grad_coarse = call(
        finish_kernel, "finish", [((1, 1), F32), ((8, 64), F32), ((8, 128), F32)], [], 1, 4,
        sums, flip(sums, "x", 1), flip(sums, "x", 2), flip(sums, "x", 3),
    )
    return (
        field,
        logits.reshape(SNAP, ROWS, NCLS, COLS),
        loss.reshape(()),
        grad_fine,
        grad_coarse,
    )


def solution(mesh):
    return jax.shard_map(
        body,
        mesh=mesh,
        in_specs=(
            P(None, "gx", "grp", None),
            P(),
            P(None, "grp", "gx"),
            P(None, "grp", "gx"),
            P(),
            P(),
            P(),
            P(),
            P(),
            P(),
        ),
        out_specs=(P(None, "gx", "grp", None), P(None, "grp", None, "gx"), P(), P(), P()),
        check_vma=False,
    )
```

```python
import functools

import jax
import jax.numpy as jnp
import numpy as np
from jax import lax
from jax.experimental import pallas as pl
from jax.experimental.pallas import tpu as pltpu
from jax.sharding import PartitionSpec as P

F32, BF16 = jnp.float32, jnp.bfloat16
AXES = ("grp", "gx")
SNAP, NCLS = 4, 8
ROWS, COLS = 8, 256
XB = 144
M = SNAP * XB
NX = 4096
CHUNK = 1024
COLUMNS = CHUNK // 128
HALF = NX // 2
UNROLL = 2
time_step = 0.2
viscosity = 0.1
GROUP_COL = (0, 1, 2, -1)


def dot_nn(a, b):
    return lax.dot_general(a, b, (((1,), (0,)), ((), ())), preferred_element_type=F32)


def dot_nt(a, b):
    return lax.dot_general(a, b, (((1,), (1,)), ((), ())), preferred_element_type=F32)


def split_two(value):
    high = value.astype(BF16)
    return high, (value - high.astype(F32)).astype(BF16)


def call(kernel, name, outs, scratch, flops, limit, *args, scalars=0):
    vmem = pl.BlockSpec(memory_space=pltpu.VMEM)
    smem = pl.BlockSpec(memory_space=pltpu.SMEM)
    return pl.pallas_call(
        kernel,
        out_shape=tuple(jax.ShapeDtypeStruct(*out) for out in outs),
        in_specs=[smem] * scalars + [vmem] * (len(args) - scalars),
        out_specs=(vmem,) * len(outs),
        scratch_shapes=[pltpu.VMEM(*one) for one in scratch],
        compiler_params=pltpu.CompilerParams(vmem_limit_bytes=limit * 1024 * 1024),
        cost_estimate=pl.CostEstimate(flops=flops, bytes_accessed=1_000_000, transcendentals=0),
        name=name,
    )(*args)


def exchange_a(x, axis):
    return lax.ppermute(x, axis, [(i, i ^ 1) for i in range(lax.axis_size(axis))])


def exchange_b(x, axis):
    count = lax.axis_size(axis)
    return lax.ppermute(x, axis, [(i, (((i + 1) ^ 1) - 1) % count) for i in range(count)])


def is_even(axis):
    return lax.rem(lax.axis_index(axis), 2) == 0


def pack_kernel(index_hbm, vel_hbm, keep_ref, give_ref, planes, vel_ref, index_ref, sems):
    fetch = pltpu.make_async_copy(index_hbm, index_ref, sems.at[0])
    fetch.start()
    copies = [pltpu.make_async_copy(vel_hbm.at[c], vel_ref.at[c], sems.at[1 + c]) for c in range(3)]
    for copy in copies:
        copy.start()
    planes[...] = jnp.zeros((96, NX), F32)
    place = lax.axis_index("gx")
    fetch.wait()
    for copy in copies:
        copy.wait()
    for snap in range(SNAP):
        local = index_ref[snap] - place * 4
        spot = jnp.clip(local, 0, 3)

        @pl.when(jnp.logical_and(local >= 0, local < 4))
        def _():
            for comp in range(3):
                planes[pl.ds((snap * 3 + comp) * ROWS, ROWS), :] = vel_ref[comp, spot]

    lane = lax.broadcasted_iota(jnp.int32, (16, 128), 1)
    core = lax.rem(place, 2)

    def targets(n, carry):
        for other, out_ref in ((0, keep_ref), (1, give_ref)):
            j = 2 * n + (core + other * (1 - 2 * core))
            depth, half = n // 2, lax.rem(n, 2)
            base = pl.multiple_of(j * COLS, COLS)
            out_ref[depth, half, 0:96, :] = planes[:, pl.ds(base, 128)].astype(BF16)
            out_ref[depth, half, 96:192, :] = planes[:, pl.ds(base + 128, 128)].astype(BF16)
            after = pl.multiple_of(lax.rem(base + COLS, NX), 128)
            before = pl.multiple_of(lax.rem(base + NX - 128, NX), 128)
            packed = jnp.zeros((16, 128), F32)
            for pair in range(6):
                edge = jnp.where(
                    lane < 64,
                    planes[pl.ds(16 * pair, 16), pl.ds(after, 128)],
                    planes[pl.ds(16 * pair, 16), pl.ds(before, 128)],
                )
                edge = pltpu.roll(edge, 16 * pair + 8, 1)
                packed = jnp.where((lane >> 4) == pair, edge, packed)
            out_ref[depth, half, 192:208, :] = packed.astype(BF16)
        return carry

    lax.fori_loop(0, 8, targets, 0, unroll=UNROLL)


def pack(velocity, index):
    vmem = pl.BlockSpec(memory_space=pltpu.VMEM)
    blocks = jax.ShapeDtypeStruct((4, 2, 208, 128), BF16)
    return pl.pallas_call(
        pack_kernel,
        out_shape=(blocks, blocks),
        in_specs=[pl.BlockSpec(memory_space=pltpu.HBM)] * 2,
        out_specs=(vmem, vmem),
        scratch_shapes=[
            pltpu.VMEM((96, NX), F32),
            pltpu.VMEM((3, 4, ROWS, NX), F32),
            pltpu.SMEM((SNAP,), jnp.int32),
            pltpu.SemaphoreType.DMA((4,)),
        ],
        compiler_params=pltpu.CompilerParams(vmem_limit_bytes=10 * 1024 * 1024),
        cost_estimate=pl.CostEstimate(flops=0, bytes_accessed=1_000_000, transcendentals=0),
        name="pack",
    )(
        pltpu.with_memory_space_constraint(index, pltpu.HBM),
        pltpu.with_memory_space_constraint(velocity, pltpu.HBM),
    )


def merge_kernel(keep_ref, got_ref, own, one, two, three):
    depth = lax.axis_index("gx") // 4
    high, low = depth // 2, lax.rem(depth, 2)
    for k, out_ref in enumerate((own, one, two, three)):
        flip_low = low if k % 2 == 0 else 1 - low
        flip_high = high if k // 2 == 0 else 1 - high
        at = 2 * flip_high + flip_low
        out_ref[...] = keep_ref[at] + got_ref[at]


def gather_kernel(own, two, one, three, mine, theirs):
    half = lax.rem(lax.axis_index("gx") // 2, 2)
    for out_ref, at in ((mine, half), (theirs, 1 - half)):
        out_ref[...] = (own[at] + two[at]) + (one[at] + three[at])


def sides(even, a_ref, b_ref, rows):
    a, b = a_ref[rows, :].astype(F32), b_ref[rows, :].astype(F32)
    return jnp.where(even, b, a), jnp.where(even, a, b)


def lines_kernel(vel_ref, a_ref, b_ref, rows):
    for comp in range(3):
        for slot, at in ((0, 6), (1, 0)):
            for z in range(4):
                for h in range(2):
                    rows[slot, pl.ds(24 * h + 8 * comp + 2 * z, 2), :] = vel_ref[
                        comp, z, at : at + 2, HALF * h : HALF * h + HALF
                    ]
    odd = lax.rem(lax.axis_index("grp"), 2)
    a_ref[...] = rows[odd].astype(BF16)
    b_ref[...] = rows[1 - odd].astype(BF16)


def line_of(slab, at):
    return jnp.concatenate([slab[at : at + 1], slab[24 + at : 25 + at]], axis=1)


def outer_lines(velocity):
    slab = ((48, HALF), BF16)
    return call(lines_kernel, "outer_lines", [slab, slab], [((2, 48, HALF), F32)], 0, 8, velocity)


def planes_kernel(vel_ref, ya_ref, yb_ref, a_ref, b_ref, rows):
    before, after = sides(is_even("grp"), ya_ref, yb_ref, pl.ds(0, 48))
    for slot, base, edge in ((0, 2, 3), (1, 0, 0)):
        rows[slot, 48:64, :] = jnp.zeros((16, NX), F32)
        for comp in range(3):
            for p in range(2):
                rows[slot, pl.ds((comp * 2 + p) * 8, 8), :] = vel_ref[comp, base + p]
            at = 8 * comp + 2 * edge
            rows[slot, pl.ds(48 + 2 * comp, 1), :] = line_of(before, at + 1)
            rows[slot, pl.ds(49 + 2 * comp, 1), :] = line_of(after, at)
    odd = lax.rem(lax.axis_index("gx"), 2)
    a_ref[...] = rows[odd].astype(BF16)
    b_ref[...] = rows[1 - odd].astype(BF16)


def outer_planes(velocity, ya, yb):
    slab = ((64, NX), BF16)
    return call(
        planes_kernel, "outer_planes", [slab, slab], [((2, 64, NX), F32)], 0, 10, velocity, ya, yb
    )


def stepped(columns, center, z_minus, z_plus, y_minus, y_plus, put):
    half, mix = 0.5 * time_step, viscosity
    lane = lax.broadcasted_iota(jnp.int32, (8, 128), 1)
    cells = [[center(d, j) for d in range(3)] for j in (-1, 0)]
    right = [[pltpu.roll(u, 1, 1) for u in column] for column in cells]
    left = [[pltpu.roll(u, 127, 1) for u in cells[1]]]
    for j in range(columns):
        mid, ahead = cells[1], [center(d, j + 1) for d in range(3)]
        right_ahead = [pltpu.roll(u, 1, 1) for u in ahead]
        left_ahead = [pltpu.roll(u, 127, 1) for u in ahead]
        plus = [mix - half * u for u in mid]
        minus = [mix + half * u for u in mid]
        for d in range(3):
            x_plus = jnp.where(lane == 127, left_ahead[d], left[0][d])
            x_minus = jnp.where(lane == 0, right[0][d], right[1][d])
            along_z = plus[0] * z_plus(d, j) + minus[0] * z_minus(d, j)
            along_y = plus[1] * y_plus(d, j) + minus[1] * y_minus(d, j)
            along_x = plus[2] * x_plus + minus[2] * x_minus
            put(d, j, ((1.0 - 6.0 * mix) * mid[d] + along_z) + (along_y + along_x))
        cells, right, left = [mid, ahead], [right[1], right_ahead], [left_ahead]


def column(n, j):
    return pl.ds(pl.multiple_of(lax.rem(n * CHUNK + 128 * j + NX, NX), 128), 128)


def step_plane(planes, edge, n, put):
    row = lax.broadcasted_iota(jnp.int32, (8, 128), 0)
    z_minus, center, z_plus = [lambda d, j, get=get: get(d, column(n, j)) for get in planes]
    rows = lambda d, j: edge(d, column(n, j))
    y_minus = lambda d, j: jnp.where(row == 0, rows(d, j), pltpu.roll(center(d, j), 1, 0))
    y_plus = lambda d, j: jnp.where(row == 7, rows(d, j), pltpu.roll(center(d, j), 7, 0))
    stepped(COLUMNS, center, z_minus, z_plus, y_minus, y_plus, put)


INNER, BELOW, ABOVE, Y_MINUS, Y_PLUS = range(5)


def step_one_kernel(vel_ref, za_ref, zb_ref, ya_ref, yb_ref, new, outer, edge, line):
    even = is_even("gx")
    for comp in range(3):
        low, high = sides(even, za_ref, zb_ref, pl.ds(16 * comp, 16))
        for p in range(2):
            outer[comp, p] = low[8 * p : 8 * p + 8]
            outer[comp, 2 + p] = high[8 * p : 8 * p + 8]
    corners = sides(even, za_ref, zb_ref, pl.ds(48, 16))
    slabs = sides(is_even("grp"), ya_ref, yb_ref, pl.ds(0, 48))
    for side, row, own, near, far in ((0, 0, 0, 1, 0), (1, 7, 7, 0, 1)):
        y_far, y_own = (Y_MINUS, Y_PLUS) if side == 0 else (Y_PLUS, Y_MINUS)
        for comp in range(3):
            for z in range(-1, 5):
                if 0 <= z < 4:
                    at = 8 * comp + 2 * z
                    value = line_of(slabs[side], at + near)
                    spot = pl.ds(4 * side + z, 1)
                    line[comp, INNER, spot, :] = value
                    line[comp, y_far, spot, :] = line_of(slabs[side], at + far)
                    line[comp, y_own, spot, :] = vel_ref[comp, z, own : own + 1, :]
                else:
                    at = 2 * comp + side
                    value = corners[0 if z < 0 else 1][at : at + 1]
                if z < 3:
                    line[comp, BELOW, pl.ds(4 * side + z + 1, 1), :] = value
                if z > 0:
                    line[comp, ABOVE, pl.ds(4 * side + z - 1, 1), :] = value
                edge[comp, z + 1, pl.ds(row, 1), :] = value

    def plane(z):
        if 0 <= z < 4:
            return lambda d, lanes: vel_ref[d, z, :, lanes]
        return lambda d, lanes: outer[d, z + 2 if z < 0 else z - 2, :, lanes]

    def chunk(n, carry):
        for z in range(-1, 5):

            def put(d, j, value):
                new[d, pl.ds(16 * (z + 1), 8), column(n, j)] = value

            step_plane(
                [plane(z - 1), plane(z), plane(z + 1)], lambda d, lanes: edge[d, z + 1, :, lanes], n, put
            )

        def put_line(d, j, value):
            for z in range(4):
                new[d, pl.ds(16 * (z + 1) + 8, 1), column(n, j)] = value[z : z + 1]
                new[d, pl.ds(16 * (z + 1) + 15, 1), column(n, j)] = value[4 + z : 5 + z]

        get = lambda kind: lambda d, j: line[d, kind, :, column(n, j)]
        stepped(COLUMNS, get(INNER), get(BELOW), get(ABOVE), get(Y_MINUS), get(Y_PLUS), put_line)
        return carry

    lax.fori_loop(0, NX // CHUNK, chunk, 0)


def step_two_kernel(new, out_ref, res, sems):
    def leave(n):
        lanes = pl.ds(pl.multiple_of(n * CHUNK, 128), CHUNK)
        return pltpu.make_async_copy(res.at[:, :, :, lanes], out_ref.at[:, :, :, lanes], sems.at[n])

    def plane(z):
        return lambda d, lanes: new[d, pl.ds(16 * (z + 1), 8), lanes]

    def chunk(n, carry):
        for z in range(4):

            def put(d, j, value):
                res[d, z, :, column(n, j)] = value

            step_plane(
                [plane(z - 1), plane(z), plane(z + 1)],
                lambda d, lanes: new[d, pl.ds(16 * (z + 1) + 8, 8), lanes], n, put,
            )
        leave(n).start()
        return carry

    lax.fori_loop(0, NX // CHUNK, chunk, 0)
    for n in range(NX // CHUNK):
        leave(n).wait()


def step_one(velocity, za, zb, ya, yb):
    return call(
        step_one_kernel, "step_one", [((3, 16 * 6, NX), F32)],
        [((3, 4, 8, NX), F32), ((3, 6, 8, NX), F32), ((3, 5, 8, NX), F32)],
        20_000_000, 24, velocity, za, zb, ya, yb,
    )[0]


def step_two(new):
    return pl.pallas_call(
        step_two_kernel,
        out_shape=jax.ShapeDtypeStruct((3, 4, ROWS, NX), F32),
        in_specs=[pl.BlockSpec(memory_space=pltpu.VMEM)],
        out_specs=pl.BlockSpec(memory_space=pltpu.HBM),
        scratch_shapes=[
            pltpu.VMEM((3, 4, ROWS, NX), F32),
            pltpu.SemaphoreType.DMA((NX // CHUNK,)),
        ],
        compiler_params=pltpu.CompilerParams(vmem_limit_bytes=12 * 1024 * 1024),
        cost_estimate=pl.CostEstimate(flops=10_000_000, bytes_accessed=1_000_000, transcendentals=0),
        name="step_two",
    )(new)


def first_layer_places():
    places = np.zeros((6, 4, 144, 32), np.float32)
    for r in range(6):
        for group, col in enumerate(GROUP_COL):
            for a in range(3):
                for b in range(3):
                    for c in range(3):
                        j = b + 1 + col
                        places[r, group, j * 24 + c * 8 + r + a, a * 9 + b * 3 + c] = 1.0
    return places


def weights_kernel(
    places_ref, first_ref, second_ref, middle_ref, joined_ref, fine_ref, coarse_ref, labf_ref, labc_ref,
    w1_ref, w2_ref, w3_ref, w4_ref, hf_ref, hc_ref, hits_fine, hits_coarse, even_ref, flat, planar,
):
    flat[...] = jnp.zeros((32, 64), F32)
    for tap in range(9):
        flat[pl.ds(3 * tap, 3), :] = first_ref[tap // 3, tap % 3].astype(F32)
    first_taps = flat[...].astype(BF16)
    for r in range(6):
        parts = [dot_nn(places_ref[r, g], first_taps) for g in range(4)]
        w1_ref[r] = jnp.concatenate(parts, axis=1).astype(BF16)

    none = jnp.zeros((64, 64), F32)

    def spread(taps, out_ref):
        for k in range(4):
            for group, col in enumerate(GROUP_COL):
                blocks = []
                for py in range(2):
                    for px in range(2):
                        a, b = k - py, col - px + 1
                        inside = 0 <= a <= 2 and 0 <= b <= 2
                        blocks.append(taps[a][b] if inside else none)
                block = jnp.concatenate(blocks, axis=1).astype(BF16)
                out_ref[pl.ds(k * 256 + group * 64, 64), :] = block

    spread([[second_ref[a, b].astype(F32).T for b in range(3)] for a in range(3)], w2_ref)

    wide_none = jnp.zeros((64, 128), F32)
    taps = [[middle_ref[a, b].astype(F32) for b in range(3)] for a in range(3)]
    for k in range(4):
        for place, b in enumerate((0, 2, 1, None)):
            blocks = []
            for e in range(2):
                inside = b is not None and 0 <= k - e <= 2
                blocks.append(taps[k - e][b] if inside else wide_none)
            block = jnp.concatenate(blocks, axis=1).astype(BF16)
            w3_ref[pl.ds(k * 256 + place * 64, 64), :] = block

    joined = [[joined_ref[a, b].astype(F32).T for b in range(3)] for a in range(3)]
    spread([[joined[a][b][128:192] for b in range(3)] for a in range(3)], w4_ref)
    for dy in range(3):
        for dx in range(3):
            blocks = []
            for py in range(2):
                for px in range(2):
                    total = jnp.zeros((128, 64), F32)
                    for a in range(3):
                        for b in range(3):
                            if (py + a - 1) // 2 + 1 == dy and (px + b - 1) // 2 + 1 == dx:
                                total = total + joined[a][b][0:128]
                    blocks.append(total)
            block = jnp.concatenate(blocks, axis=1).astype(BF16)
            w4_ref[pl.ds(1024 + (dy * 3 + dx) * 128, 128), :] = block

    col = lax.broadcasted_iota(jnp.int32, (256, 256), 0)
    planar_col = lax.broadcasted_iota(jnp.int32, (256, 256), 1)
    to_planar = (col == 2 * (planar_col & 127) + (planar_col >> 7)).astype(F32).astype(BF16)
    planar[...] = dot_nn(labf_ref[...].astype(F32).astype(BF16), to_planar)
    classes = lax.broadcasted_iota(jnp.int32, (NCLS, 128), 0)
    for y in range(4):
        for snap in range(SNAP):
            lanes = pl.ds(128 * (4 * y + snap), 128)
            hits_coarse[:, lanes] = (classes == labc_ref[pl.ds(snap * 4 + y, 1), :]).astype(F32)
            for py in range(2):
                row = pl.ds(snap * 8 + 2 * y + py, 1)
                for px in range(2):
                    label = planar[row, pl.ds(128 * px, 128)]
                    hits_fine[pl.ds((2 * py + px) * 8, 8), lanes] = (classes.astype(F32) == label).astype(F32)

    spot = lax.broadcasted_iota(jnp.int32, (XB, 384), 0)
    wanted = jnp.where(spot >= 142, 2 * spot + 94, 2 * spot - 2)
    wanted = jnp.where(wanted < 0, wanted + 384, wanted)
    hit = lax.broadcasted_iota(jnp.int32, (XB, 384), 1) == wanted
    even_ref[...] = hit.astype(F32).astype(BF16)

    head = fine_ref[...]
    high = head.astype(BF16).astype(F32)
    empty = jnp.zeros((NCLS, 64), F32)
    rows = []
    for part in (high, head - high):
        for spot in range(4):
            rows.append(jnp.concatenate([part if i == spot else empty for i in range(4)], axis=1))
    hf_ref[...] = jnp.concatenate(rows, axis=0).astype(BF16)
    head = coarse_ref[...]
    high = head.astype(BF16).astype(F32)
    hc_ref[...] = jnp.concatenate([high, head - high], axis=0).astype(BF16)


def block_weights(
    conv_first, conv_second, conv_middle, conv_joined, head_fine, head_coarse, labels_fine, labels_coarse
):
    swapped = (0, 1, 3, 2)
    return call(
        weights_kernel, "block_weights",
        [
            ((6, 144, 256), BF16), ((1024, 256), BF16), ((1024, 256), BF16),
            ((1024 + 1152, 256), BF16), ((64, 256), BF16), ((16, 128), BF16),
            ((32, 2048), F32), ((8, 2048), F32), ((XB, 384), BF16),
        ],
        [((32, 64), F32), ((32, 256), F32)], 0, 12,
        jnp.asarray(first_layer_places(), BF16), jnp.transpose(conv_first, swapped), conv_second,
        jnp.transpose(conv_middle, swapped), conv_joined, head_fine, head_coarse,
        labels_fine.reshape(SNAP * ROWS, COLS), labels_coarse.reshape(SNAP * 4, 128),
    )


def before(value):
    return pltpu.roll(value, 1, 0)


def after(value):
    return pltpu.roll(value, M - 1, 0)


def first_kernel(a_ref, mid_ref, b_ref, w1_ref, even_ref, h1, win, taps):
    row384 = lax.broadcasted_iota(jnp.int32, (8, 384), 0)
    up, down = sides(is_even("grp"), a_ref, b_ref, pl.ds(0, 208))
    tiles = [up, mid_ref[...].astype(F32), down]
    for q in range(12):
        pieces = []
        for tile in tiles:
            edge = tile[192 + 8 * (q % 2) : 200 + 8 * (q % 2)]
            edge = pltpu.roll(edge, 128 - (16 * (q // 2) + 8), 1)
            pieces.append(
                jnp.concatenate([tile[8 * q : 8 * q + 8], tile[96 + 8 * q : 104 + 8 * q], edge], axis=1)
            )
        top, center, bottom = pieces
        snap, comp = q // 3, q % 3
        rows = pl.ds(comp * 8, 8)
        win[0, snap, rows, :] = jnp.where(row384 < 6, pltpu.roll(top, 6, 0), pltpu.roll(center, 6, 0))
        win[1, snap, rows, :] = center
        win[2, snap, rows, :] = jnp.where(row384 < 2, pltpu.roll(center, 2, 0), pltpu.roll(bottom, 2, 0))

    even = even_ref[...]
    own = lax.broadcasted_iota(jnp.int32, (XB, 144), 0) < 142
    for group in range(3):
        found = []
        for snap in range(SNAP):
            window = win[group, snap]
            shifted = [window] + [pltpu.roll(window, 384 - j, 1) for j in range(1, 6)]
            stack = jnp.concatenate(shifted, axis=0).astype(BF16)
            found.append(dot_nt(even, stack))
        for snap in range(SNAP):
            rows = jnp.where(own, found[snap], found[(snap + 1) % SNAP])
            taps[group, pl.ds(snap * XB, XB), :] = rows.astype(BF16)

    for i in range(18):
        out = dot_nn(taps[i // 6], w1_ref[i % 6])
        h1[i] = jnp.maximum(out, 0.0).astype(BF16)


def second_kernel(h1, w2_ref, h2, ph):
    side = lax.broadcasted_iota(jnp.int32, (M, 128), 1) < 64

    def pool(q, out):
        pooled = jnp.maximum(out[:, 0:128], out[:, 128:256])
        pooled = jnp.maximum(pooled, pltpu.roll(pooled, 64, 1))
        ph[q, :, 0:128] = jnp.where(side, before(pooled), after(pooled)).astype(BF16)
        ph[q, :, 128:256] = pooled.astype(BF16)

    def row(q):
        lhs = jnp.concatenate([h1[2 * q + k] for k in range(4)], axis=1)
        return jnp.maximum(dot_nn(lhs, w2_ref[...]), 0.0)

    for q in range(8):
        out = row(q)
        if 0 < q < 7:
            for py in range(2):
                part = out[:, 128 * py : 128 * py + 128]
                h2[2 * q - 2 + py, :, 0:128] = part.astype(BF16)
                beside = jnp.where(side, after(part), before(part))
                h2[2 * q - 2 + py, :, 128:256] = beside.astype(BF16)
        pool(q, out)


def class_terms(logits, onehot):
    peak = jnp.max(logits, axis=0, keepdims=True)
    powers = jnp.exp(logits - peak)
    total = jnp.sum(powers, axis=0, keepdims=True)
    lost = onehot * (peak + jnp.log(total) - logits)
    return lost, powers / total - onehot


def cells(kept, lanes):
    return jnp.concatenate(
        [kept[y, pl.ds(snap * XB, 128), lanes] for y in kept_rows(kept) for snap in range(SNAP)], axis=0
    )


def kept_rows(kept):
    return range(1, 5) if kept.shape[0] == 6 else range(4)


def fold(lost):
    total = lost[:, 0:128]
    for block in range(1, 16):
        total = total + lost[:, 128 * block : 128 * block + 128]
    return total


def middle_kernel(ph, w3_ref, hc_ref, hits_ref, mh, sums_ref):
    for t in range(3):
        lhs = jnp.concatenate([ph[2 * t + k] for k in range(4)], axis=1)
        out = jnp.maximum(dot_nn(lhs, w3_ref[...]), 0.0)
        for e in range(2):
            value = out[:, 128 * e : 128 * e + 128]
            row = 2 * t + e
            mh[row, :, 0:128] = before(value).astype(BF16)
            mh[row, :, 128:256] = value.astype(BF16)
            mh[row, :, 256:384] = after(value).astype(BF16)

    feature = cells(mh, pl.ds(128, 128))
    both = dot_nt(hc_ref[...], feature)
    lost, grad = class_terms(both[0:8] + both[8:16], hits_ref[...])
    high = grad.astype(BF16).astype(F32)
    slopes = jnp.concatenate([high, grad - high], axis=0).astype(BF16)
    total = dot_nn(slopes, feature)
    coarse_cells = 262144.0
    sums_ref[0:8, :] = (total[0:8] + total[8:16]) * (1.0 / coarse_cells)
    sums_ref[8:16, :] = fold(lost) * (1.0 / coarse_cells)


def decoded_kernel(
    h2, mh, w4_ref, hf_ref, hits_ref, coarse_ref, planar_ref, sums_ref, dec
):
    for y in range(4):
        lhs = jnp.concatenate(
            [h2[2 * y + 1 + k] for k in range(4)] + [mh[y + k] for k in range(3)], axis=1
        )
        dec[y] = jnp.maximum(dot_nn(lhs, w4_ref[...]), 0.0).astype(BF16)

    feature = cells(dec, pl.ds(0, 256))
    both = dot_nt(hf_ref[...], feature)
    logits = both[0:32] + both[32:64]
    planar_ref[...] = logits
    lost_fine = jnp.zeros((NCLS, 2048), F32)
    slopes = []
    for py in range(2):
        for px in range(2):
            at = (2 * py + px) * 8
            lost, grad = class_terms(logits[at : at + 8], hits_ref[pl.ds(at, 8), :])
            lost_fine = lost_fine + lost
            slopes.append(grad)
    high, low = split_two(jnp.concatenate(slopes, axis=0))
    grad_fine = dot_nn(jnp.concatenate([high, low], axis=0), feature)

    fine_cells = 1048576.0
    total = jnp.zeros((NCLS, 64), F32)
    for spot in range(4):
        for part in (0, 32):
            block = grad_fine[part + 8 * spot : part + 8 * spot + 8]
            total = total + block[:, 64 * spot : 64 * spot + 64]
    loss = jnp.sum(fold(lost_fine)) * (1.0 / fine_cells) + jnp.sum(coarse_ref[8:16, :])
    sums_ref[0:8, :] = coarse_ref[0:8, :]
    sums_ref[8:16, :] = jnp.concatenate(
        [total * (1.0 / fine_cells), jnp.broadcast_to(loss, (NCLS, 64))], axis=1
    )


def ordered_kernel(planar_ref, logits_ref):
    col = lax.broadcasted_iota(jnp.int32, (256, 256), 0)
    planar_col = lax.broadcasted_iota(jnp.int32, (256, 256), 1)
    to_cols = (planar_col == 2 * (col & 127) + (col >> 7)).astype(F32).astype(BF16)
    logits = planar_ref[...]
    order = [(snap, y, py) for snap in range(SNAP) for y in range(4) for py in range(2)]
    halves = []
    for px in range(2):
        blocks = []
        for snap, y, py in order:
            lane = 128 * (4 * y + snap)
            blocks.append(logits[(2 * py + px) * 8 : (2 * py + px) * 8 + 8, lane : lane + 128])
        halves.append(jnp.concatenate(blocks, axis=0))
    whole = jnp.concatenate(halves, axis=1)
    high = whole.astype(BF16)
    rest = whole - high.astype(F32)
    middle_term = rest.astype(BF16)
    low = (rest - middle_term.astype(F32)).astype(BF16)
    ordered = dot_nn(high, to_cols) + dot_nn(middle_term, to_cols) + dot_nn(low, to_cols)
    for row in range(32):
        logits_ref[row] = ordered[8 * row : 8 * row + 8]


def first(a, mid, b, w1, even):
    return call(
        first_kernel, "first", [((18, M, 256), BF16)],
        [((3, SNAP, 24, 384), F32), ((3, M, 144), BF16)],
        2_000_000_000, 14, a, mid, b, w1, even,
    )[0]


def second(h1, w2):
    return call(
        second_kernel, "second", [((12, M, 256), BF16), ((8, M, 256), BF16)],
        [], 2_500_000_000, 18, h1, w2,
    )


def middle(ph, w3, hc, labels):
    return call(
        middle_kernel, "middle", [((6, M, 384), BF16), ((16, 128), F32)],
        [], 1_000_000_000, 12, ph, w3, hc, labels,
    )


def decoded(h2, mh, w4, hf, labels, coarse):
    return call(
        decoded_kernel, "decoded", [((32, 2048), F32), ((16, 128), F32)],
        [((4, M, 256), BF16)],
        2_500_000_000, 16, h2, mh, w4, hf, labels, coarse,
    )


def ordered(planar):
    return call(
        ordered_kernel, "ordered", [((32, NCLS, COLS), F32)], [], 300_000_000, 6, planar
    )[0]


def mesh_pairs(change):
    pairs = []
    for device in range(128):
        grp, gx = device // 16, device % 16
        at = {"x": (gx // 2 % 2) * 2 + grp // 4, "y": grp % 4, "z": gx // 4, "core": gx % 2}
        change(at)
        grp = (at["x"] % 2) * 4 + at["y"]
        gx = (at["z"] * 2 + at["x"] // 2) * 2 + at["core"]
        pairs.append((device, grp * 16 + gx))
    return pairs


def flip(x, name, bits):
    def change(at):
        at[name] ^= bits

    return lax.ppermute(x, AXES, mesh_pairs(change))


def finish_kernel(a, b, c, d, loss, fine, coarse):
    total = (a[...] + b[...]) + (c[...] + d[...])
    coarse[...] = total[0:8]
    fine[...] = total[8:16, 0:64]
    loss[...] = total[8:9, 64:65]


tie = lax.optimization_barrier


def near(x):
    return pltpu.with_memory_space_constraint(x, pltpu.VMEM)


def body(
    velocity, snapshot_index, labels_fine, labels_coarse,
    conv_first, conv_second, conv_middle, conv_joined, head_fine, head_coarse,
):
    keep, give = pack(velocity, snapshot_index)
    line_a, line_b = outer_lines(velocity)
    weights = block_weights(
        conv_first, conv_second, conv_middle, conv_joined, head_fine, head_coarse, labels_fine, labels_coarse
    )
    got = exchange_a(give, "gx")
    block = ((2, 208, 128), BF16)
    own, one, two, three = call(merge_kernel, "merge", [block] * 4, [], 1, 8, near(keep), near(got))
    own, line_a, line_b = tie((own, line_a, line_b))
    two, one, three = flip(two, "z", 2), flip(one, "z", 1), flip(three, "z", 3)
    line_a, line_b = exchange_a(line_a, "grp"), exchange_b(line_b, "grp")
    own, weights = tie((own, weights))
    block = ((208, 128), BF16)
    mine, theirs = call(
        gather_kernel, "gather", [block] * 2, [], 3_000_000_000, 8, near(own), near(two), near(one), near(three)
    )
    got = lax.ppermute(theirs, "gx", [(i, i ^ 2) for i in range(16)])
    mine, line_a, line_b = tie((mine, line_a, line_b))
    plane_a, plane_b = outer_planes(velocity, line_a, line_b)
    tile = mine + got
    tile, plane_a, plane_b = tie((tile, plane_a, plane_b))
    tile_a, tile_b = exchange_a(tile, "grp"), exchange_b(tile, "grp")
    plane_b, plane_a = exchange_b(plane_b, "gx"), exchange_a(plane_a, "gx")
    w1, w2, w3, w4, hf, hc, hits_fine, hits_coarse, even = weights
    h2, ph = second(first(tile_a, tile, tile_b, w1, even), w2)
    mh, coarse = middle(ph, w3, hc, hits_coarse)
    planar, sums = decoded(h2, mh, w4, hf, hits_fine, coarse)

    got = flip(sums, "core", 1)
    logits = ordered(planar)
    sums, logits, plane_a, plane_b = tie((sums + got, logits, plane_a, plane_b))
    got = flip(sums, "z", 1)
    new = step_one(velocity, plane_a, plane_b, line_a, line_b)
    sums, new = tie((sums + got, new))
    got = flip(sums, "z", 3)
    field = step_two(new)
    sums, field = tie((sums + got, field))
    sums = (sums + flip(sums, "y", 1)) + (flip(sums, "y", 2) + flip(sums, "y", 3))
    loss, grad_fine, grad_coarse = call(
        finish_kernel, "finish", [((1, 1), F32), ((8, 64), F32), ((8, 128), F32)], [], 1, 4,
        sums, flip(sums, "x", 1), flip(sums, "x", 2), flip(sums, "x", 3),
    )
    return (
        field,
        logits.reshape(SNAP, ROWS, NCLS, COLS),
        loss.reshape(()),
        grad_fine,
        grad_coarse,
    )


def solution(mesh):
    return jax.shard_map(
        body,
        mesh=mesh,
        in_specs=(
            P(None, "gx", "grp", None),
            P(),
            P(None, "grp", "gx"),
            P(None, "grp", "gx"),
            P(),
            P(),
            P(),
            P(),
            P(),
            P(),
        ),
        out_specs=(P(None, "gx", "grp", None), P(None, "grp", None, "gx"), P(), P(), P()),
        check_vma=False,
    )
```
